128 devices in a mesh: outer: 8 (over x, core), inner: 16 (over y, z).
Axes of the slice: x: 4, y: 4, z: 4, core: 2. Of those that a mesh axis runs over, the one named last changes fastest.
Arguments:
- rhs: float32 [262144, 128], P(('outer', 'inner')), may hold values from -6 to 6
- near_blocks: bfloat16 [1024, 8, 256, 256], P(('outer', 'inner')), may hold values from -0.125 to 0.125
- near_index: int32 [1024, 8], P(('outer', 'inner')), may hold values from 0 to 11
- near_mask: int32 [1024, 8], P(('outer', 'inner')), may hold values 0 or 1
- basis: bfloat16 [1024, 64, 256], P(('outer', 'inner')), may hold values from -0.375 to 0.375
- far_blocks: bfloat16 [1024, 48, 64, 64], P(('outer', 'inner')), may hold values from -0.109375 to 0.109375
- far_slot: int32 [1024, 48], P(('outer', 'inner')), may hold values from 0 to 63
- far_mask: int32 [1024, 48], P(('outer', 'inner')), may hold values 0 or 1
- send_slot: int32 [128, 16, 4], P(('outer', 'inner')), may hold values from 0 to 7, as said below
- transfer: bfloat16 [1024, 64, 64], P(('outer', 'inner')), may hold values from -0.25 to 0.25
- top_blocks: bfloat16 [8, 8, 64, 64], P('outer'), may hold values from -0.25 to 0.25
Outputs:
- krylov: float32 [5, 262144, 128], P(None, ('outer', 'inner'))
- hessenberg: float32 [5, 4, 128], replicated
The draws below stay inside these ranges and needn't reach their ends.
Inputs may be any that keep to these rules, and one draw needn't show every extreme that they name: `send_slot`: for each sender subtree and receiver of its branch, the 4 entries are distinct local leaves of the sender.
All inputs are finite; a program needn't handle non-finite values. No bound on the sum of `near_mask` or of `far_mask` on one device may be relied on, other than what follows from the above.
Results may differ from the reference program's by a relative error of at most 0.028.
Values may be sent and summed in bfloat16 or wider, within the bound.
No kernel may reach another device: no remote copies, remote signals or barrier semaphores. Data moves between devices by JAX's collectives and lax.ppermute only.
A program may use at most 128 MiB of HBM per device.

```python
import jax
import jax.numpy as jnp
from jax import lax

LEAF = 256
RANK = 64
LEAVES_DEV = 8
RHS = 128
NEAR = 8
FAR = 48
SLOTS = 4
HW = 2
STEPS = 4
SUBTREES = 128
BRANCHES = 8
LEAVES = 1024
POINTS = 262144
N_OUTER = 8
N_INNER = 16


def draw_send_slot(key, part):
    key = jax.random.fold_in(key, 7)
    many_keys = jax.random.split(key, SUBTREES * N_INNER)
    chosen = jax.vmap(lambda single: jax.random.permutation(single, LEAVES_DEV)[:SLOTS])(many_keys)
    wanted = chosen.reshape(N_OUTER, N_INNER, N_INNER, SLOTS)
    return jnp.transpose(wanted, (0, 2, 1, 3)).reshape(SUBTREES, N_INNER, SLOTS).astype(jnp.int32)


def touch_ends(result, own_key, smallest, top_value):
    place = [jax.random.randint(jax.random.fold_in(own_key, axis), (), 0, length) for axis, length in enumerate(result.shape)]
    main_axis = result.shape.index(max(result.shape))
    beside = place[:main_axis] + [(place[main_axis] + 1) % result.shape[main_axis]] + place[main_axis + 1:]
    return result.at[tuple(place)].set(smallest).at[tuple(beside)].set(top_value)


def block_levels(stream_key, shape, cuts, smallest, top_value):
    loudness, own = 1.0, jax.random.fold_in(stream_key, 6)
    for dim, parts in cuts:
        draws = jnp.exp(jax.random.uniform(jax.random.fold_in(own, dim), (parts,), jnp.float32, smallest / len(cuts), top_value / len(cuts)))
        loudness = loudness * jnp.repeat(draws, shape[dim] // parts).reshape([-1 if axis == dim else 1 for axis in range(len(shape))])
    return loudness


def normal_values(stream_key, extent, spread, limit, cuts=(), held_as=jnp.bfloat16):
    values = jax.random.normal(stream_key, extent, jnp.float32) * spread
    if len(cuts) > 0:
        values = block_levels(stream_key, extent, cuts, -0.22, 0.18) * values
    return jnp.clip(values, min=-limit, max=limit).astype(held_as)


def setup_inputs(seed: int = 0) -> dict:
    keys = jax.random.split(jax.random.key(seed), 12)
    rhs = normal_values(keys[0], (POINTS, RHS), 1.0, 6.0, ((0, 128),), jnp.float32)
    near_blocks = normal_values(keys[1], (LEAVES, NEAR, LEAF, LEAF), (LEAF * NEAR) ** -0.5, 0.125, ((0, 128),))
    near_index = touch_ends(jax.random.randint(keys[2], (LEAVES, NEAR), 0, LEAVES_DEV + 2 * HW), jax.random.fold_in(keys[2], 1), 0, (LEAVES_DEV + 2 * HW) - 1).astype(jnp.int32)
    near_mask = touch_ends((jax.random.randint(keys[3], (LEAVES, NEAR), 0, 4) < 3).astype(jnp.int32), jax.random.fold_in(keys[3], 1), 0, 1)
    basis = normal_values(keys[4], (LEAVES, RANK, LEAF), LEAF ** -0.5, 0.375, ((0, 128),))
    far_blocks = normal_values(keys[5], (LEAVES, FAR, RANK, RANK), (RANK * FAR) ** -0.5, 0.109375, ((0, 128),))
    far_slot = touch_ends(jax.random.randint(keys[6], (LEAVES, FAR), 0, N_INNER * SLOTS), jax.random.fold_in(keys[6], 1), 0, (N_INNER * SLOTS) - 1).astype(jnp.int32)
    far_mask = touch_ends((jax.random.randint(keys[7], (LEAVES, FAR), 0, 4) < 3).astype(jnp.int32), jax.random.fold_in(keys[7], 1), 0, 1)
    send_slot = draw_send_slot(jax.random.fold_in(keys[11], 71), 0)
    transfer = normal_values(keys[9], (LEAVES, RANK, RANK), (RANK * LEAVES_DEV) ** -0.5, 0.25, ((0, 128),))
    top_blocks = normal_values(keys[10], (BRANCHES, BRANCHES, RANK, RANK), (RANK * BRANCHES) ** -0.5, 0.25, ((0, 8),))
    return dict(rhs=rhs, near_blocks=near_blocks, near_index=near_index, near_mask=near_mask, basis=basis, far_blocks=far_blocks, far_slot=far_slot, far_mask=far_mask, send_slot=send_slot, transfer=transfer, top_blocks=top_blocks)


def apply_operator(vector, near_blocks, near_index, near_mask, basis, far_blocks, far_slot, far_mask, send_slot, transfer, top_blocks):
    fine = N_INNER
    leaf_flat = vector.astype(jnp.bfloat16).reshape(LEAVES, LEAF, RHS)
    device = jnp.arange(SUBTREES, dtype=jnp.int32)[:, None, None]
    position = device % fine * LEAVES_DEV + near_index.reshape(SUBTREES, LEAVES_DEV, NEAR) - HW
    valid = (position >= 0) & (position < fine * LEAVES_DEV)
    neighbour = device // fine * fine * LEAVES_DEV + jnp.clip(position, 0, fine * LEAVES_DEV - 1)
    near_weight = jnp.where(valid, near_mask.reshape(SUBTREES, LEAVES_DEV, NEAR), 0).astype(jnp.float32)

    def near_device(items):
        blocks, rows, weight = items
        values = leaf_flat[rows].astype(jnp.float32) * weight[:, :, None, None]
        return jnp.einsum('lnij,lnjr->lir', blocks.astype(jnp.float32), values)
    near_part = lax.map(near_device, (near_blocks.reshape(SUBTREES, LEAVES_DEV, NEAR, LEAF, LEAF), neighbour, near_weight))
    skeleton = jnp.einsum('lki,lir->lkr', basis.astype(jnp.float32), leaf_flat.astype(jnp.float32)).astype(jnp.bfloat16)
    slots = far_slot.reshape(SUBTREES, LEAVES_DEV, FAR)
    sender = device // fine * fine + slots // SLOTS
    local_leaf = send_slot[sender, device % fine, slots % SLOTS]
    far_rows = sender * LEAVES_DEV + local_leaf
    far_weight = far_mask.reshape(SUBTREES, LEAVES_DEV, FAR).astype(jnp.float32)

    def far_device(items):
        blocks, rows, weight = items
        values = skeleton[rows].astype(jnp.float32) * weight[:, :, None, None]
        return jnp.einsum('lfab,lfbr->lar', blocks.astype(jnp.float32), values)
    local_far = lax.map(far_device, (far_blocks.reshape(SUBTREES, LEAVES_DEV, FAR, RANK, RANK), far_rows, far_weight)).reshape(LEAVES, RANK, RHS)
    partial_up = jnp.einsum('lab,lar->lbr', transfer.astype(jnp.float32), skeleton.astype(jnp.float32))
    branch_up = lax.optimization_barrier(jnp.sum(partial_up.reshape(BRANCHES, fine * LEAVES_DEV, RANK, RHS), axis=1)).astype(jnp.bfloat16)
    off_diagonal = (jnp.arange(BRANCHES)[:, None] != jnp.arange(BRANCHES)[None, :]).astype(jnp.float32)
    top_masked = top_blocks.astype(jnp.float32) * off_diagonal[:, :, None, None]
    incoming = jnp.einsum('bcxy,cyr->bxr', top_masked, branch_up.astype(jnp.float32))
    leaf_incoming = jnp.repeat(incoming.astype(jnp.bfloat16), fine * LEAVES_DEV, axis=0)
    downward = jnp.einsum('lab,lbr->lar', transfer.astype(jnp.float32), leaf_incoming.astype(jnp.float32))
    combined = (local_far + downward).astype(jnp.bfloat16)
    far_part = jnp.einsum('lki,lkr->lir', basis.astype(jnp.float32), combined.astype(jnp.float32))
    return vector + (near_part.reshape(LEAVES, LEAF, RHS) + far_part).reshape(POINTS, RHS)

def reference(rhs, near_blocks, near_index, near_mask, basis, far_blocks, far_slot, far_mask, send_slot, transfer, top_blocks):
    scale = jnp.sqrt(lax.optimization_barrier(jnp.sum(rhs * rhs, axis=0)) / POINTS + 1e-06)
    vectors = [rhs / scale]
    hessenberg = jnp.zeros((STEPS + 1, STEPS, RHS), jnp.float32)
    for iteration in range(STEPS):
        image = apply_operator(vectors[-1], near_blocks, near_index, near_mask, basis, far_blocks, far_slot, far_mask, send_slot, transfer, top_blocks)
        stacked = jnp.stack(vectors)
        project = lax.optimization_barrier(jnp.sum(stacked * image[None], axis=1)) / POINTS
        image = image - lax.optimization_barrier(jnp.sum(project[:, None, :] * stacked, axis=0))
        height = jnp.sqrt(lax.optimization_barrier(jnp.sum(image * image, axis=0)) / POINTS + 1e-06)
        hessenberg = hessenberg.at[:iteration + 1, iteration].set(project)
        hessenberg = hessenberg.at[iteration + 1, iteration].set(height)
        vectors.append(image / height)
    return (jnp.stack(vectors), hessenberg)
```

```python
import functools

import jax
import jax.numpy as jnp
from jax import lax
from jax.experimental import pallas as pl
from jax.experimental.pallas import tpu as pltpu
from jax.sharding import PartitionSpec as P

HW = 2
STEPS = 4
EPS = 1e-06
PIECES = 3
DOT_ROWS = 16
STATE_ROWS = 64
VMEM_BYTES = 60 * 1024 * 1024
BF16 = jnp.bfloat16
F32 = jnp.float32


def dot(a, b):
    return jnp.dot(a, b, preferred_element_type=F32)


def dot_first(a, b):
    return lax.dot_general(a, b, (((0,), (0,)), ((), ())), preferred_element_type=F32)


def store_split(ref, values, count):
    rest = values
    ref[...] = jnp.zeros(ref.shape, F32)
    for piece in range(PIECES):
        part = rest.astype(BF16).astype(F32)
        ref[piece * 5 : piece * 5 + count, :] = part[:count]
        rest = rest - part


def joined(rows):
    return [rows[i : i + 1] + rows[5 + i : 6 + i] + rows[10 + i : 11 + i] for i in range(5)]


def entry_row(i, l):
    low, high = min(i, l), max(i, l)
    return 20 + high * (high + 1) // 2 + low


def basis_row(i, l):
    return 32 + i * (i + 1) // 2 + l


def coefficients(m, grams, state_in, state_out):
    last = m - 1
    entry = lambda i, l: state_in[entry_row(i, l) : entry_row(i, l) + 1, :]
    expand = lambda i, l: state_in[basis_row(i, l) : basis_row(i, l) + 1, :]

    def put(row, value):
        state_out[row : row + 1, :] = value

    dots = []
    for i in range(m):
        dots.append(sum(expand(i, l) * grams[l] for l in range(i + 1)))
    weights = [dots[i] + entry(i, last) for i in range(m)]
    spread = [sum(weights[l] * entry(i, l) for l in range(m)) for i in range(m)]
    square = grams[m]
    for i in range(m):
        square = square + weights[i] * (weights[i] + spread[i] - 2.0 * dots[i])
    total = jnp.maximum(square, 0.0) + EPS
    root = jnp.sqrt(total)
    inverse = 1.0 / root
    for l in range(m):
        value = sum(weights[i] * expand(i, l) for i in range(l, m))
        put(basis_row(m, l), -inverse * value)
    put(basis_row(m, m), inverse)
    for i in range(m):
        put(i * STEPS + last, weights[i] + (1.0 if i == last else 0.0))
    if m > 0:
        put(m * STEPS + last, root)
    if m < STEPS:
        for i in range(m):
            put(entry_row(i, m), (-entry(i, last) - spread[i]) * inverse)
        put(entry_row(m, m), -EPS / total)
    return weights, inverse


def whole(a):
    zeros = (0,) * len(a.shape)
    return pl.BlockSpec(a.shape, lambda l, *_: zeros)


def by_leaf(shape):
    zeros = (0,) * (len(shape) - 1)
    return pl.BlockSpec(shape, lambda l, *_: (l,) + zeros)


def gather_sum_kernel(recv_ref, *refs, lead):
    (*_, out_ref, rows_ref, split, semaphore) = refs
    rows = rows_ref.shape[1]
    rank = rows - DOT_ROWS
    copy = pltpu.make_async_copy(recv_ref.at[:, lead : lead + rows], rows_ref, semaphore)
    copy.start()
    copy.wait()
    total = rows_ref[0].astype(F32)
    for i in range(1, rows_ref.shape[0]):
        total = total + rows_ref[i].astype(F32)
    store_split(split, jnp.concatenate(joined(total[rank:]), axis=0), 5)
    dots = split[...].astype(BF16)
    for c in range(out_ref.shape[0]):
        if rank > 0:
            out_ref[c, :rank] = total[:rank].astype(BF16)
        out_ref[c, rank:] = dots


def gather_sum(recv, lead, outer, *earlier):
    inner, rows, columns = recv.shape
    rows = rows - lead
    return pl.pallas_call(
        functools.partial(gather_sum_kernel, lead=lead),
        in_specs=[pl.BlockSpec(memory_space=pl.ANY)] * (1 + len(earlier)),
        out_specs=pl.BlockSpec(memory_space=pltpu.VMEM),
        scratch_shapes=[
            pltpu.VMEM((inner, rows, columns), BF16),
            pltpu.VMEM((DOT_ROWS, columns), F32),
            pltpu.SemaphoreType.DMA,
        ],
        out_shape=jax.ShapeDtypeStruct((outer, rows, columns), BF16),
        compiler_params=pltpu.CompilerParams(vmem_limit_bytes=VMEM_BYTES),
        cost_estimate=pl.CostEstimate(flops=1 << 20, bytes_accessed=1 << 19, transcendentals=0),
        name="gather_sum",
    )(recv, *earlier)


def from_branches(ups_ref, rank):
    rows = ups_ref[0, rank:].astype(F32)
    for c in range(1, ups_ref.shape[0]):
        rows = rows + ups_ref[c, rank:].astype(F32)
    return joined(rows)


ANY = pl.BlockSpec(memory_space=pl.ANY)
SMEM = pl.BlockSpec(memory_space=pltpu.SMEM)
CHUNKS = 4


def call(kernel, args, in_specs, out_shape, out_specs, scratch, name, flops, moved, aliases={}):
    return pl.pallas_call(
        kernel,
        in_specs=in_specs,
        out_specs=out_specs,
        out_shape=out_shape,
        scratch_shapes=scratch,
        input_output_aliases=aliases,
        compiler_params=pltpu.CompilerParams(vmem_limit_bytes=VMEM_BYTES),
        cost_estimate=pl.CostEstimate(flops=flops, bytes_accessed=moved, transcendentals=0),
        name=name,
    )(*args)


def tie_kernel(send_in, before, after, send_out):
    pass


def tie(send, before, after):
    shape = jax.ShapeDtypeStruct(send.shape, send.dtype)
    return call(
        tie_kernel, (send, before, after), [ANY] * 3, shape, ANY, [], "tie", 0, 1 << 10, {0: 0}
    )


def pack_kernel(mask_ref, far_ref, out_ref, blocks, packed, arrived, left):
    leaves, entries, rank, _ = blocks.shape
    fetch = lambda l: pltpu.make_async_copy(far_ref.at[l], blocks.at[l], arrived.at[l])
    store = lambda l: pltpu.make_async_copy(packed.at[l], out_ref.at[l], left.at[l])
    for leaf in range(leaves):
        fetch(leaf).start()

    def body(leaf, carry):
        fetch(leaf).wait()
        for pair in range(entries // 2):
            sides = []
            for f in (2 * pair, 2 * pair + 1):
                weight = mask_ref[leaf, f].astype(F32).astype(BF16)
                sides.append(blocks[leaf, f] * weight)
            columns = slice(pair * 2 * rank, (pair + 1) * 2 * rank)
            packed[leaf, :, columns] = jnp.concatenate(sides, axis=1)
        store(leaf).start()
        return carry

    lax.fori_loop(0, leaves, body, 0)
    for leaf in range(leaves):
        store(leaf).wait()


def pack_far(far_blocks, far_mask):
    leaves, entries, rank, _ = far_blocks.shape
    shape = (leaves, rank, entries * rank)
    return call(
        pack_kernel,
        (far_mask, far_blocks),
        [SMEM, ANY],
        jax.ShapeDtypeStruct(shape, BF16),
        ANY,
        [
            pltpu.VMEM(far_blocks.shape, BF16),
            pltpu.VMEM(shape, BF16),
            pltpu.SemaphoreType.DMA((leaves,)),
            pltpu.SemaphoreType.DMA((leaves,)),
        ],
        "pack_far",
        0,
        12 << 20,
    )


def near_kernel(index_ref, mask_ref, blocks_ref, before_ref, own_ref, after_ref, *refs):
    (*_, out_ref, blocks, padded, result, arrived, halo, left) = refs
    leaves, entries = blocks.shape[:2]
    width = before_ref.shape[0]
    half = entries // 2
    size = result.shape[1]

    def fetch(leaf, part):
        piece = pl.ds(part * half, half)
        return pltpu.make_async_copy(
            blocks_ref.at[leaf, piece], blocks.at[leaf, piece], arrived.at[leaf, part]
        )

    def store(leaf):
        rows = pl.ds(pl.multiple_of(leaf * size, size), size)
        return pltpu.make_async_copy(result.at[leaf], out_ref.at[rows], left.at[leaf])

    sides = [
        pltpu.make_async_copy(own_ref, padded.at[pl.ds(width, leaves)], halo.at[0]),
        pltpu.make_async_copy(before_ref, padded.at[pl.ds(0, width)], halo.at[1]),
        pltpu.make_async_copy(after_ref, padded.at[pl.ds(width + leaves, width)], halo.at[2]),
    ]
    for side in sides:
        side.start()
    for leaf in range(leaves):
        for part in range(2):
            fetch(leaf, part).start()
    for side in sides:
        side.wait()

    def body(leaf, carry):
        fetch(leaf, 0).wait()
        fetch(leaf, 1).wait()
        total = None
        for n in range(entries):
            weight = mask_ref[leaf, n].astype(F32).astype(BF16)
            term = dot(blocks[leaf, n], padded[index_ref[leaf, n]] * weight)
            total = term if total is None else total + term
        result[leaf] = total
        store(leaf).start()
        return carry

    lax.fori_loop(0, leaves, body, 0)
    for leaf in range(leaves):
        store(leaf).wait()


def near_field(near_index, near_mask, near_blocks, before, own, after, *earlier):
    leaves, entries, size, _ = near_blocks.shape
    width, columns = before.shape[0], own.shape[2]
    return call(
        near_kernel,
        (near_index, near_mask, near_blocks, before, own, after) + earlier,
        [SMEM, SMEM] + [ANY] * (4 + len(earlier)),
        jax.ShapeDtypeStruct((leaves * size, columns), F32),
        ANY,
        [
            pltpu.VMEM(near_blocks.shape, BF16),
            pltpu.VMEM((leaves + 2 * width, size, columns), BF16),
            pltpu.VMEM((leaves, size, columns), F32),
            pltpu.SemaphoreType.DMA((leaves, 2)),
            pltpu.SemaphoreType.DMA((3,)),
            pltpu.SemaphoreType.DMA((leaves,)),
        ],
        "near_field",
        2 * near_blocks.size * columns,
        2 * near_blocks.size,
    )


def far_kernel(far_slot, recv_ref, far_ref, earlier_ref, out_ref, *scratch):
    packed, skeletons, gathered, result, arrived, came, left = scratch
    leaves, rank, depth = packed.shape
    inner, rows, _ = skeletons.shape
    slots = rows // rank
    part = inner // CHUNKS

    def get(i):
        some = pl.ds(i * part, part)
        return pltpu.make_async_copy(
            recv_ref.at[some, pl.ds(0, rows)], skeletons.at[some], came.at[i]
        )

    fetch = lambda l: pltpu.make_async_copy(far_ref.at[l], packed.at[l], arrived.at[l])
    store = lambda l: pltpu.make_async_copy(result.at[l], out_ref.at[l], left.at[l])
    for i in range(CHUNKS):
        get(i).start()
    for leaf in range(leaves):
        fetch(leaf).start()
    for i in range(CHUNKS):
        get(i).wait()

    def body(leaf, carry):
        fetch(leaf).wait()
        for f in range(depth // rank):
            slot = far_slot[leaf, f]
            start = pl.multiple_of(slot % slots * rank, rank)
            gathered[f * rank : (f + 1) * rank] = skeletons[slot // slots, pl.ds(start, rank)]
        result[leaf] = dot(packed[leaf], gathered[...])
        store(leaf).start()
        return carry

    lax.fori_loop(0, leaves, body, 0)
    for leaf in range(leaves):
        store(leaf).wait()


def far_field(far_slot, recv, packed, slots, earlier):
    leaves, rank, depth = packed.shape
    inner, _, columns = recv.shape
    shape = (leaves, rank, columns)
    return call(
        far_kernel,
        (far_slot, recv, packed, earlier),
        [SMEM, ANY, ANY, ANY],
        jax.ShapeDtypeStruct(shape, F32),
        ANY,
        [
            pltpu.VMEM(packed.shape, BF16),
            pltpu.VMEM((inner, slots * rank, columns), BF16),
            pltpu.VMEM((depth, columns), BF16),
            pltpu.VMEM(shape, F32),
            pltpu.SemaphoreType.DMA((leaves,)),
            pltpu.SemaphoreType.DMA((CHUNKS,)),
            pltpu.SemaphoreType.DMA((leaves,)),
        ],
        "far_field",
        2 * packed.size * columns,
        2 * packed.size + (1 << 20),
    )


def stage_kernel(*refs, k, points):
    refs = list(refs)
    take = lambda count: [refs.pop(0) for _ in range(count)]
    m = k - 1
    first, sends = k == 0, k < STEPS
    send_slot, branch = take(2)
    zs = take(max(k, 1))
    if not first:
        ups_any, state_any, top_any, far_any, near_any = take(5)
    basis_any, transfer_any = take(2)
    if not first:
        state_out, z_any = take(2)
    (send_any,) = take(1)
    if sends:
        coarse_any, low_any, high_any = take(3)
    basis, transfer, vectors, result, sums, send, split, sent, arrived, came, left = take(11)
    if sends:
        coarse, skeletons, upward, out = take(4)
    if not first:
        ups, state, top, far, near, coef, incoming = take(7)

    leaves, rank, size = basis.shape
    group = leaves // CHUNKS

    def rows(i):
        return pl.ds(pl.multiple_of(i * group * size, group * size), group * size)

    def some(i):
        return pl.ds(i * group, group)

    def fetches(i):
        pairs = [(z.at[rows(i)], vectors.at[l, rows(i)]) for l, z in enumerate(zs)]
        pairs.append((basis_any.at[some(i)], basis.at[some(i)]))
        pairs.append((transfer_any.at[some(i)], transfer.at[some(i)]))
        if not first:
            pairs.append((near_any.at[rows(i)], near.at[rows(i)]))
            pairs.append((far_any.at[some(i)], far.at[some(i)]))
        return [
            pltpu.make_async_copy(source, target, arrived.at[n, i])
            for n, (source, target) in enumerate(pairs)
        ]

    def stores(i):
        pairs = []
        if not first:
            pairs.append((result.at[rows(i)], z_any.at[rows(i)]))
        if sends:
            pairs.append((coarse.at[some(i)], coarse_any.at[some(i)]))
        return [
            pltpu.make_async_copy(source, target, left.at[n, i])
            for n, (source, target) in enumerate(pairs)
        ]

    if not first:
        small = [
            pltpu.make_async_copy(source, target, came.at[n])
            for n, (source, target) in enumerate(
                [(ups_any, ups), (state_any, state), (top_any, top)]
            )
        ]
        for copy in small:
            copy.start()
    for i in range(CHUNKS):
        for copy in fetches(i):
            copy.start()

    sums[...] = jnp.zeros(sums.shape, F32)
    if sends:
        upward[...] = jnp.zeros(upward.shape, F32)
    if not first:
        for copy in small:
            copy.wait()
        total = None
        for c in range(ups.shape[0]):
            weight = (branch[0] != c).astype(F32).astype(BF16)
            term = dot(top[0, c] * weight, ups[c, :rank])
            total = term if total is None else total + term
        incoming[...] = total.astype(BF16)
        grams = [row / points for row in from_branches(ups, rank)]
        state_out[...] = state[...]
        weights, inverse = coefficients(m, grams, state, state_out)
        for i, weight in enumerate(weights):
            coef[i : i + 1, :] = weight
        coef[STEPS : STEPS + 1, :] = inverse

    def one_leaf(leaf):
        own = pl.ds(pl.multiple_of(leaf * size, size), size)
        others = [vectors[l, own] for l in range(len(zs))]
        if first:
            z = others.pop()
        else:
            combined = far[leaf] + dot(transfer[leaf], incoming[...])
            z = near[own] + dot_first(basis[leaf], combined.astype(BF16))
            for i in range(m):
                z = z - coef[i : i + 1, :] * others[i + 1]
            z = z * coef[STEPS : STEPS + 1, :]
            result[own] = z
        if sends:
            rounded = z.astype(BF16)
            coarse[leaf] = rounded
            skeleton = dot(basis[leaf], rounded).astype(BF16)
            skeletons[leaf] = skeleton
            upward[...] += dot_first(transfer[leaf], skeleton)
        for i, other in enumerate(others + [z]):
            sums[i] += jnp.sum((z * other).reshape(size // 8, 8, z.shape[1]), axis=0)

    def body(i, carry):
        for copy in fetches(i):
            copy.wait()
        for j in range(group):
            one_leaf(i * group + j)
        for copy in stores(i):
            copy.start()
        return carry

    lax.fori_loop(0, CHUNKS, body, 0)

    if sends:
        halos = [
            pltpu.make_async_copy(coarse.at[pl.ds(0, HW)], low_any, out.at[0]),
            pltpu.make_async_copy(coarse.at[pl.ds(leaves - HW, HW)], high_any, out.at[1]),
        ]
        for copy in halos:
            copy.start()
    products = [jnp.sum(sums[i], axis=0, keepdims=True) for i in range(k + 1)]
    products = jnp.concatenate(products + [jnp.zeros_like(products[0])] * (7 - k), axis=0)
    store_split(split, products, k + 1)
    dots = split[...].astype(BF16)
    inner = send.shape[0]
    share = inner // sent.shape[0]

    def leave(i):
        part = pl.ds(i * share, share)
        return pltpu.make_async_copy(send.at[part], send_any.at[part], sent.at[i])

    if sends:
        lifted = upward[...].astype(BF16)
        slots = send_slot.shape[0]
        for r in range(inner):
            for s in range(slots):
                send[r, s * rank : (s + 1) * rank] = skeletons[send_slot[s, r]]
            send[r, slots * rank : (slots + 1) * rank] = lifted
            send[r, (slots + 1) * rank :] = dots
            if r % share == share - 1:
                leave(r // share).start()
    else:
        for r in range(inner):
            send[r] = dots
        for i in range(sent.shape[0]):
            leave(i).start()
    for i in range(CHUNKS):
        for copy in stores(i):
            copy.wait()
    if sends:
        for copy in halos:
            copy.wait()
    for i in range(sent.shape[0]):
        leave(i).wait()


def stage(k, points, send_slot, branch, zs, basis, transfer, later):
    leaves, rank, size = basis.shape
    first, sends = k == 0, k < STEPS
    columns = zs[0].shape[1]
    slots, inner = send_slot.shape
    tall = (leaves * size, columns)
    args = [send_slot, branch] + list(zs)
    if not first:
        ups, state, top, local_far, near = later
        args += [ups, state, top, local_far, near]
    args += [basis, transfer]
    names, shapes, out_specs = [], [], []

    def get(name, shape, dtype, spec=ANY):
        names.append(name)
        shapes.append(jax.ShapeDtypeStruct(shape, dtype))
        out_specs.append(spec)

    if not first:
        get("state", state.shape, F32, pl.BlockSpec(memory_space=pltpu.VMEM))
        get("z", tall, F32)
    sent = (inner, ((slots + 1) * rank if sends else 0) + DOT_ROWS, columns)
    get("send", sent, BF16)
    if sends:
        get("coarse", (leaves, size, columns), BF16)
        get("low", (HW, size, columns), BF16)
        get("high", (HW, size, columns), BF16)

    semaphores = pltpu.SemaphoreType.DMA
    scratch = [
        pltpu.VMEM(basis.shape, BF16),
        pltpu.VMEM(transfer.shape, BF16),
        pltpu.VMEM((len(zs),) + tall, F32),
        pltpu.VMEM(tall if not first else (8, columns), F32),
        pltpu.VMEM((STEPS + 1, 8, columns), F32),
        pltpu.VMEM(sent, BF16),
        pltpu.VMEM((DOT_ROWS, columns), F32),
        semaphores((CHUNKS if sends else 1,)),
        semaphores((len(zs) + 4, CHUNKS)),
        semaphores((3,)),
        semaphores((2, CHUNKS)),
    ]
    if sends:
        scratch += [
            pltpu.VMEM((leaves, size, columns), BF16),
            pltpu.VMEM((leaves, rank, columns), BF16),
            pltpu.VMEM((rank, columns), F32),
            semaphores((2,)),
        ]
    if not first:
        scratch += [
            pltpu.VMEM(ups.shape, BF16),
            pltpu.VMEM(state.shape, F32),
            pltpu.VMEM(top.shape, BF16),
            pltpu.VMEM(local_far.shape, F32),
            pltpu.VMEM(tall, F32),
            pltpu.VMEM((8, columns), F32),
            pltpu.VMEM((rank, columns), BF16),
        ]
    outs = call(
        functools.partial(stage_kernel, k=k, points=points),
        args,
        [SMEM, SMEM] + [ANY] * (len(args) - 2),
        shapes,
        out_specs,
        scratch,
        f"stage{k}",
        1 << 27,
        (k + 4) << 20,
    )
    return dict(zip(names, outs))


def basis_kernel(state_ref, *refs):
    zs, krylov_out = refs[:-1], refs[-1]
    values = [ref[...] for ref in zs]
    for i in range(len(zs)):
        vector = None
        for l in range(i + 1):
            row = basis_row(i, l)
            term = state_ref[row : row + 1, :] * values[l]
            vector = term if vector is None else vector + term
        krylov_out[i] = vector


def basis_vectors(state, zs, leaves):
    points, columns = zs[0].shape
    size = points // leaves
    return pl.pallas_call(
        basis_kernel,
        grid=(leaves,),
        in_specs=[whole(state)] + [by_leaf((size, columns))] * len(zs),
        out_specs=pl.BlockSpec((len(zs), size, columns), lambda l: (0, l, 0)),
        out_shape=jax.ShapeDtypeStruct((written(len(zs)), points, columns), F32),
        compiler_params=pltpu.CompilerParams(vmem_limit_bytes=VMEM_BYTES),
        cost_estimate=pl.CostEstimate(flops=1 << 23, bytes_accessed=8 << 20, transcendentals=0),
        name="basis_vectors",
    )(state, *zs)


def written(count):
    return STEPS + 1


def last_kernel(ups_any, state_any, krylov_in, *refs, points):
    zs = refs[: STEPS + 1]
    krylov_out, hess_out, ups, state_in, state_out, vectors, result = refs[STEPS + 1 : -3]
    came, arrived, left = refs[-3:]
    part = result.shape[0] // CHUNKS

    def rows(i):
        return pl.ds(pl.multiple_of(i * part, part), part)

    def fetches(i):
        return [
            pltpu.make_async_copy(z.at[rows(i)], vectors.at[l, rows(i)], arrived.at[l, i])
            for l, z in enumerate(zs)
        ]

    def store(i):
        return pltpu.make_async_copy(
            result.at[rows(i)], krylov_out.at[STEPS, rows(i)], left.at[i]
        )

    small = [
        pltpu.make_async_copy(ups_any, ups, came.at[0]),
        pltpu.make_async_copy(state_any, state_in, came.at[1]),
    ]
    for copy in small:
        copy.start()
    for i in range(CHUNKS):
        for copy in fetches(i):
            copy.start()
    for copy in small:
        copy.wait()
    grams = [row / points for row in from_branches(ups, 0)]
    state_out[...] = state_in[...]
    coefficients(STEPS, grams, state_in, state_out)
    for i in range(STEPS + 1):
        for j in range(STEPS):
            row = i * STEPS + j
            if i <= j + 1:
                hess_out[i, j : j + 1, :] = state_out[row : row + 1, :]
            else:
                hess_out[i, j : j + 1, :] = jnp.zeros((1, hess_out.shape[2]), F32)

    def body(i, carry):
        for copy in fetches(i):
            copy.wait()
        vector = None
        for l in range(STEPS + 1):
            row = basis_row(STEPS, l)
            term = state_out[row : row + 1, :] * vectors[l, rows(i)]
            vector = term if vector is None else vector + term
        result[rows(i)] = vector
        store(i).start()
        return carry

    lax.fori_loop(0, CHUNKS, body, 0)
    for i in range(CHUNKS):
        store(i).wait()


def last(points, ups, state, krylov, zs):
    columns = state.shape[1]
    hess = (STEPS + 1, STEPS, columns)
    return call(
        functools.partial(last_kernel, points=points),
        [ups, state, krylov] + list(zs),
        [ANY] * (3 + len(zs)),
        [jax.ShapeDtypeStruct(krylov.shape, F32), jax.ShapeDtypeStruct(hess, F32)],
        [ANY, pl.BlockSpec(memory_space=pltpu.VMEM)],
        [
            pltpu.VMEM(ups.shape, BF16),
            pltpu.VMEM(state.shape, F32),
            pltpu.VMEM(state.shape, F32),
            pltpu.VMEM((len(zs),) + zs[0].shape, F32),
            pltpu.VMEM(zs[0].shape, F32),
            pltpu.SemaphoreType.DMA((2,)),
            pltpu.SemaphoreType.DMA((len(zs), CHUNKS)),
            pltpu.SemaphoreType.DMA((CHUNKS,)),
        ],
        "last_vector",
        1 << 22,
        6 << 20,
        {2: 0},
    )


def shards(
    rhs,
    near_blocks,
    near_index,
    near_mask,
    basis,
    far_blocks,
    far_slot,
    far_mask,
    send_slot,
    transfer,
    top_blocks,
):
    outer, inner = lax.axis_size("outer"), lax.axis_size("inner")
    points = outer * inner * rhs.shape[0]
    leaves, rank = basis.shape[0], basis.shape[1]
    slots = send_slot.shape[2]
    branch = lax.axis_index("outer").astype(jnp.int32).reshape(1)
    up_pairs = [(i, i + 1) for i in range(inner - 1)]
    down_pairs = [(j, i) for i, j in up_pairs]
    wanted = send_slot[0].T
    packed = pack_far(far_blocks, far_mask)

    def exchange(array, axis):
        return lax.all_to_all(array, axis, split_axis=0, concat_axis=0, tiled=True)

    zs = [rhs]
    state = jnp.zeros((STATE_ROWS, rhs.shape[1]), F32)
    out = stage(0, points, wanted, branch, zs, basis, transfer, None)
    for k in range(1, STEPS + 1):
        before = lax.ppermute(out["high"], "inner", up_pairs)
        after = lax.ppermute(out["low"], "inner", down_pairs)
        recv = exchange(tie(out["send"], before, after), "inner")
        earlier = (packed,) if k == 1 else ()
        near = near_field(
            near_index, near_mask, near_blocks, before, out["coarse"], after, *earlier
        )
        summed = gather_sum(recv, slots * rank, outer, near)
        ups = exchange(summed, "outer")
        local_far = far_field(far_slot, recv, packed, slots, summed)
        later = (ups, state, top_blocks, local_far, near)
        out = stage(k, points, wanted, branch, zs, basis, transfer, later)
        state = out["state"]
        zs = zs + [out["z"]]
    krylov = basis_vectors(state, zs[:STEPS], leaves)
    recv = exchange(out["send"], "inner")
    ups = exchange(gather_sum(recv, 0, outer, krylov), "outer")
    return tuple(last(points, ups, state, krylov, zs))


def solution(mesh):
    return jax.shard_map(
        shards,
        mesh=mesh,
        in_specs=(
            P(("outer", "inner"), None),
            P(("outer", "inner"), None, None, None),
            P(("outer", "inner"), None),
            P(("outer", "inner"), None),
            P(("outer", "inner"), None, None),
            P(("outer", "inner"), None, None, None),
            P(("outer", "inner"), None),
            P(("outer", "inner"), None),
            P(("outer", "inner"), None, None),
            P(("outer", "inner"), None, None),
            P("outer", None, None, None),
        ),
        out_specs=(P(None, ("outer", "inner"), None), P()),
        check_vma=False,
    )
```

```python
import functools

import jax
import jax.numpy as jnp
from jax import lax
from jax.experimental import pallas as pl
from jax.experimental.pallas import tpu as pltpu
from jax.sharding import PartitionSpec as P

HW = 2
STEPS = 4
EPS = 1e-06
PIECES = 3
DOT_ROWS = 16
STATE_ROWS = 64
VMEM_BYTES = 32 * 1024 * 1024
BF16 = jnp.bfloat16
F32 = jnp.float32


def dot(a, b):
    return jnp.dot(a, b, preferred_element_type=F32)


def dot_first(a, b):
    return lax.dot_general(a, b, (((0,), (0,)), ((), ())), preferred_element_type=F32)


def store_split(ref, values, count):
    rest = values
    ref[...] = jnp.zeros(ref.shape, F32)
    for piece in range(PIECES):
        part = rest.astype(BF16).astype(F32)
        ref[piece * 5 : piece * 5 + count, :] = part[:count]
        rest = rest - part


def joined(rows):
    return [rows[i : i + 1] + rows[5 + i : 6 + i] + rows[10 + i : 11 + i] for i in range(5)]


def entry_row(i, l):
    low, high = min(i, l), max(i, l)
    return 20 + high * (high + 1) // 2 + low


def basis_row(i, l):
    return 32 + i * (i + 1) // 2 + l


def coefficients(m, grams, state_in, state_out):
    last = m - 1
    entry = lambda i, l: state_in[entry_row(i, l) : entry_row(i, l) + 1, :]
    expand = lambda i, l: state_in[basis_row(i, l) : basis_row(i, l) + 1, :]

    def put(row, value):
        state_out[row : row + 1, :] = value

    dots = []
    for i in range(m):
        dots.append(sum(expand(i, l) * grams[l] for l in range(i + 1)))
    weights = [dots[i] + entry(i, last) for i in range(m)]
    spread = [sum(weights[l] * entry(i, l) for l in range(m)) for i in range(m)]
    square = grams[m]
    for i in range(m):
        square = square + weights[i] * (weights[i] + spread[i] - 2.0 * dots[i])
    total = jnp.maximum(square, 0.0) + EPS
    root = jnp.sqrt(total)
    inverse = 1.0 / root
    for l in range(m):
        value = sum(weights[i] * expand(i, l) for i in range(l, m))
        put(basis_row(m, l), -inverse * value)
    put(basis_row(m, m), inverse)
    for i in range(m):
        put(i * STEPS + last, weights[i] + (1.0 if i == last else 0.0))
    if m > 0:
        put(m * STEPS + last, root)
    if m < STEPS:
        for i in range(m):
            put(entry_row(i, m), (-entry(i, last) - spread[i]) * inverse)
        put(entry_row(m, m), -EPS / total)
    return weights, inverse


def from_branches(ups_ref, rank):
    rows = ups_ref[0, rank:].astype(F32)
    for c in range(1, ups_ref.shape[0]):
        rows = rows + ups_ref[c, rank:].astype(F32)
    return joined(rows)


SMEM = pl.BlockSpec(memory_space=pltpu.SMEM)
VMEM = pl.BlockSpec(memory_space=pltpu.VMEM)
HBM = pl.BlockSpec(memory_space=pl.ANY)
AFTER = pl.BlockSpec(memory_space=pl.ANY)
AFTER_VMEM = pl.BlockSpec(memory_space=pl.ANY)
LOOSE = pl.BlockSpec(memory_space=pl.ANY)
FREE = pl.BlockSpec(memory_space=pltpu.VMEM)
AHEAD = 3
PIN = True


def call(kernel, args, in_specs, outs, scratch, name, flops, moved, aliases={}):
    def pinned(array, spec):
        if not PIN or not any(spec is one for one in (VMEM, HBM, AFTER, AFTER_VMEM)):
            return array
        in_vmem = spec is VMEM or spec is AFTER_VMEM
        return pltpu.with_memory_space_constraint(array, pltpu.VMEM if in_vmem else pltpu.HBM)

    def shape_of(shape, dtype, spec):
        if not PIN or not (spec is VMEM or spec is HBM):
            return jax.ShapeDtypeStruct(shape, dtype)
        return (pltpu.VMEM if spec is VMEM else pltpu.HBM)(shape, dtype)

    return pl.pallas_call(
        kernel,
        in_specs=list(in_specs),
        out_specs=[spec for _, _, spec in outs],
        out_shape=[shape_of(*out) for out in outs],
        scratch_shapes=scratch,
        input_output_aliases=aliases,
        compiler_params=pltpu.CompilerParams(vmem_limit_bytes=VMEM_BYTES),
        cost_estimate=pl.CostEstimate(flops=flops, bytes_accessed=moved, transcendentals=0),
        name=name,
    )(*[pinned(array, spec) for array, spec in zip(args, in_specs)])


def semaphores(*shape):
    return pltpu.SemaphoreType.DMA(shape)


def windowed(count, ahead, fetch, work):
    def start(i):
        for j, copy in enumerate(fetch(i)):
            copy.start(priority=j % 2)

    def body(i, carry):
        @pl.when(i + ahead < count)
        def _():
            start(i + ahead)

        for copy in fetch(i):
            copy.wait()
        work(i)
        return carry

    def begin():
        for i in range(min(ahead, count)):
            start(i)

    return begin, lambda: lax.fori_loop(0, count, body, 0)


def slab(i, size):
    return pl.ds(pl.multiple_of(i * size, size), size)


def pack_kernel(mask_ref, slot_ref, far_ref, out_ref, blocks, total, packed, arrived, left):
    leaves, entries, rank, _ = blocks.shape
    sources, _, width = packed.shape
    slots = width // rank

    def fetch(leaf):
        halves = [pl.ds(j * (entries // 2), entries // 2) for j in range(2)]
        return [
            pltpu.make_async_copy(far_ref.at[leaf, half], blocks.at[leaf, half], arrived.at[leaf, j])
            for j, half in enumerate(halves)
        ]

    def store(leaf):
        rows = slab(leaf, rank)
        return pltpu.make_async_copy(packed.at[:, rows], out_ref.at[:, rows], left.at[leaf])

    def work(leaf):
        total[...] = jnp.zeros(total.shape, F32)
        for f in range(entries):
            weight = mask_ref[leaf, f].astype(F32)
            total[slot_ref[leaf, f]] += blocks[leaf, f].astype(F32) * weight
        rows = slab(leaf, rank)
        for source in range(sources):
            sides = [total[source * slots + s] for s in range(slots)]
            packed[source, rows] = jnp.concatenate(sides, axis=1).astype(BF16)
        store(leaf).start()

    begin, run = windowed(leaves, AHEAD, fetch, work)
    begin()
    run()
    for leaf in range(leaves):
        store(leaf).wait()


def pack_far(far_blocks, far_mask, far_slot, inner, slots):
    leaves, entries, rank, _ = far_blocks.shape
    shape = (inner, leaves * rank, slots * rank)
    return call(
        pack_kernel,
        (far_mask, far_slot, far_blocks),
        (SMEM, SMEM, HBM),
        [(shape, BF16, HBM)],
        [
            pltpu.VMEM(far_blocks.shape, BF16),
            pltpu.VMEM((inner * slots, rank, rank), F32),
            pltpu.VMEM(shape, BF16),
            semaphores(leaves, 2),
            semaphores(leaves),
        ],
        "pack_far",
        0,
        10 << 20,
    )[0]


def near_kernel(index_ref, mask_ref, blocks_ref, own_ref, *refs):
    out_ref, blocks, own, result, arrived, came, left = refs[-7:]
    leaves, entries, size, _ = blocks.shape
    half = entries // 2

    def fetch(i):
        leaf, pairs = i // 2, [pl.ds(i % 2 * half + j * half // 2, half // 2) for j in range(2)]
        return [
            pltpu.make_async_copy(
                blocks_ref.at[leaf, pair], blocks.at[leaf, pair], arrived.at[i, j]
            )
            for j, pair in enumerate(pairs)
        ]

    def store(leaf):
        return pltpu.make_async_copy(
            result.at[leaf], out_ref.at[slab(leaf, size)], left.at[leaf]
        )

    def work(i):
        leaf, part = i // 2, i % 2
        total = None
        for j in range(half):
            n = part * half + j
            place = index_ref[leaf, n] - HW
            inside = (place >= 0) & (place < leaves)
            weight = jnp.where(inside, mask_ref[leaf, n], 0).astype(F32).astype(BF16)
            values = own[jnp.clip(place, 0, leaves - 1)] * weight
            term = dot(blocks[leaf, n], values)
            total = term if total is None else total + term

        @pl.when(part == 0)
        def _():
            result[leaf] = total

        @pl.when(part == 1)
        def _():
            result[leaf] += total
            store(leaf).start()

    begin, run = windowed(2 * leaves, 2 * AHEAD, fetch, work)
    copy = pltpu.make_async_copy(own_ref, own, came)
    copy.start()
    begin()
    copy.wait()
    run()
    for leaf in range(leaves):
        store(leaf).wait()


def near_field(near_index, near_mask, near_blocks, own, *earlier):
    leaves, _, size, _ = near_blocks.shape
    columns = own.shape[2]
    return call(
        near_kernel,
        (near_index, near_mask, near_blocks, own) + earlier,
        (SMEM, SMEM, HBM, HBM) + (AFTER,) * len(earlier),
        [((leaves * size, columns), F32, HBM)],
        [
            pltpu.VMEM(near_blocks.shape, BF16),
            pltpu.VMEM(own.shape, BF16),
            pltpu.VMEM((leaves, size, columns), F32),
            semaphores(2 * leaves, 2),
            semaphores(),
            semaphores(leaves),
        ],
        "near_field",
        2 * near_blocks.size * columns,
        2 * near_blocks.size,
    )[0]


def gather_sum_kernel(recv, *refs, lead):
    out_ref, split = refs[-2:]
    rank = out_ref.shape[1] - DOT_ROWS
    total = recv[0, lead:].astype(F32)
    for i in range(1, recv.shape[0]):
        total = total + recv[i, lead:].astype(F32)
    store_split(split, jnp.concatenate(joined(total[rank:]), axis=0), 5)
    dots = split[...].astype(BF16)
    for c in range(out_ref.shape[0]):
        if rank > 0:
            out_ref[c, :rank] = total[:rank].astype(BF16)
        out_ref[c, rank:] = dots


def gather_sum(recv, lead, outer, earlier):
    _, rows, columns = recv.shape
    return call(
        functools.partial(gather_sum_kernel, lead=lead),
        (recv, earlier),
        (VMEM, AFTER),
        [((outer, rows - lead, columns), BF16, VMEM)],
        [pltpu.VMEM((DOT_ROWS, columns), F32)],
        "gather_sum",
        1 << 20,
        1 << 19,
    )[0]


def late_kernel(index_ref, mask_ref, recv, packed_ref, blocks_ref, before, after, near_ref, *refs):
    out_ref, far_ref, packed, blocks, halo, near, far = refs[1:8]
    arrived, came, fetched, near_came, left, far_left = refs[8:]
    leaves, entries, size, _ = blocks.shape
    sources, _, width = packed.shape
    reach = before.shape[0]

    rows = packed.shape[1] // 2

    def fetch(i):
        halves = [pl.ds(j * rows, rows) for j in range(2)]
        return [
            pltpu.make_async_copy(packed_ref.at[i, half], packed.at[i, half], arrived.at[i, j])
            for j, half in enumerate(halves)
        ]

    sides = [
        pltpu.make_async_copy(before, halo.at[pl.ds(0, reach)], came.at[0]),
        pltpu.make_async_copy(after, halo.at[pl.ds(reach, reach)], came.at[1]),
    ]

    def get(leaf):
        return pltpu.make_async_copy(
            near_ref.at[slab(leaf, size)], near.at[leaf], near_came.at[leaf]
        )

    def store(leaf):
        return pltpu.make_async_copy(near.at[leaf], out_ref.at[slab(leaf, size)], left.at[leaf])

    def for_halo(leaf, do):
        for n in range(entries):
            place = index_ref[leaf, n]
            low = place < reach

            @pl.when((mask_ref[leaf, n] != 0) & (low | (place >= reach + leaves)))
            def _():
                block = pltpu.make_async_copy(
                    blocks_ref.at[leaf, n], blocks.at[leaf, n], fetched.at[leaf, n]
                )
                do(n, jnp.where(low, place, place - leaves), block)

    def ask(leaf, carry):
        for_halo(leaf, lambda n, place, block: block.start(priority=n % 2))
        return carry

    def work(i):
        term = dot(packed[i], recv[i, :width])

        @pl.when(i == 0)
        def _():
            far[...] = term

        @pl.when(i > 0)
        def _():
            far[...] += term

    def add(leaf, carry):
        get(leaf).wait()

        def one(n, place, block):
            block.wait()
            near[leaf] += dot(blocks[leaf, n], halo[place])

        for_halo(leaf, one)
        store(leaf).start()
        return carry

    begin, run = windowed(sources, 2 * AHEAD, fetch, work)
    begin()
    for side in sides:
        side.start()
    lax.fori_loop(0, leaves, ask, 0)
    for leaf in range(leaves):
        get(leaf).start(priority=leaf % 2)
    run()
    out = pltpu.make_async_copy(far, far_ref, far_left)
    out.start()
    for side in sides:
        side.wait()
    lax.fori_loop(0, leaves, add, 0)
    for leaf in range(leaves):
        store(leaf).wait()
    out.wait()


def late_fields(near_index, near_mask, recv, packed, near_blocks, before, after, near, earlier):
    leaves, _, size, _ = near_blocks.shape
    sources, rows, _ = packed.shape
    columns = recv.shape[2]
    halo = (2 * before.shape[0],) + before.shape[1:]
    return call(
        late_kernel,
        (near_index, near_mask, recv, packed, near_blocks, before, after, near, earlier),
        (SMEM, SMEM, VMEM, HBM, HBM, LOOSE, LOOSE, HBM, AFTER_VMEM),
        [(near.shape, F32, HBM), ((rows, columns), F32, HBM)],
        [
            pltpu.VMEM(packed.shape, BF16),
            pltpu.VMEM(near_blocks.shape, BF16),
            pltpu.VMEM(halo, BF16),
            pltpu.VMEM((leaves, size, columns), F32),
            pltpu.VMEM((rows, columns), F32),
            semaphores(sources, 2),
            semaphores(2),
            semaphores(leaves, near_blocks.shape[1]),
            semaphores(leaves),
            semaphores(leaves),
            semaphores(),
        ],
        "late_fields",
        2 * packed.size * columns,
        2 * packed.size + (1 << 20),
    )


def stage_kernel(*refs, k, points):
    refs = list(refs)
    take = lambda count: [refs.pop(0) for _ in range(count)]
    m = k - 1
    first, sends = k == 0, k < STEPS
    send_slot, branch = take(2)
    zs = take(max(k, 1))
    if not first:
        ups, state, top_any, far_any, near_any = take(5)
    basis_any, transfer_any = take(2)
    if not first:
        (z_any,) = take(1)
    state_out, send = take(2)
    if sends:
        coarse_any, low_any, high_any = take(3)
    basis, transfer, vectors, sums, split, arrived, came, left = take(8)
    if sends:
        coarse, skeletons, upward, out = take(4)
    if not first:
        top, far, near, result, coef, incoming = take(6)

    leaves, rank, size = basis.shape

    def fetch(i):
        pairs = [(z.at[slab(i, size)], vectors.at[l, i]) for l, z in enumerate(zs)]
        if first:
            half = size // 2
            rows = [pl.ds(pl.multiple_of(i * size + j * half, half), half) for j in range(2)]
            pairs = [(zs[0].at[rows[j]], vectors.at[0, i, pl.ds(j * half, half)]) for j in range(2)]
        else:
            pairs.append((near_any.at[slab(i, size)], near.at[i]))
            pairs.append((far_any.at[slab(i, rank)], far.at[i]))
        return [
            pltpu.make_async_copy(source, target, arrived.at[n, i])
            for n, (source, target) in enumerate(pairs)
        ]

    def stores(i):
        pairs = []
        if not first:
            pairs.append((result.at[i], z_any.at[slab(i, size)]))
        if sends:
            pairs.append((coarse.at[i], coarse_any.at[i]))
        return [
            pltpu.make_async_copy(source, target, left.at[n, i])
            for n, (source, target) in enumerate(pairs)
        ]

    def one_leaf(leaf):
        others = [vectors[l, leaf] for l in range(len(zs))]
        if first:
            z = others.pop()
        else:
            combined = far[leaf] + dot(transfer[leaf], incoming[...])
            z = near[leaf] + dot_first(basis[leaf], combined.astype(BF16))
            for i in range(m):
                z = z - coef[i : i + 1, :] * others[i + 1]
            z = z * coef[STEPS : STEPS + 1, :]
            result[leaf] = z
        if sends:
            rounded = z.astype(BF16)
            coarse[leaf] = rounded
        for j, copy in enumerate(stores(leaf)):
            copy.start(priority=j)
        if sends:
            skeleton = dot(basis[leaf], rounded).astype(BF16)
            skeletons[leaf] = skeleton
            upward[...] += dot_first(transfer[leaf], skeleton)
        for i, other in enumerate(others + [z]):
            sums[i] += jnp.sum((z * other).reshape(size // 8, 8, z.shape[1]), axis=0)

    begin, run = windowed(leaves, AHEAD, fetch, one_leaf)
    small = [
        pltpu.make_async_copy(basis_any, basis, came.at[0]),
        pltpu.make_async_copy(transfer_any, transfer, came.at[1]),
    ]
    if not first:
        small.insert(0, pltpu.make_async_copy(top_any, top, came.at[2]))
    for j, copy in enumerate(small):
        copy.start(priority=(j + 1) % 2)
    begin()
    sums[...] = jnp.zeros(sums.shape, F32)
    if sends:
        upward[...] = jnp.zeros(upward.shape, F32)
    if first:
        state_out[...] = jnp.zeros(state_out.shape, F32)
    else:
        grams = [row / points for row in from_branches(ups, rank)]
        state_out[...] = state[...]
        weights, inverse = coefficients(m, grams, state, state_out)
        for i, weight in enumerate(weights):
            coef[i : i + 1, :] = weight
        coef[STEPS : STEPS + 1, :] = inverse
        small.pop(0).wait()
        total = None
        for c in range(ups.shape[0]):
            weight = (branch[0] != c).astype(F32).astype(BF16)
            term = dot(top[0, c] * weight, ups[c, :rank])
            total = term if total is None else total + term
        incoming[...] = total.astype(BF16)
    for copy in small:
        copy.wait()
    run()

    if sends:
        halos = [
            pltpu.make_async_copy(coarse.at[pl.ds(0, HW)], low_any, out.at[0]),
            pltpu.make_async_copy(coarse.at[pl.ds(leaves - HW, HW)], high_any, out.at[1]),
        ]
        for j, copy in enumerate(halos):
            copy.start(priority=j)
    products = [jnp.sum(sums[i], axis=0, keepdims=True) for i in range(k + 1)]
    products = jnp.concatenate(products + [jnp.zeros_like(products[0])] * (7 - k), axis=0)
    store_split(split, products, k + 1)
    dots = split[...].astype(BF16)
    inner = send.shape[0]
    if sends:
        lifted = upward[...].astype(BF16)
        slots = send_slot.shape[0]
        for r in range(inner):
            for s in range(slots):
                send[r, s * rank : (s + 1) * rank] = skeletons[send_slot[s, r]]
            send[r, slots * rank : (slots + 1) * rank] = lifted
            send[r, (slots + 1) * rank :] = dots
    else:
        for r in range(inner):
            send[r] = dots
    for i in range(leaves):
        for copy in stores(i):
            copy.wait()
    if sends:
        for copy in halos:
            copy.wait()


def stage(k, points, send_slot, branch, zs, basis, transfer, later):
    leaves, rank, size = basis.shape
    first, sends = k == 0, k < STEPS
    columns = zs[0].shape[1]
    slots, inner = send_slot.shape
    tall = (leaves, size, columns)
    names, outs = [], []

    def get(name, shape, dtype, spec):
        names.append(name)
        outs.append((shape, dtype, spec))

    args = [send_slot, branch] + list(zs)
    specs = [SMEM, SMEM] + [HBM] * len(zs)
    if not first:
        args += list(later)
        specs += [VMEM, VMEM, HBM, HBM, HBM]
    args += [basis, transfer]
    specs += [HBM, HBM]
    if not first:
        get("z", (leaves * size, columns), F32, HBM)
    get("state", (STATE_ROWS, columns), F32, VMEM)
    rows = ((slots + 1) * rank if sends else 0) + DOT_ROWS
    get("send", (inner, rows, columns), BF16, VMEM)
    if sends:
        get("coarse", tall, BF16, HBM)
        get("low", (HW, size, columns), BF16, LOOSE)
        get("high", (HW, size, columns), BF16, LOOSE)

    scratch = [
        pltpu.VMEM(basis.shape, BF16),
        pltpu.VMEM(transfer.shape, BF16),
        pltpu.VMEM((len(zs),) + tall, F32),
        pltpu.VMEM((STEPS + 1, 8, columns), F32),
        pltpu.VMEM((DOT_ROWS, columns), F32),
        semaphores(len(zs) + 2, leaves),
        semaphores(3),
        semaphores(2, leaves),
    ]
    if sends:
        scratch += [
            pltpu.VMEM(tall, BF16),
            pltpu.VMEM((leaves, rank, columns), BF16),
            pltpu.VMEM((rank, columns), F32),
            semaphores(2),
        ]
    if not first:
        scratch += [
            pltpu.VMEM(later[2].shape, BF16),
            pltpu.VMEM((leaves, rank, columns), F32),
            pltpu.VMEM(tall, F32),
            pltpu.VMEM(tall, F32),
            pltpu.VMEM((8, columns), F32),
            pltpu.VMEM((rank, columns), BF16),
        ]
    results = call(
        functools.partial(stage_kernel, k=k, points=points),
        args,
        specs,
        outs,
        scratch,
        f"stage{k}",
        1 << 27,
        (k + 4) << 20,
    )
    return dict(zip(names, results))


def vectors_kernel(*refs, known, points):
    refs = list(refs)
    take = lambda count: [refs.pop(0) for _ in range(count)]
    (state,) = take(1)
    if not known:
        (ups,) = take(1)
    zs = take(known if known else STEPS + 1)
    if known:
        (krylov,) = take(1)
    else:
        _, krylov, hess_out = take(3)
    vectors, result, arrived, left = take(4)
    (after,) = take(1) if not known else (state,)
    parts = arrived.shape[1]
    part = result.shape[1] // parts
    wanted = range(known) if known else [STEPS]

    def fetch(i):
        return [
            pltpu.make_async_copy(
                z.at[slab(i, part)], vectors.at[l, slab(i, part)], arrived.at[l, i]
            )
            for l, z in enumerate(zs)
        ]

    def store(n, i):
        return pltpu.make_async_copy(
            result.at[n, slab(i, part)], krylov.at[wanted[n], slab(i, part)], left.at[n, i]
        )

    def work(i):
        for n, j in enumerate(wanted):
            vector = None
            for l in range(j + 1):
                row = basis_row(j, l)
                term = after[row : row + 1, :] * vectors[l, slab(i, part)]
                vector = term if vector is None else vector + term
            result[n, slab(i, part)] = vector
            store(n, i).start()

    begin, run = windowed(parts, AHEAD, fetch, work)
    begin()
    if not known:
        grams = [row / points for row in from_branches(ups, 0)]
        after[...] = state[...]
        coefficients(STEPS, grams, state, after)
    run()
    if not known:
        for i in range(STEPS + 1):
            for j in range(STEPS):
                row = i * STEPS + j
                if i <= j + 1:
                    hess_out[i, j : j + 1, :] = after[row : row + 1, :]
                else:
                    hess_out[i, j : j + 1, :] = jnp.zeros((1, hess_out.shape[2]), F32)
    for n in range(len(wanted)):
        for i in range(parts):
            store(n, i).wait()


def basis_vectors(state, zs, parts):
    known = len(zs)
    tall = zs[0].shape
    return call(
        functools.partial(vectors_kernel, known=known, points=0),
        [state] + zs,
        [VMEM] + [HBM] * known,
        [((STEPS + 1,) + tall, F32, HBM)],
        [
            pltpu.VMEM((known,) + tall, F32),
            pltpu.VMEM((known,) + tall, F32),
            semaphores(known, parts),
            semaphores(known, parts),
        ],
        "basis_vectors",
        1 << 23,
        8 << 20,
    )[0]


def last(points, ups, state, krylov, zs, parts):
    tall = zs[0].shape
    return call(
        functools.partial(vectors_kernel, known=0, points=points),
        [state, ups] + list(zs) + [krylov],
        [VMEM, VMEM] + [HBM] * len(zs) + [HBM],
        [(krylov.shape, F32, HBM), ((STEPS + 1, STEPS, tall[1]), F32, FREE)],
        [
            pltpu.VMEM((len(zs),) + tall, F32),
            pltpu.VMEM((1,) + tall, F32),
            semaphores(len(zs), parts),
            semaphores(1, parts),
            pltpu.VMEM(state.shape, F32),
        ],
        "last_vector",
        1 << 22,
        6 << 20,
        {2 + len(zs): 0},
    )


def shards(
    rhs,
    near_blocks,
    near_index,
    near_mask,
    basis,
    far_blocks,
    far_slot,
    far_mask,
    send_slot,
    transfer,
    top_blocks,
):
    outer, inner = lax.axis_size("outer"), lax.axis_size("inner")
    points = outer * inner * rhs.shape[0]
    leaves, rank = basis.shape[:2]
    slots = send_slot.shape[2]
    branch = lax.axis_index("outer").astype(jnp.int32).reshape(1)
    up_pairs = [(i, i + 1) for i in range(inner - 1)]
    down_pairs = [(j, i) for i, j in up_pairs]
    wanted = send_slot[0].T

    def exchange(array, axis):
        return lax.all_to_all(array, axis, split_axis=0, concat_axis=0, tiled=True)

    out = stage(0, points, wanted, branch, [rhs], basis, transfer, None)
    packed = pack_far(far_blocks, far_mask, far_slot, inner, slots)
    zs, state = [rhs], out["state"]
    for k in range(1, STEPS + 1):
        recv = exchange(out["send"], "inner")
        before = lax.ppermute(out["high"], "inner", up_pairs)
        after = lax.ppermute(out["low"], "inner", down_pairs)
        earlier = (packed,) if k == 1 else ()
        near = near_field(near_index, near_mask, near_blocks, out["coarse"], *earlier)
        summed = gather_sum(recv, slots * rank, outer, near)
        ups = exchange(summed, "outer")
        near, local_far = late_fields(
            near_index, near_mask, recv, packed, near_blocks, before, after, near, summed
        )
        later = (ups, state, top_blocks, local_far, near)
        out = stage(k, points, wanted, branch, zs, basis, transfer, later)
        state = out["state"]
        zs = zs + [out["z"]]
    krylov = basis_vectors(state, zs[:STEPS], leaves)
    recv = exchange(out["send"], "inner")
    ups = exchange(gather_sum(recv, 0, outer, krylov), "outer")
    return tuple(last(points, ups, state, krylov, zs, leaves))


def solution(mesh):
    return jax.shard_map(
        shards,
        mesh=mesh,
        in_specs=(
            P(("outer", "inner"), None),
            P(("outer", "inner"), None, None, None),
            P(("outer", "inner"), None),
            P(("outer", "inner"), None),
            P(("outer", "inner"), None, None),
            P(("outer", "inner"), None, None, None),
            P(("outer", "inner"), None),
            P(("outer", "inner"), None),
            P(("outer", "inner"), None, None),
            P(("outer", "inner"), None, None),
            P("outer", None, None, None),
        ),
        out_specs=(P(None, ("outer", "inner"), None), P()),
        check_vma=False,
    )
```

```python
import functools

import jax
import jax.numpy as jnp
from jax import lax
from jax.experimental import pallas as pl
from jax.experimental.pallas import tpu as pltpu
from jax.sharding import PartitionSpec as P

HW = 2
STEPS = 4
EPS = 1e-06
PIECES = 3
DOT_ROWS = 16
STATE_ROWS = 64
VMEM_BYTES = 32 * 1024 * 1024
BF16 = jnp.bfloat16
F32 = jnp.float32


def dot(a, b):
    return jnp.dot(a, b, preferred_element_type=F32)


def dot_first(a, b):
    return lax.dot_general(a, b, (((0,), (0,)), ((), ())), preferred_element_type=F32)


def store_split(ref, values, count):
    rest = values
    ref[...] = jnp.zeros(ref.shape, F32)
    for piece in range(PIECES):
        part = rest.astype(BF16).astype(F32)
        ref[piece * 5 : piece * 5 + count, :] = part[:count]
        rest = rest - part


def joined(rows):
    return [rows[i : i + 1] + rows[5 + i : 6 + i] + rows[10 + i : 11 + i] for i in range(5)]


def entry_row(i, l):
    low, high = min(i, l), max(i, l)
    return 20 + high * (high + 1) // 2 + low


def basis_row(i, l):
    return 32 + i * (i + 1) // 2 + l


def coefficients(m, grams, state_in, state_out):
    last = m - 1
    entry = lambda i, l: state_in[entry_row(i, l) : entry_row(i, l) + 1, :]
    expand = lambda i, l: state_in[basis_row(i, l) : basis_row(i, l) + 1, :]

    def put(row, value):
        state_out[row : row + 1, :] = value

    dots = []
    for i in range(m):
        dots.append(sum(expand(i, l) * grams[l] for l in range(i + 1)))
    weights = [dots[i] + entry(i, last) for i in range(m)]
    spread = [sum(weights[l] * entry(i, l) for l in range(m)) for i in range(m)]
    square = grams[m]
    for i in range(m):
        square = square + weights[i] * (weights[i] + spread[i] - 2.0 * dots[i])
    total = jnp.maximum(square, 0.0) + EPS
    root = jnp.sqrt(total)
    inverse = 1.0 / root
    for l in range(m):
        value = sum(weights[i] * expand(i, l) for i in range(l, m))
        put(basis_row(m, l), -inverse * value)
    put(basis_row(m, m), inverse)
    for i in range(m):
        put(i * STEPS + last, weights[i] + (1.0 if i == last else 0.0))
    if m > 0:
        put(m * STEPS + last, root)
    if m < STEPS:
        for i in range(m):
            put(entry_row(i, m), (-entry(i, last) - spread[i]) * inverse)
        put(entry_row(m, m), -EPS / total)
    return weights, inverse


def from_branches(ups_ref, rank):
    rows = ups_ref[0, rank:].astype(F32)
    for c in range(1, ups_ref.shape[0]):
        rows = rows + ups_ref[c, rank:].astype(F32)
    return joined(rows)


SMEM = pl.BlockSpec(memory_space=pltpu.SMEM)
VMEM = pl.BlockSpec(memory_space=pltpu.VMEM)
HBM = pl.BlockSpec(memory_space=pl.ANY)
AFTER = pl.BlockSpec(memory_space=pl.ANY)
AFTER_VMEM = pl.BlockSpec(memory_space=pl.ANY)
LOOSE = pl.BlockSpec(memory_space=pl.ANY)
FREE = pl.BlockSpec(memory_space=pltpu.VMEM)
AHEAD = 3
CHUNKS = 4
PIN = True


def call(kernel, args, in_specs, outs, scratch, name, flops, moved, aliases={}):
    def pinned(array, spec):
        if not PIN or not any(spec is one for one in (VMEM, HBM, AFTER, AFTER_VMEM)):
            return array
        in_vmem = spec is VMEM or spec is AFTER_VMEM
        return pltpu.with_memory_space_constraint(array, pltpu.VMEM if in_vmem else pltpu.HBM)

    def shape_of(shape, dtype, spec):
        if not PIN or not (spec is VMEM or spec is HBM):
            return jax.ShapeDtypeStruct(shape, dtype)
        return (pltpu.VMEM if spec is VMEM else pltpu.HBM)(shape, dtype)

    return pl.pallas_call(
        kernel,
        in_specs=list(in_specs),
        out_specs=[spec for _, _, spec in outs],
        out_shape=[shape_of(*out) for out in outs],
        scratch_shapes=scratch,
        input_output_aliases=aliases,
        compiler_params=pltpu.CompilerParams(vmem_limit_bytes=VMEM_BYTES),
        cost_estimate=pl.CostEstimate(flops=flops, bytes_accessed=moved, transcendentals=0),
        name=name,
    )(*[pinned(array, spec) for array, spec in zip(args, in_specs)])


def semaphores(*shape):
    return pltpu.SemaphoreType.DMA(shape)


def windowed(count, ahead, fetch, work):
    def start(i):
        for j, copy in enumerate(fetch(i)):
            copy.start(priority=j % 2)

    def body(i, carry):
        @pl.when(i + ahead < count)
        def _():
            start(i + ahead)

        for copy in fetch(i):
            copy.wait()
        work(i)
        return carry

    def begin():
        for i in range(min(ahead, count)):
            start(i)

    return begin, lambda: lax.fori_loop(0, count, body, 0)


def slab(i, size):
    return pl.ds(pl.multiple_of(i * size, size), size)


def pack_kernel(branch, mask_ref, slot_ref, index_ref, near_mask_ref, far_ref, *refs):
    basis_ref, transfer_ref, top_ref = refs[:3]
    out_ref, count_ref, list_ref, basis_out, transfer_out, top_out = refs[3:9]
    blocks, total, packed, basis, transfer, top, turned, lifting, row, arrived, left, came = refs[9:]
    leaves, entries, rank, _ = blocks.shape
    sources, _, width = packed.shape
    slots = width // rank
    near_entries = index_ref.shape[1]

    def fetch(leaf):
        return [pltpu.make_async_copy(far_ref.at[leaf], blocks.at[leaf], arrived.at[leaf])]

    def store(leaf):
        rows = slab(leaf, rank)
        return pltpu.make_async_copy(packed.at[:, rows], out_ref.at[:, rows], left.at[leaf])

    def work(leaf):
        total[...] = jnp.zeros(total.shape, F32)
        for f in range(entries):
            weight = mask_ref[leaf, f].astype(F32)
            total[slot_ref[leaf, f]] += blocks[leaf, f].astype(F32) * weight
        rows = slab(leaf, rank)
        for source in range(sources):
            sides = [total[source * slots + s] for s in range(slots)]
            packed[source, rows] = jnp.concatenate(sides, axis=1).astype(BF16)
        store(leaf).start()

    def list_one(i, count):
        leaf, n = i // near_entries, i % near_entries
        place = index_ref[leaf, n]
        hit = (near_mask_ref[leaf, n] != 0) & ((place < HW) | (place >= HW + leaves))
        list_ref[i] = 0

        @pl.when(hit)
        def _():
            list_ref[count] = i

        return count + hit.astype(jnp.int32)

    small = [
        pltpu.make_async_copy(basis_ref, basis, came.at[0]),
        pltpu.make_async_copy(transfer_ref, transfer, came.at[1]),
        pltpu.make_async_copy(top_ref, top, came.at[2]),
    ]
    for copy in small:
        copy.start()
    begin, run = windowed(leaves, AHEAD, fetch, work)
    begin()
    count_ref[0] = lax.fori_loop(0, list_ref.shape[0], list_one, 0)
    for copy in small:
        copy.wait()
    turn = lambda a: a.astype(F32).T.astype(BF16)
    for leaf in range(leaves):
        turned[leaf] = turn(basis[leaf])
    for pair in range(leaves // 2):
        columns = slice(pair * 2 * rank, (pair + 1) * 2 * rank)
        sides = [turn(transfer[2 * pair + j]) for j in range(2)]
        lifting[:, columns] = jnp.concatenate(sides, axis=1)
    for pair in range(top.shape[1] // 2):
        columns = slice(pair * 2 * rank, (pair + 1) * 2 * rank)
        sides = []
        for c in (2 * pair, 2 * pair + 1):
            sides.append(top[0, c] * (branch[0] != c).astype(F32).astype(BF16))
        row[:, columns] = jnp.concatenate(sides, axis=1)
    results = [
        pltpu.make_async_copy(turned, basis_out, came.at[0]),
        pltpu.make_async_copy(lifting, transfer_out, came.at[1]),
        pltpu.make_async_copy(row, top_out, came.at[2]),
    ]
    for copy in results:
        copy.start()
    run()
    for leaf in range(leaves):
        store(leaf).wait()
    for copy in results:
        copy.wait()


def pack(branch, basis, transfer, top_blocks, far_blocks, far_mask, far_slot, near_index, near_mask, inner, slots):
    leaves, entries, rank, _ = far_blocks.shape
    shape = (inner, leaves * rank, slots * rank)
    turned = (leaves, basis.shape[2], rank)
    lifting = (rank, leaves * rank)
    row = (rank, top_blocks.shape[1] * rank)
    return call(
        pack_kernel,
        (branch, far_mask, far_slot, near_index, near_mask, far_blocks, basis, transfer, top_blocks),
        (SMEM,) * 5 + (HBM,) * 4,
        [
            (shape, BF16, HBM),
            ((1,), jnp.int32, SMEM),
            ((near_index.size,), jnp.int32, SMEM),
            (turned, BF16, HBM),
            (lifting, BF16, HBM),
            (row, BF16, HBM),
        ],
        [
            pltpu.VMEM(far_blocks.shape, BF16),
            pltpu.VMEM((inner * slots, rank, rank), F32),
            pltpu.VMEM(shape, BF16),
            pltpu.VMEM(basis.shape, BF16),
            pltpu.VMEM(transfer.shape, BF16),
            pltpu.VMEM(top_blocks.shape, BF16),
            pltpu.VMEM(turned, BF16),
            pltpu.VMEM(lifting, BF16),
            pltpu.VMEM(row, BF16),
            semaphores(leaves),
            semaphores(leaves),
            semaphores(3),
        ],
        "pack",
        0,
        10 << 20,
    )


def near_kernel(index_ref, mask_ref, blocks_ref, own_ref, *refs):
    out_ref, blocks, own, result, arrived, came, left = refs[-7:]
    leaves, entries, size, _ = blocks.shape

    def fetch(leaf):
        halves = [pl.ds(j * (entries // 2), entries // 2) for j in range(2)]
        return [
            pltpu.make_async_copy(
                blocks_ref.at[leaf, half], blocks.at[leaf, half], arrived.at[leaf, j]
            )
            for j, half in enumerate(halves)
        ]

    def store(leaf):
        return pltpu.make_async_copy(
            result.at[leaf], out_ref.at[leaf], left.at[leaf]
        )

    def work(leaf):
        total = None
        for n in range(entries):
            place = index_ref[leaf, n] - HW
            inside = (place >= 0) & (place < leaves)
            weight = jnp.where(inside, mask_ref[leaf, n], 0).astype(F32).astype(BF16)
            values = own[jnp.clip(place, 0, leaves - 1)] * weight
            term = dot(blocks[leaf, n], values)
            total = term if total is None else total + term
        result[leaf] = total
        store(leaf).start()

    begin, run = windowed(leaves, AHEAD, fetch, work)
    copy = pltpu.make_async_copy(own_ref, own, came)
    copy.start()
    begin()
    copy.wait()
    run()
    for leaf in range(leaves):
        store(leaf).wait()


def near_field(near_index, near_mask, near_blocks, own, *earlier):
    leaves, _, size, _ = near_blocks.shape
    columns = own.shape[2]
    return call(
        near_kernel,
        (near_index, near_mask, near_blocks, own) + earlier,
        (SMEM, SMEM, HBM, HBM) + (AFTER,) * len(earlier),
        [((leaves, size, columns), F32, HBM)],
        [
            pltpu.VMEM(near_blocks.shape, BF16),
            pltpu.VMEM(own.shape, BF16),
            pltpu.VMEM((leaves, size, columns), F32),
            semaphores(leaves, 2),
            semaphores(),
            semaphores(leaves),
        ],
        "near_field",
        2 * near_blocks.size * columns,
        2 * near_blocks.size,
    )[0]


def gather_sum_kernel(recv, *refs, lead):
    out_ref, split = refs[-2:]
    rank = out_ref.shape[0] - DOT_ROWS
    total = recv[0, lead:].astype(F32)
    for i in range(1, recv.shape[0]):
        total = total + recv[i, lead:].astype(F32)
    store_split(split, jnp.concatenate(joined(total[rank:]), axis=0), 5)
    if rank > 0:
        out_ref[:rank] = total[:rank].astype(BF16)
    out_ref[rank:] = split[...].astype(BF16)


def gather_sum(recv, lead, earlier):
    _, rows, columns = recv.shape
    return call(
        functools.partial(gather_sum_kernel, lead=lead),
        (recv, earlier),
        (VMEM, AFTER),
        [((rows - lead, columns), BF16, VMEM)],
        [pltpu.VMEM((DOT_ROWS, columns), F32)],
        "gather_sum",
        1 << 20,
        1 << 19,
    )[0]


def stack_kernel(*refs):
    for i, ref in enumerate(refs[:-2]):
        refs[-1][i] = ref[...]


def over_branches(summed, outer, earlier, between):
    shifts = [[(o, (o + 2 * j) % outer) for o in range(outer)] for j in range(1, outer // 2)]
    parts = [summed] + [lax.ppermute(summed, "outer", shift) for shift in shifts]
    column = call(
        stack_kernel,
        parts + [earlier],
        [VMEM] * len(parts) + [AFTER_VMEM],
        [((len(parts),) + summed.shape, BF16, VMEM)],
        [],
        "stack",
        0,
        1 << 18,
    )[0]
    other = lax.ppermute(column, "outer", [(o, o ^ 1) for o in range(outer)])
    return column, other, between(column)


def in_order(branch, column, other, ups):
    count = ups.shape[0]
    for j in range(count // 2):
        ups[lax.rem(branch[0] + count - 2 * j, count)] = column[j]
        mate = branch[0] + 1 - 2 * lax.rem(branch[0], 2)
        ups[lax.rem(mate + count - 2 * j, count)] = other[j]


def far_kernel(recv, packed_ref, _, far, packed, arrived):
    sources, _, width = packed.shape
    share = sources // CHUNKS

    def fetch(i):
        some = slab(i, share)
        return [pltpu.make_async_copy(packed_ref.at[some], packed.at[some], arrived.at[i])]

    def work(i):
        term = None
        for j in range(share):
            source = i * share + j
            one = dot(packed[source], recv[source, :width])
            term = one if term is None else term + one

        @pl.when(i == 0)
        def _():
            far[...] = term

        @pl.when(i > 0)
        def _():
            far[...] += term

    begin, run = windowed(CHUNKS, CHUNKS, fetch, work)
    begin()
    run()


def far_field(recv, packed, earlier):
    sources, rows, _ = packed.shape
    return call(
        far_kernel,
        (recv, packed, earlier),
        (VMEM, HBM, AFTER_VMEM),
        [((rows, recv.shape[2]), F32, VMEM)],
        [pltpu.VMEM(packed.shape, BF16), semaphores(CHUNKS)],
        "far_field",
        2 * packed.size * recv.shape[2],
        2 * packed.size,
    )[0]


def halo_kernel(count_ref, list_ref, index_ref, blocks_ref, before, after, near_ref, *refs):
    refs = list(refs)
    take = lambda count: [refs.pop(0) for _ in range(count)]
    held = (len(refs) - 8) // 2
    sources = take(held)
    take(1)
    near, *targets = take(1 + held)
    blocks, halo, came, fetched, near_came, loaded = take(6)
    leaves = near.shape[0]
    reach = before.shape[0]
    entries = blocks_ref.shape[1]
    sides = [
        pltpu.make_async_copy(before, halo.at[pl.ds(0, reach)], came.at[0]),
        pltpu.make_async_copy(after, halo.at[pl.ds(reach, reach)], came.at[1]),
    ]
    get = [
        pltpu.make_async_copy(near_ref.at[leaf], near.at[leaf], near_came.at[leaf])
        for leaf in range(leaves)
    ]
    load = [
        pltpu.make_async_copy(source, target, loaded.at[i])
        for i, (source, target) in enumerate(zip(sources, targets))
    ]

    def block(i):
        entry = list_ref[i]
        return pltpu.make_async_copy(
            blocks_ref.at[entry // entries, entry % entries], blocks.at[i], fetched.at[i]
        )

    def ask(i, carry):
        block(i).start()
        return carry

    count = count_ref[0]
    at_once = 4

    def add(group, carry):
        terms = []
        for j in range(at_once):
            i = group * at_once + j

            @pl.when(i < count)
            def _():
                block(i).wait()

        for j in range(at_once):
            i = jnp.minimum(group * at_once + j, count - 1)
            weight = (group * at_once + j < count).astype(F32).astype(BF16)
            entry = list_ref[i]
            leaf = entry // entries
            place = index_ref[leaf, entry % entries]
            values = halo[jnp.where(place < reach, place, place - leaves)] * weight
            terms.append((leaf, dot(blocks[i], values)))
        for leaf, term in terms:
            near[leaf] += term
        return carry

    for side in sides:
        side.start()
    lax.fori_loop(0, count, ask, 0)
    for copy in get + load:
        copy.start()
    for copy in sides + get:
        copy.wait()
    lax.fori_loop(0, (count + at_once - 1) // at_once, add, 0)
    for copy in load:
        copy.wait()


def halo_part(listed, near_index, near_blocks, before, after, near, held, earlier):
    leaves, entries, size, _ = near_blocks.shape
    halo = (2 * before.shape[0],) + before.shape[1:]
    return call(
        halo_kernel,
        (*listed, near_index, near_blocks, before, after, near, *held, earlier),
        (SMEM, SMEM, SMEM, HBM, LOOSE, LOOSE) + (HBM,) * (1 + len(held)) + (AFTER_VMEM,),
        [(a.shape, a.dtype, VMEM) for a in (near, *held)],
        [
            pltpu.VMEM((leaves * entries, size, size), BF16),
            pltpu.VMEM(halo, BF16),
            semaphores(2),
            semaphores(leaves * entries),
            semaphores(leaves),
            semaphores(len(held)),
        ],
        "halo_part",
        1 << 28,
        6 << 20,
    )


def load_kernel(*refs):
    count = (len(refs) - 2) // 2
    copies = [
        pltpu.make_async_copy(refs[i], refs[count + 1 + i], refs[-1].at[i]) for i in range(count)
    ]
    for copy in copies:
        copy.start()
    for copy in copies:
        copy.wait()


def load(arrays, earlier):
    return call(
        load_kernel,
        (*arrays, earlier),
        (HBM,) * len(arrays) + (AFTER_VMEM,),
        [(a.shape, a.dtype, VMEM) for a in arrays],
        [semaphores(len(arrays))],
        "load",
        0,
        5 << 20,
    )


def stage_kernel(*refs, k, points):
    refs = list(refs)
    take = lambda count: [refs.pop(0) for _ in range(count)]
    m = k - 1
    first, sends = k == 0, k < STEPS
    send_slot, branch = take(2)
    if first:
        z_any, basis_any, transfer_any = take(3)
    else:
        column, other, state, far, near, basis, turned, transfer, lifting, top = take(10)
        zs = take(k)
        (z_any,) = take(1)
    state_out, send = take(2)
    if sends:
        coarse_any, low_any, high_any = take(3)
    sums, split, arrived, left = take(4)
    if sends:
        coarse, skeletons, out = take(3)
    if first:
        basis, transfer, vectors, came = take(4)
    else:
        ups, result, coef, combined = take(4)

    leaves, rank, size = basis.shape
    group = leaves // CHUNKS

    def fetch(i):
        if not first:
            return []
        some = slab(i, group)
        return [pltpu.make_async_copy(z_any.at[some], vectors.at[some], arrived.at[i])]

    def stores(i):
        some = slab(i, group)
        pairs = []
        if not first:
            pairs.append((result.at[some], z_any.at[some]))
        if sends:
            pairs.append((coarse.at[some], coarse_any.at[some]))
        return [
            pltpu.make_async_copy(source, target, left.at[n, i])
            for n, (source, target) in enumerate(pairs)
        ]

    def work(i):
        for j in range(group):
            leaf = i * group + j
            if first:
                others = []
                z = vectors[leaf]
            else:
                others = [ref[leaf] for ref in zs]
                z = near[leaf] + dot(turned[leaf], combined[slab(leaf, rank)])
                for l in range(m):
                    z = z - coef[l : l + 1, :] * others[l + 1]
                z = z * coef[STEPS : STEPS + 1, :]
                result[leaf] = z
            if sends:
                rounded = z.astype(BF16)
                coarse[leaf] = rounded
                skeletons[slab(leaf, rank)] = dot(basis[leaf], rounded).astype(BF16)
            for l, vector in enumerate(others + [z]):
                sums[l] += jnp.sum((z * vector).reshape(size // 8, 8, z.shape[1]), axis=0)
        for copy in stores(i):
            copy.start()

    begin, run = windowed(CHUNKS, CHUNKS, fetch, work)
    if first:
        small = [
            pltpu.make_async_copy(basis_any, basis, came.at[0]),
            pltpu.make_async_copy(transfer_any, transfer, came.at[1]),
        ]
        for copy in small:
            copy.start()
    begin()
    sums[...] = jnp.zeros(sums.shape, F32)
    if first:
        state_out[...] = jnp.zeros(state_out.shape, F32)
        for copy in small:
            copy.wait()
    else:
        in_order(branch, column, other, ups)
        count, columns = ups.shape[0], ups.shape[2]
        incoming = dot(top[...], ups[:, :rank].reshape(count * rank, columns)).astype(BF16)
        down = dot(transfer[...].reshape(leaves * rank, rank), incoming)
        combined[...] = (far[...] + down).astype(BF16)
        grams = [row / points for row in from_branches(ups, rank)]
        state_out[...] = state[...]
        weights, inverse = coefficients(m, grams, state, state_out)
        for i, weight in enumerate(weights):
            coef[i : i + 1, :] = weight
        coef[STEPS : STEPS + 1, :] = inverse
    run()

    if sends:
        halos = [
            pltpu.make_async_copy(coarse.at[pl.ds(0, HW)], low_any, out.at[0]),
            pltpu.make_async_copy(coarse.at[pl.ds(leaves - HW, HW)], high_any, out.at[1]),
        ]
        for copy in halos:
            copy.start()
        if first:
            lifted = dot_first(transfer[...].reshape(leaves * rank, rank), skeletons[...])
        else:
            lifted = dot(lifting[...], skeletons[...])
        lifted = lifted.astype(BF16)
    products = [jnp.sum(sums[i], axis=0, keepdims=True) for i in range(k + 1)]
    products = jnp.concatenate(products + [jnp.zeros_like(products[0])] * (7 - k), axis=0)
    store_split(split, products, k + 1)
    dots = split[...].astype(BF16)
    inner = send.shape[0]
    if sends:
        slots = send_slot.shape[0]
        for r in range(inner):
            for s in range(slots):
                send[r, s * rank : (s + 1) * rank] = skeletons[slab(send_slot[s, r], rank)]
            send[r, slots * rank : (slots + 1) * rank] = lifted
            send[r, (slots + 1) * rank :] = dots
    else:
        for r in range(inner):
            send[r] = dots
    for i in range(CHUNKS):
        for copy in stores(i):
            copy.wait()
    if sends:
        for copy in halos:
            copy.wait()


def stage(k, points, send_slot, branch, rhs, basis, transfer, later):
    leaves, rank, size = basis.shape
    first, sends = k == 0, k < STEPS
    tall = rhs.shape
    columns = tall[2]
    slots, inner = send_slot.shape
    names, outs = [], []

    def get(name, shape, dtype, spec):
        names.append(name)
        outs.append((shape, dtype, spec))

    args, specs = [send_slot, branch], [SMEM, SMEM]
    if first:
        args += [rhs, basis, transfer]
        specs += [HBM] * 3
    else:
        args += later
        specs += [VMEM] * len(later)
        get("z", tall, F32, HBM)
    get("state", (STATE_ROWS, columns), F32, VMEM)
    rows = ((slots + 1) * rank if sends else 0) + DOT_ROWS
    get("send", (inner, rows, columns), BF16, VMEM)
    if sends:
        get("coarse", tall, BF16, HBM)
        get("low", (HW, size, columns), BF16, LOOSE)
        get("high", (HW, size, columns), BF16, LOOSE)

    scratch = [
        pltpu.VMEM((STEPS + 1, 8, columns), F32),
        pltpu.VMEM((DOT_ROWS, columns), F32),
        semaphores(CHUNKS),
        semaphores(2, CHUNKS),
    ]
    if sends:
        scratch += [
            pltpu.VMEM(tall, BF16),
            pltpu.VMEM((leaves * rank, columns), BF16),
            semaphores(2),
        ]
    if first:
        scratch += [
            pltpu.VMEM(basis.shape, BF16),
            pltpu.VMEM(transfer.shape, BF16),
            pltpu.VMEM(tall, F32),
            semaphores(2),
        ]
    else:
        column = later[0].shape
        scratch += [
            pltpu.VMEM((2 * column[0],) + column[1:], BF16),
            pltpu.VMEM(tall, F32),
            pltpu.VMEM((8, columns), F32),
            pltpu.VMEM((leaves * rank, columns), BF16),
        ]
    results = call(
        functools.partial(stage_kernel, k=k, points=points),
        args,
        specs,
        outs,
        scratch,
        f"stage{k}",
        1 << 27,
        (k + 4) << 20,
    )
    return dict(zip(names, results))


def vectors_kernel(*refs, known, points):
    refs = list(refs)
    take = lambda count: [refs.pop(0) for _ in range(count)]
    (state,) = take(1)
    if not known:
        branch, column, other = take(3)
    zs = take(known if known else STEPS + 1)
    if known:
        (krylov,) = take(1)
    else:
        _, krylov, hess_out = take(3)
    if known:
        vectors, result, arrived, left = take(4)
        after = state
    else:
        result, left, after, ups = take(4)
        vectors = zs
    parts = left.shape[1]
    group = zs[0].shape[0] // parts
    size = zs[0].shape[1]
    wanted = range(known) if known else [STEPS]

    def fetch(i):
        some = slab(i, group)
        return [
            pltpu.make_async_copy(z.at[some], vectors.at[l, some], arrived.at[l, i])
            for l, z in enumerate(zs if known else [])
        ]

    def store(n, i):
        some = slab(i, group)
        return pltpu.make_async_copy(result.at[n, some], krylov.at[wanted[n], some], left.at[n, i])

    def work(i):
        for j in range(group):
            leaf = i * group + j
            for n, which in enumerate(wanted):
                vector = None
                for l in range(which + 1):
                    row = basis_row(which, l)
                    values = vectors[l, leaf] if known else vectors[l][leaf]
                    term = after[row : row + 1, :] * values
                    vector = term if vector is None else vector + term
                result[n, leaf] = vector
        for n in range(len(wanted)):
            store(n, i).start()

    begin, run = windowed(parts, parts, fetch, work)
    begin()
    if not known:
        in_order(branch, column, other, ups)
        grams = [row / points for row in from_branches(ups, 0)]
        after[...] = state[...]
        coefficients(STEPS, grams, state, after)
    run()
    if not known:
        for i in range(STEPS + 1):
            for j in range(STEPS):
                row = i * STEPS + j
                if i <= j + 1:
                    hess_out[i, j : j + 1, :] = after[row : row + 1, :]
                else:
                    hess_out[i, j : j + 1, :] = jnp.zeros((1, hess_out.shape[2]), F32)
    for n in range(len(wanted)):
        for i in range(parts):
            store(n, i).wait()


def basis_vectors(state, zs, parts):
    known = len(zs)
    tall = zs[0].shape
    return call(
        functools.partial(vectors_kernel, known=known, points=0),
        [state] + zs,
        [VMEM] + [HBM] * known,
        [((STEPS + 1,) + tall, F32, HBM)],
        [
            pltpu.VMEM((known,) + tall, F32),
            pltpu.VMEM((known,) + tall, F32),
            semaphores(known, parts),
            semaphores(known, parts),
        ],
        "basis_vectors",
        1 << 23,
        8 << 20,
    )[0]


def last(points, branch, column, other, state, krylov, zs, parts):
    tall = zs[0].shape
    return call(
        functools.partial(vectors_kernel, known=0, points=points),
        [state, branch, column, other] + list(zs) + [krylov],
        [VMEM, SMEM, VMEM, VMEM] + [VMEM] * len(zs) + [HBM],
        [(krylov.shape, F32, HBM), ((STEPS + 1, STEPS, tall[2]), F32, FREE)],
        [
            pltpu.VMEM((1,) + tall, F32),
            semaphores(1, parts),
            pltpu.VMEM(state.shape, F32),
            pltpu.VMEM((2 * column.shape[0],) + column.shape[1:], BF16),
        ],
        "last_vector",
        1 << 22,
        6 << 20,
        {4 + len(zs): 0},
    )


def shards(
    rhs,
    near_blocks,
    near_index,
    near_mask,
    basis,
    far_blocks,
    far_slot,
    far_mask,
    send_slot,
    transfer,
    top_blocks,
):
    outer, inner = lax.axis_size("outer"), lax.axis_size("inner")
    points = outer * inner * rhs.shape[0]
    leaves, rank = basis.shape[:2]
    slots = send_slot.shape[2]
    branch = lax.axis_index("outer").astype(jnp.int32).reshape(1)
    up_pairs = [(i, i + 1) for i in range(inner - 1)]
    down_pairs = [(j, i) for i, j in up_pairs]
    wanted = send_slot[0].T

    def exchange(array, axis):
        return lax.all_to_all(array, axis, split_axis=0, concat_axis=0, tiled=True)

    zs = [rhs.reshape(leaves, -1, rhs.shape[1])]
    out = stage(0, points, wanted, branch, zs[0], basis, transfer, None)
    packed, count, entries, turned, lifting, top = pack(
        branch, basis, transfer, top_blocks, far_blocks, far_mask, far_slot, near_index, near_mask,
        inner, slots,
    )
    listed = (count, entries)
    state = out["state"]
    for k in range(1, STEPS + 1):
        recv = exchange(out["send"], "inner")
        before = lax.ppermute(out["high"], "inner", up_pairs)
        after = lax.ppermute(out["low"], "inner", down_pairs)
        earlier = (packed,) if k == 1 else ()
        near = near_field(near_index, near_mask, near_blocks, out["coarse"], *earlier)
        summed = gather_sum(recv, slots * rank, near)
        local_far = far_field(recv, packed, summed)

        def between(column):
            held = (basis, turned, transfer, lifting, top, *zs)
            return halo_part(
                listed, near_index, near_blocks, before, after, near, held, column
            )

        column, other, (near, *held) = over_branches(summed, outer, local_far, between)
        later = [column, other, state, local_far, near, *held]
        out = stage(k, points, wanted, branch, zs[0], basis, transfer, later)
        state = out["state"]
        zs = zs + [out["z"]]
    krylov = basis_vectors(state, zs[:STEPS], CHUNKS)
    recv = exchange(out["send"], "inner")
    summed = gather_sum(recv, 0, krylov)
    loaded = load(zs, summed)
    column, other, loaded = over_branches(summed, outer, loaded[0], lambda column: loaded)
    krylov, hessenberg = last(points, branch, column, other, state, krylov, loaded, CHUNKS)
    return krylov.reshape(STEPS + 1, *rhs.shape), hessenberg


def solution(mesh):
    return jax.shard_map(
        shards,
        mesh=mesh,
        in_specs=(
            P(("outer", "inner"), None),
            P(("outer", "inner"), None, None, None),
            P(("outer", "inner"), None),
            P(("outer", "inner"), None),
            P(("outer", "inner"), None, None),
            P(("outer", "inner"), None, None, None),
            P(("outer", "inner"), None),
            P(("outer", "inner"), None),
            P(("outer", "inner"), None, None),
            P(("outer", "inner"), None, None),
            P("outer", None, None, None),
        ),
        out_specs=(P(None, ("outer", "inner"), None), P()),
        check_vma=False,
    )
```

```python
import functools

import jax
import jax.numpy as jnp
from jax import lax
from jax.experimental import pallas as pl
from jax.experimental.pallas import tpu as pltpu
from jax.sharding import PartitionSpec as P

HW = 2
STEPS = 4
EPS = 1e-06
PIECES = 3
DOT_ROWS = 16
STATE_ROWS = 64
VMEM_BYTES = 32 * 1024 * 1024
BF16 = jnp.bfloat16
F32 = jnp.float32


def dot(a, b):
    return jnp.dot(a, b, preferred_element_type=F32)


def dot_first(a, b):
    return lax.dot_general(a, b, (((0,), (0,)), ((), ())), preferred_element_type=F32)


def store_split(ref, values, count):
    rest = values
    ref[...] = jnp.zeros(ref.shape, F32)
    for piece in range(PIECES):
        part = rest.astype(BF16).astype(F32)
        ref[piece * 5 : piece * 5 + count, :] = part[:count]
        rest = rest - part


def joined(rows):
    return [rows[i : i + 1] + rows[5 + i : 6 + i] + rows[10 + i : 11 + i] for i in range(5)]


def entry_row(i, l):
    low, high = min(i, l), max(i, l)
    return 20 + high * (high + 1) // 2 + low


def basis_row(i, l):
    return 32 + i * (i + 1) // 2 + l


def coefficients(m, grams, state_in, state_out):
    last = m - 1
    entry = lambda i, l: state_in[entry_row(i, l) : entry_row(i, l) + 1, :]
    expand = lambda i, l: state_in[basis_row(i, l) : basis_row(i, l) + 1, :]

    def put(row, value):
        state_out[row : row + 1, :] = value

    dots = []
    for i in range(m):
        dots.append(sum(expand(i, l) * grams[l] for l in range(i + 1)))
    weights = [dots[i] + entry(i, last) for i in range(m)]
    spread = [sum(weights[l] * entry(i, l) for l in range(m)) for i in range(m)]
    square = grams[m]
    for i in range(m):
        square = square + weights[i] * (weights[i] + spread[i] - 2.0 * dots[i])
    total = jnp.maximum(square, 0.0) + EPS
    root = jnp.sqrt(total)
    inverse = 1.0 / root
    for l in range(m):
        value = sum(weights[i] * expand(i, l) for i in range(l, m))
        put(basis_row(m, l), -inverse * value)
    put(basis_row(m, m), inverse)
    for i in range(m):
        put(i * STEPS + last, weights[i] + (1.0 if i == last else 0.0))
    if m > 0:
        put(m * STEPS + last, root)
    if m < STEPS:
        for i in range(m):
            put(entry_row(i, m), (-entry(i, last) - spread[i]) * inverse)
        put(entry_row(m, m), -EPS / total)
    return weights, inverse


def from_branches(ups_ref, rank):
    rows = ups_ref[0, rank:].astype(F32)
    for c in range(1, ups_ref.shape[0]):
        rows = rows + ups_ref[c, rank:].astype(F32)
    return joined(rows)


SMEM = pl.BlockSpec(memory_space=pltpu.SMEM)
VMEM = pl.BlockSpec(memory_space=pltpu.VMEM)
HBM = pl.BlockSpec(memory_space=pl.ANY)
AFTER = pl.BlockSpec(memory_space=pl.ANY)
AFTER_VMEM = pl.BlockSpec(memory_space=pl.ANY)
LOOSE = pl.BlockSpec(memory_space=pl.ANY)
FREE = pl.BlockSpec(memory_space=pltpu.VMEM)
AHEAD = 3
CHUNKS = 4
PIN = True


def call(kernel, args, in_specs, outs, scratch, name, flops, moved, aliases={}):
    def pinned(array, spec):
        if not PIN or not any(spec is one for one in (VMEM, HBM, AFTER, AFTER_VMEM)):
            return array
        in_vmem = spec is VMEM or spec is AFTER_VMEM
        return pltpu.with_memory_space_constraint(array, pltpu.VMEM if in_vmem else pltpu.HBM)

    def shape_of(shape, dtype, spec):
        if not PIN or not (spec is VMEM or spec is HBM):
            return jax.ShapeDtypeStruct(shape, dtype)
        return (pltpu.VMEM if spec is VMEM else pltpu.HBM)(shape, dtype)

    return pl.pallas_call(
        kernel,
        in_specs=list(in_specs),
        out_specs=[spec for _, _, spec in outs],
        out_shape=[shape_of(*out) for out in outs],
        scratch_shapes=scratch,
        input_output_aliases=aliases,
        compiler_params=pltpu.CompilerParams(vmem_limit_bytes=VMEM_BYTES),
        cost_estimate=pl.CostEstimate(flops=flops, bytes_accessed=moved, transcendentals=0),
        name=name,
    )(*[pinned(array, spec) for array, spec in zip(args, in_specs)])


def semaphores(*shape):
    return pltpu.SemaphoreType.DMA(shape)


def windowed(count, ahead, fetch, work):
    def start(i):
        for j, copy in enumerate(fetch(i)):
            copy.start(priority=j % 2)

    def body(i, carry):
        @pl.when(i + ahead < count)
        def _():
            start(i + ahead)

        for copy in fetch(i):
            copy.wait()
        work(i)
        return carry

    def begin():
        for i in range(min(ahead, count)):
            start(i)

    return begin, lambda: lax.fori_loop(0, count, body, 0)


def slab(i, size):
    return pl.ds(pl.multiple_of(i * size, size), size)


def pack_kernel(branch, mask_ref, slot_ref, index_ref, near_mask_ref, far_ref, *refs):
    basis_ref, transfer_ref, top_ref = refs[:3]
    out_ref, count_ref, list_ref, basis_out, transfer_out, top_out = refs[3:9]
    blocks, total, packed, basis, transfer, top, turned, lifting, row, arrived, left, came = refs[9:]
    leaves, entries, rank, _ = blocks.shape
    sources, _, width = packed.shape
    slots = width // rank
    near_entries = index_ref.shape[1]

    def fetch(leaf):
        return [pltpu.make_async_copy(far_ref.at[leaf], blocks.at[leaf], arrived.at[leaf])]

    def store(leaf):
        rows = slab(leaf, rank)
        return pltpu.make_async_copy(packed.at[:, rows], out_ref.at[:, rows], left.at[leaf])

    def work(leaf):
        total[...] = jnp.zeros(total.shape, F32)
        for f in range(entries):
            weight = mask_ref[leaf, f].astype(F32)
            total[slot_ref[leaf, f]] += blocks[leaf, f].astype(F32) * weight
        rows = slab(leaf, rank)
        for source in range(sources):
            sides = [total[source * slots + s] for s in range(slots)]
            packed[source, rows] = jnp.concatenate(sides, axis=1).astype(BF16)
        store(leaf).start()

    def list_one(i, count):
        leaf, n = i // near_entries, i % near_entries
        place = index_ref[leaf, n]
        hit = (near_mask_ref[leaf, n] != 0) & ((place < HW) | (place >= HW + leaves))
        list_ref[i] = 0

        @pl.when(hit)
        def _():
            list_ref[count] = i

        return count + hit.astype(jnp.int32)

    small = [
        pltpu.make_async_copy(basis_ref, basis, came.at[0]),
        pltpu.make_async_copy(transfer_ref, transfer, came.at[1]),
        pltpu.make_async_copy(top_ref, top, came.at[2]),
    ]
    for copy in small:
        copy.start()
    begin, run = windowed(leaves, AHEAD, fetch, work)
    begin()
    count_ref[0] = lax.fori_loop(0, list_ref.shape[0], list_one, 0)
    for copy in small:
        copy.wait()
    turn = lambda a: a.astype(F32).T.astype(BF16)
    for leaf in range(leaves):
        turned[leaf] = turn(basis[leaf])
    for pair in range(leaves // 2):
        columns = slice(pair * 2 * rank, (pair + 1) * 2 * rank)
        sides = [turn(transfer[2 * pair + j]) for j in range(2)]
        lifting[:, columns] = jnp.concatenate(sides, axis=1)
    for pair in range(top.shape[1] // 2):
        columns = slice(pair * 2 * rank, (pair + 1) * 2 * rank)
        sides = []
        for c in (2 * pair, 2 * pair + 1):
            sides.append(top[0, c] * (branch[0] != c).astype(F32).astype(BF16))
        row[:, columns] = jnp.concatenate(sides, axis=1)
    results = [
        pltpu.make_async_copy(turned, basis_out, came.at[0]),
        pltpu.make_async_copy(lifting, transfer_out, came.at[1]),
        pltpu.make_async_copy(row, top_out, came.at[2]),
    ]
    for copy in results:
        copy.start()
    run()
    for leaf in range(leaves):
        store(leaf).wait()
    for copy in results:
        copy.wait()


def pack(branch, basis, transfer, top_blocks, far_blocks, far_mask, far_slot, near_index, near_mask, inner, slots):
    leaves, entries, rank, _ = far_blocks.shape
    shape = (inner, leaves * rank, slots * rank)
    turned = (leaves, basis.shape[2], rank)
    lifting = (rank, leaves * rank)
    row = (rank, top_blocks.shape[1] * rank)
    return call(
        pack_kernel,
        (branch, far_mask, far_slot, near_index, near_mask, far_blocks, basis, transfer, top_blocks),
        (SMEM,) * 5 + (HBM,) * 4,
        [
            (shape, BF16, HBM),
            ((1,), jnp.int32, SMEM),
            ((near_index.size,), jnp.int32, SMEM),
            (turned, BF16, HBM),
            (lifting, BF16, HBM),
            (row, BF16, HBM),
        ],
        [
            pltpu.VMEM(far_blocks.shape, BF16),
            pltpu.VMEM((inner * slots, rank, rank), F32),
            pltpu.VMEM(shape, BF16),
            pltpu.VMEM(basis.shape, BF16),
            pltpu.VMEM(transfer.shape, BF16),
            pltpu.VMEM(top_blocks.shape, BF16),
            pltpu.VMEM(turned, BF16),
            pltpu.VMEM(lifting, BF16),
            pltpu.VMEM(row, BF16),
            semaphores(leaves),
            semaphores(leaves),
            semaphores(3),
        ],
        "pack",
        0,
        10 << 20,
    )


def near_kernel(index_ref, mask_ref, blocks_ref, own_ref, *refs):
    out_ref, blocks, own, result, arrived, came, left = refs[-7:]
    leaves, entries, size, _ = blocks.shape

    def fetch(leaf):
        halves = [pl.ds(j * (entries // 2), entries // 2) for j in range(2)]
        return [
            pltpu.make_async_copy(
                blocks_ref.at[leaf, half], blocks.at[leaf, half], arrived.at[leaf, j]
            )
            for j, half in enumerate(halves)
        ]

    def store(leaf):
        return pltpu.make_async_copy(
            result.at[leaf], out_ref.at[leaf], left.at[leaf]
        )

    def work(leaf):
        total = None
        for n in range(entries):
            place = index_ref[leaf, n] - HW
            inside = (place >= 0) & (place < leaves)
            weight = jnp.where(inside, mask_ref[leaf, n], 0).astype(F32).astype(BF16)
            values = own[jnp.clip(place, 0, leaves - 1)] * weight
            term = dot(blocks[leaf, n], values)
            total = term if total is None else total + term
        result[leaf] = total
        store(leaf).start()

    begin, run = windowed(leaves, AHEAD, fetch, work)
    copy = pltpu.make_async_copy(own_ref, own, came)
    copy.start()
    begin()
    copy.wait()
    run()
    for leaf in range(leaves):
        store(leaf).wait()


def near_field(near_index, near_mask, near_blocks, own, *earlier):
    leaves, _, size, _ = near_blocks.shape
    columns = own.shape[2]
    return call(
        near_kernel,
        (near_index, near_mask, near_blocks, own) + earlier,
        (SMEM, SMEM, HBM, HBM) + (AFTER,) * len(earlier),
        [((leaves, size, columns), F32, HBM)],
        [
            pltpu.VMEM(near_blocks.shape, BF16),
            pltpu.VMEM(own.shape, BF16),
            pltpu.VMEM((leaves, size, columns), F32),
            semaphores(leaves, 2),
            semaphores(),
            semaphores(leaves),
        ],
        "near_field",
        2 * near_blocks.size * columns,
        2 * near_blocks.size,
    )[0]


def gather_sum_kernel(recv, *refs, lead):
    out_ref, split = refs[-2:]
    rank = out_ref.shape[0] - DOT_ROWS
    total = recv[0, lead:].astype(F32)
    for i in range(1, recv.shape[0]):
        total = total + recv[i, lead:].astype(F32)
    store_split(split, jnp.concatenate(joined(total[rank:]), axis=0), 5)
    if rank > 0:
        out_ref[:rank] = total[:rank].astype(BF16)
    out_ref[rank:] = split[...].astype(BF16)


def gather_sum(recv, lead, earlier):
    _, rows, columns = recv.shape
    return call(
        functools.partial(gather_sum_kernel, lead=lead),
        (recv, earlier),
        (VMEM, AFTER),
        [((rows - lead, columns), BF16, VMEM)],
        [pltpu.VMEM((DOT_ROWS, columns), F32)],
        "gather_sum",
        1 << 20,
        1 << 19,
    )[0]


def stack_kernel(*refs):
    for i, ref in enumerate(refs[:-2]):
        refs[-1][i] = ref[...]


def over_branches(summed, outer, earlier, between):
    shifts = [[(o, (o + 2 * j) % outer) for o in range(outer)] for j in range(1, outer // 2)]
    parts = [summed] + [lax.ppermute(summed, "outer", shift) for shift in shifts]
    column = call(
        stack_kernel,
        parts + [earlier],
        [VMEM] * len(parts) + [AFTER_VMEM],
        [((len(parts),) + summed.shape, BF16, VMEM)],
        [],
        "stack",
        0,
        1 << 18,
    )[0]
    other = lax.ppermute(column, "outer", [(o, o ^ 1) for o in range(outer)])
    return column, other, between(column)


def in_order(branch, column, other, ups):
    count = ups.shape[0]
    for j in range(count // 2):
        ups[lax.rem(branch[0] + count - 2 * j, count)] = column[j]
        mate = branch[0] + 1 - 2 * lax.rem(branch[0], 2)
        ups[lax.rem(mate + count - 2 * j, count)] = other[j]


def far_kernel(count_ref, list_ref, recv, packed_ref, blocks_ref, *refs):
    held = (len(refs) - 7) // 2
    sources, (_, far, blocks), targets = refs[:held], refs[held : held + 3], refs[held + 3 : -4]
    packed, arrived, fetched, loaded = refs[-4:]
    share = packed.shape[0] // CHUNKS
    width = packed.shape[2]
    entries = blocks_ref.shape[1]
    count = count_ref[0]

    def fetch(i):
        some = slab(i, share)
        return [pltpu.make_async_copy(packed_ref.at[some], packed.at[some], arrived.at[i])]

    def block(i):
        entry = list_ref[i]
        return pltpu.make_async_copy(
            blocks_ref.at[entry // entries, entry % entries], blocks.at[i], fetched.at[i]
        )

    def ask(i, carry):
        block(i).start()
        return carry

    def have(i, carry):
        block(i).wait()
        return carry

    def work(i):
        term = None
        for j in range(share):
            source = i * share + j
            one = dot(packed[source], recv[source, :width])
            term = one if term is None else term + one

        @pl.when(i == 0)
        def _():
            far[...] = term

        @pl.when(i > 0)
        def _():
            far[...] += term

    loads = [
        pltpu.make_async_copy(source, target, loaded.at[i])
        for i, (source, target) in enumerate(zip(sources, targets))
    ]
    begin, run = windowed(CHUNKS, CHUNKS, fetch, work)
    begin()
    lax.fori_loop(0, count, ask, 0)
    for copy in loads:
        copy.start()
    run()
    lax.fori_loop(0, count, have, 0)
    for copy in loads:
        copy.wait()


def far_field(listed, recv, packed, near_blocks, held, earlier):
    sources, rows, _ = packed.shape
    leaves, entries, size, _ = near_blocks.shape
    outs = [((rows, recv.shape[2]), F32, VMEM), ((leaves * entries, size, size), BF16, VMEM)]
    far, blocks, *held = call(
        far_kernel,
        (*listed, recv, packed, near_blocks, *held, earlier),
        (SMEM, SMEM, VMEM, HBM, HBM) + (HBM,) * len(held) + (AFTER_VMEM,),
        outs + [(a.shape, a.dtype, VMEM) for a in held],
        [
            pltpu.VMEM(packed.shape, BF16),
            semaphores(CHUNKS),
            semaphores(leaves * entries),
            semaphores(len(held)),
        ],
        "far_field",
        2 * packed.size * recv.shape[2],
        2 * packed.size,
    )
    return far, blocks, held


def halo_kernel(count_ref, list_ref, index_ref, blocks, before, after, near_in, _, near, halo):
    leaves, reach, entries = near.shape[0], before.shape[0], index_ref.shape[1]
    halo[:reach] = before[...]
    halo[reach:] = after[...]
    count = count_ref[0]
    at_once = 8

    def add(group, carry):
        terms = []
        for j in range(at_once):
            i = jnp.minimum(group * at_once + j, count - 1)
            weight = (group * at_once + j < count).astype(F32).astype(BF16)
            entry = list_ref[i]
            leaf = entry // entries
            place = index_ref[leaf, entry % entries]
            values = halo[jnp.where(place < reach, place, place - leaves)] * weight
            terms.append((leaf, dot(blocks[i], values)))
        for leaf, term in terms:
            near[leaf] += term
        return carry

    lax.fori_loop(0, (count + at_once - 1) // at_once, add, 0)


def halo_part(listed, near_index, blocks, before, after, near, earlier):
    return call(
        halo_kernel,
        (*listed, near_index, blocks, before, after, near, earlier),
        (SMEM, SMEM, SMEM, VMEM, VMEM, VMEM, VMEM, AFTER_VMEM),
        [(near.shape, F32, VMEM)],
        [pltpu.VMEM((2 * before.shape[0],) + before.shape[1:], BF16)],
        "halo_part",
        1 << 28,
        2 << 20,
        {6: 0},
    )[0]


def sum_kernel(place, *refs):
    *parts, _, out, rows, split = refs
    count = len(parts)
    for j, part in enumerate(parts):
        rows[lax.rem(place[0] + count - j, count)] = part[...].astype(F32)
    total = rows[0]
    for i in range(1, count):
        total = total + rows[i]
    store_split(split, jnp.concatenate(joined(total), axis=0), 5)
    out[...] = split[...].astype(BF16)


def sum_over(dots, axis, stride, count, earlier, after):
    if count == 1:
        return dots
    place = lax.rem(lax.axis_index(axis).astype(jnp.int32) // stride, count).reshape(1)
    size = lax.axis_size(axis)

    def moved(i, j):
        at = i // stride % count
        return i + ((at + j) % count - at) * stride

    parts = [dots]
    for j in range(1, count):
        parts.append(lax.ppermute(dots, axis, [(i, moved(i, j)) for i in range(size)]))
    return call(
        sum_kernel,
        (place, *parts, earlier),
        (SMEM,) + (VMEM,) * count + (after,),
        [(dots.shape, BF16, VMEM)],
        [pltpu.VMEM((count,) + dots.shape, F32), pltpu.VMEM((DOT_ROWS, dots.shape[1]), F32)],
        "sum_over",
        0,
        1 << 18,
    )[0]


def load_kernel(*refs):
    count = (len(refs) - 2) // 2
    copies = [
        pltpu.make_async_copy(refs[i], refs[count + 1 + i], refs[-1].at[i]) for i in range(count)
    ]
    for copy in copies:
        copy.start()
    for copy in copies:
        copy.wait()


def load(arrays, earlier):
    return call(
        load_kernel,
        (*arrays, earlier),
        (HBM,) * len(arrays) + (AFTER_VMEM,),
        [(a.shape, a.dtype, VMEM) for a in arrays],
        [semaphores(len(arrays))],
        "load",
        0,
        5 << 20,
    )


def stage_kernel(*refs, k, points):
    refs = list(refs)
    take = lambda count: [refs.pop(0) for _ in range(count)]
    m = k - 1
    first, sends = k == 0, k < STEPS
    send_slot, branch = take(2)
    if first:
        z_any, basis_any, transfer_any = take(3)
    else:
        column, other, state, far, near, basis, turned, transfer, lifting, top = take(10)
        zs = take(k)
        (z_any,) = take(1)
    state_out, send = take(2)
    if sends:
        coarse_any, low_any, high_any = take(3)
    sums, split, arrived, left = take(4)
    if sends:
        coarse, skeletons, out = take(3)
    if first:
        basis, transfer, vectors, came = take(4)
    else:
        ups, result, coef, combined = take(4)

    leaves, rank, size = basis.shape
    group = leaves // CHUNKS

    def fetch(i):
        if not first:
            return []
        some = slab(i, group)
        return [pltpu.make_async_copy(z_any.at[some], vectors.at[some], arrived.at[i])]

    def stores(i):
        some = slab(i, group)
        pairs = []
        if not first:
            pairs.append((result.at[some], z_any.at[some]))
        if sends:
            pairs.append((coarse.at[some], coarse_any.at[some]))
        return [
            pltpu.make_async_copy(source, target, left.at[n, i])
            for n, (source, target) in enumerate(pairs)
        ]

    def work(i):
        for j in range(group):
            leaf = i * group + j
            if first:
                others = []
                z = vectors[leaf]
            else:
                others = [ref[leaf] for ref in zs]
                z = near[leaf] + dot(turned[leaf], combined[slab(leaf, rank)])
                for l in range(m):
                    z = z - coef[l : l + 1, :] * others[l + 1]
                z = z * coef[STEPS : STEPS + 1, :]
                result[leaf] = z
            if sends:
                rounded = z.astype(BF16)
                coarse[leaf] = rounded
                skeletons[slab(leaf, rank)] = dot(basis[leaf], rounded).astype(BF16)
            for l, vector in enumerate(others + [z]):
                sums[l] += jnp.sum((z * vector).reshape(size // 8, 8, z.shape[1]), axis=0)
        for copy in stores(i):
            copy.start()

    begin, run = windowed(CHUNKS, CHUNKS, fetch, work)
    if first:
        small = [
            pltpu.make_async_copy(basis_any, basis, came.at[0]),
            pltpu.make_async_copy(transfer_any, transfer, came.at[1]),
        ]
        for copy in small:
            copy.start()
    begin()
    sums[...] = jnp.zeros(sums.shape, F32)
    if first:
        state_out[...] = jnp.zeros(state_out.shape, F32)
        for copy in small:
            copy.wait()
    else:
        in_order(branch, column, other, ups)
        count, columns = ups.shape[0], ups.shape[2]
        incoming = dot(top[...], ups[:, :rank].reshape(count * rank, columns)).astype(BF16)
        down = dot(transfer[...].reshape(leaves * rank, rank), incoming)
        combined[...] = (far[...] + down).astype(BF16)
        grams = [row / points for row in from_branches(ups, rank)]
        state_out[...] = state[...]
        weights, inverse = coefficients(m, grams, state, state_out)
        for i, weight in enumerate(weights):
            coef[i : i + 1, :] = weight
        coef[STEPS : STEPS + 1, :] = inverse
    run()

    if sends:
        halos = [
            pltpu.make_async_copy(coarse.at[pl.ds(0, HW)], low_any, out.at[0]),
            pltpu.make_async_copy(coarse.at[pl.ds(leaves - HW, HW)], high_any, out.at[1]),
        ]
        for copy in halos:
            copy.start()
        if first:
            lifted = dot_first(transfer[...].reshape(leaves * rank, rank), skeletons[...])
        else:
            lifted = dot(lifting[...], skeletons[...])
        lifted = lifted.astype(BF16)
    products = [jnp.sum(sums[i], axis=0, keepdims=True) for i in range(k + 1)]
    products = jnp.concatenate(products + [jnp.zeros_like(products[0])] * (7 - k), axis=0)
    store_split(split, products, k + 1)
    dots = split[...].astype(BF16)
    if sends:
        slots, inner = send_slot.shape
        for r in range(inner):
            for s in range(slots):
                send[r, s * rank : (s + 1) * rank] = skeletons[slab(send_slot[s, r], rank)]
            send[r, slots * rank : (slots + 1) * rank] = lifted
            send[r, (slots + 1) * rank :] = dots
    else:
        send[...] = dots
    for i in range(CHUNKS):
        for copy in stores(i):
            copy.wait()
    if sends:
        for copy in halos:
            copy.wait()


def stage(k, points, send_slot, branch, rhs, basis, transfer, later):
    leaves, rank, size = basis.shape
    first, sends = k == 0, k < STEPS
    tall = rhs.shape
    columns = tall[2]
    slots, inner = send_slot.shape
    names, outs = [], []

    def get(name, shape, dtype, spec):
        names.append(name)
        outs.append((shape, dtype, spec))

    args, specs = [send_slot, branch], [SMEM, SMEM]
    if first:
        args += [rhs, basis, transfer]
        specs += [HBM] * 3
    else:
        args += later
        specs += [VMEM] * len(later)
        get("z", tall, F32, HBM)
    get("state", (STATE_ROWS, columns), F32, VMEM)
    rows = (slots + 1) * rank + DOT_ROWS
    get("send", (inner, rows, columns) if sends else (DOT_ROWS, columns), BF16, VMEM)
    if sends:
        get("coarse", tall, BF16, HBM)
        get("low", (HW, size, columns), BF16, LOOSE)
        get("high", (HW, size, columns), BF16, LOOSE)

    scratch = [
        pltpu.VMEM((STEPS + 1, 8, columns), F32),
        pltpu.VMEM((DOT_ROWS, columns), F32),
        semaphores(CHUNKS),
        semaphores(2, CHUNKS),
    ]
    if sends:
        scratch += [
            pltpu.VMEM(tall, BF16),
            pltpu.VMEM((leaves * rank, columns), BF16),
            semaphores(2),
        ]
    if first:
        scratch += [
            pltpu.VMEM(basis.shape, BF16),
            pltpu.VMEM(transfer.shape, BF16),
            pltpu.VMEM(tall, F32),
            semaphores(2),
        ]
    else:
        column = later[0].shape
        scratch += [
            pltpu.VMEM((2 * column[0],) + column[1:], BF16),
            pltpu.VMEM(tall, F32),
            pltpu.VMEM((8, columns), F32),
            pltpu.VMEM((leaves * rank, columns), BF16),
        ]
    results = call(
        functools.partial(stage_kernel, k=k, points=points),
        args,
        specs,
        outs,
        scratch,
        f"stage{k}",
        1 << 27,
        (k + 4) << 20,
    )
    return dict(zip(names, results))


def vectors_kernel(*refs, wanted, held, final, points):
    refs = list(refs)
    take = lambda count: [refs.pop(0) for _ in range(count)]
    (state,) = take(1)
    if final:
        branch, column, other = take(3)
    zs = take(wanted[-1] + 1)
    _, krylov = take(2)
    if final:
        (hess_out,) = take(1)
    result, left = take(2)
    if final:
        after, ups = take(2)
    else:
        after = state
    if not held:
        vectors, arrived = take(2)
    parts = left.shape[1]
    group = zs[0].shape[0] // parts

    def fetch(i):
        if held:
            return []
        some = slab(i, group)
        return [
            pltpu.make_async_copy(z.at[some], vectors.at[l, some], arrived.at[l, i])
            for l, z in enumerate(zs)
        ]

    def store(n, i):
        some = slab(i, group)
        return pltpu.make_async_copy(result.at[n, some], krylov.at[wanted[n], some], left.at[n, i])

    def work(i):
        for j in range(group):
            leaf = i * group + j
            for n, which in enumerate(wanted):
                vector = None
                for l in range(which + 1):
                    row = basis_row(which, l)
                    values = zs[l][leaf] if held else vectors[l, leaf]
                    term = after[row : row + 1, :] * values
                    vector = term if vector is None else vector + term
                result[n, leaf] = vector
        for n in range(len(wanted)):
            store(n, i).start()

    begin, run = windowed(parts, parts, fetch, work)
    begin()
    if final:
        in_order(branch, column, other, ups)
        grams = [row / points for row in from_branches(ups, 0)]
        after[...] = state[...]
        coefficients(STEPS, grams, state, after)
    run()
    if final:
        for i in range(STEPS + 1):
            for j in range(STEPS):
                row = i * STEPS + j
                if i <= j + 1:
                    hess_out[i, j : j + 1, :] = after[row : row + 1, :]
                else:
                    hess_out[i, j : j + 1, :] = jnp.zeros((1, hess_out.shape[2]), F32)
    for n in range(len(wanted)):
        for i in range(parts):
            store(n, i).wait()


def vectors(state, zs, wanted, before, parts, products=None, points=0):
    final = products is not None
    held = wanted[0] > 0
    tall = zs[0].shape
    count = wanted[-1] + 1
    shape = (STEPS + 1,) + tall
    scratch = [pltpu.VMEM((len(wanted),) + tall, F32), semaphores(len(wanted), parts)]
    outs = [(shape, F32, HBM)]
    args, specs = [state], [VMEM]
    if final:
        args += products
        specs += [SMEM, VMEM, VMEM]
        column = products[1].shape
        outs.append(((STEPS + 1, STEPS, tall[2]), F32, FREE))
        scratch += [
            pltpu.VMEM(state.shape, F32),
            pltpu.VMEM((2 * column[0],) + column[1:], BF16),
        ]
    args += zs[:count]
    specs += [VMEM if held else HBM] * count
    args.append(before)
    specs.append(HBM if held else AFTER)
    if not held:
        scratch += [pltpu.VMEM((count,) + tall, F32), semaphores(count, parts)]
    return call(
        functools.partial(
            vectors_kernel, wanted=wanted, held=held, final=final, points=points
        ),
        args,
        specs,
        outs,
        scratch,
        "last_vector" if final else "vectors",
        1 << 23,
        len(wanted) << 21,
        {len(args) - 1: 0} if held else {},
    )


def shards(
    rhs,
    near_blocks,
    near_index,
    near_mask,
    basis,
    far_blocks,
    far_slot,
    far_mask,
    send_slot,
    transfer,
    top_blocks,
):
    outer, inner = lax.axis_size("outer"), lax.axis_size("inner")
    points = outer * inner * rhs.shape[0]
    leaves, rank = basis.shape[:2]
    slots = send_slot.shape[2]
    branch = lax.axis_index("outer").astype(jnp.int32).reshape(1)
    up_pairs = [(i, i + 1) for i in range(inner - 1)]
    down_pairs = [(j, i) for i, j in up_pairs]
    wanted = send_slot[0].T

    def exchange(array, axis):
        return lax.all_to_all(array, axis, split_axis=0, concat_axis=0, tiled=True)

    zs = [rhs.reshape(leaves, -1, rhs.shape[1])]
    out = stage(0, points, wanted, branch, zs[0], basis, transfer, None)
    packed, count, entries, turned, lifting, top = pack(
        branch, basis, transfer, top_blocks, far_blocks, far_mask, far_slot, near_index, near_mask,
        inner, slots,
    )
    listed = (count, entries)
    state = out["state"]
    for k in range(1, STEPS + 1):
        recv = exchange(out["send"], "inner")
        before = lax.ppermute(out["high"], "inner", up_pairs)
        after = lax.ppermute(out["low"], "inner", down_pairs)
        earlier = (packed,) if k == 1 else ()
        near = near_field(near_index, near_mask, near_blocks, out["coarse"], *earlier)
        done = near
        if k == STEPS:
            krylov = done = vectors(state, zs, list(range(STEPS - 1)), near, CHUNKS)[0]
        summed = gather_sum(recv, slots * rank, done)
        held = (near, basis, turned, transfer, lifting, top, *zs)
        local_far, blocks, held = far_field(listed, recv, packed, near_blocks, held, summed)
        near, *held = held

        def between(column):
            return halo_part(listed, near_index, blocks, before, after, near, column)

        column, other, near = over_branches(summed, outer, local_far, between)
        later = [column, other, state, local_far, near, *held]
        out = stage(k, points, wanted, branch, zs[0], basis, transfer, later)
        state = out["state"]
        zs = zs + [out["z"]]
    low = 4 if inner % 4 == 0 else inner
    loaded = load(zs, out["send"])
    summed = sum_over(out["send"], "inner", 1, low, loaded[0], AFTER_VMEM)
    krylov = vectors(state, loaded, [STEPS - 1], krylov, CHUNKS)[0]
    summed = sum_over(summed, "inner", low, inner // low, krylov, AFTER)
    column, other, _ = over_branches(summed, outer, loaded[0], lambda column: None)
    products = [branch, column, other]
    krylov, hessenberg = vectors(state, loaded, [STEPS], krylov, CHUNKS, products, points)
    return krylov.reshape(STEPS + 1, *rhs.shape), hessenberg


def solution(mesh):
    return jax.shard_map(
        shards,
        mesh=mesh,
        in_specs=(
            P(("outer", "inner"), None),
            P(("outer", "inner"), None, None, None),
            P(("outer", "inner"), None),
            P(("outer", "inner"), None),
            P(("outer", "inner"), None, None),
            P(("outer", "inner"), None, None, None),
            P(("outer", "inner"), None),
            P(("outer", "inner"), None),
            P(("outer", "inner"), None, None),
            P(("outer", "inner"), None, None),
            P("outer", None, None, None),
        ),
        out_specs=(P(None, ("outer", "inner"), None), P()),
        check_vma=False,
    )
```

```python
import functools

import jax
import jax.numpy as jnp
from jax import lax
from jax.experimental import pallas as pl
from jax.experimental.pallas import tpu as pltpu
from jax.sharding import PartitionSpec as P

HW = 2
STEPS = 4
EPS = 1e-06
PIECES = 3
DOT_ROWS = 16
STATE_ROWS = 64
VMEM_BYTES = 32 * 1024 * 1024
BF16 = jnp.bfloat16
F32 = jnp.float32


def dot(a, b):
    return jnp.dot(a, b, preferred_element_type=F32)


def dot_first(a, b):
    return lax.dot_general(a, b, (((0,), (0,)), ((), ())), preferred_element_type=F32)


def store_split(ref, values, count):
    rest = values
    ref[...] = jnp.zeros(ref.shape, F32)
    for piece in range(PIECES):
        part = rest.astype(BF16).astype(F32)
        ref[piece * 5 : piece * 5 + count, :] = part[:count]
        rest = rest - part


def joined(rows):
    return [rows[i : i + 1] + rows[5 + i : 6 + i] + rows[10 + i : 11 + i] for i in range(5)]


def entry_row(i, l):
    low, high = min(i, l), max(i, l)
    return 20 + high * (high + 1) // 2 + low


def basis_row(i, l):
    return 32 + i * (i + 1) // 2 + l


def coefficients(m, grams, state_in, state_out):
    last = m - 1
    entry = lambda i, l: state_in[entry_row(i, l) : entry_row(i, l) + 1, :]
    expand = lambda i, l: state_in[basis_row(i, l) : basis_row(i, l) + 1, :]

    def put(row, value):
        state_out[row : row + 1, :] = value

    dots = []
    for i in range(m):
        dots.append(sum(expand(i, l) * grams[l] for l in range(i + 1)))
    weights = [dots[i] + entry(i, last) for i in range(m)]
    spread = [sum(weights[l] * entry(i, l) for l in range(m)) for i in range(m)]
    square = grams[m]
    for i in range(m):
        square = square + weights[i] * (weights[i] + spread[i] - 2.0 * dots[i])
    total = jnp.maximum(square, 0.0) + EPS
    root = jnp.sqrt(total)
    inverse = 1.0 / root
    for l in range(m):
        value = sum(weights[i] * expand(i, l) for i in range(l, m))
        put(basis_row(m, l), -inverse * value)
    put(basis_row(m, m), inverse)
    for i in range(m):
        put(i * STEPS + last, weights[i] + (1.0 if i == last else 0.0))
    if m > 0:
        put(m * STEPS + last, root)
    if m < STEPS:
        for i in range(m):
            put(entry_row(i, m), (-entry(i, last) - spread[i]) * inverse)
        put(entry_row(m, m), -EPS / total)
    return weights, inverse


def from_branches(ups_ref, rank):
    rows = ups_ref[0, rank:].astype(F32)
    for c in range(1, ups_ref.shape[0]):
        rows = rows + ups_ref[c, rank:].astype(F32)
    return joined(rows)


SMEM = pl.BlockSpec(memory_space=pltpu.SMEM)
VMEM = pl.BlockSpec(memory_space=pltpu.VMEM)
HBM = pl.BlockSpec(memory_space=pl.ANY)
AFTER = pl.BlockSpec(memory_space=pl.ANY)
AFTER_VMEM = pl.BlockSpec(memory_space=pl.ANY)
LOOSE = pl.BlockSpec(memory_space=pl.ANY)
FREE = pl.BlockSpec(memory_space=pltpu.VMEM)
AHEAD = 3
CHUNKS = 4
PIN = True


def call(kernel, args, in_specs, outs, scratch, name, flops, moved, aliases={}):
    def pinned(array, spec):
        if not PIN or not any(spec is one for one in (VMEM, HBM, SMEM, AFTER, AFTER_VMEM)):
            return array
        in_vmem = spec is VMEM or spec is AFTER_VMEM
        return pltpu.with_memory_space_constraint(array, pltpu.VMEM if in_vmem else pltpu.HBM)

    def shape_of(shape, dtype, spec):
        if not PIN or not (spec is VMEM or spec is HBM):
            return jax.ShapeDtypeStruct(shape, dtype)
        return (pltpu.VMEM if spec is VMEM else pltpu.HBM)(shape, dtype)

    return pl.pallas_call(
        kernel,
        in_specs=list(in_specs),
        out_specs=[spec for _, _, spec in outs],
        out_shape=[shape_of(*out) for out in outs],
        scratch_shapes=scratch,
        input_output_aliases=aliases,
        compiler_params=pltpu.CompilerParams(vmem_limit_bytes=VMEM_BYTES),
        cost_estimate=pl.CostEstimate(flops=flops, bytes_accessed=moved, transcendentals=0),
        name=name,
    )(*[pinned(array, spec) for array, spec in zip(args, in_specs)])


def semaphores(*shape):
    return pltpu.SemaphoreType.DMA(shape)


def windowed(count, ahead, fetch, work):
    def start(i):
        for j, copy in enumerate(fetch(i)):
            copy.start(priority=j % 2)

    def body(i, carry):
        @pl.when(i + ahead < count)
        def _():
            start(i + ahead)

        for copy in fetch(i):
            copy.wait()
        work(i)
        return carry

    def begin():
        for i in range(min(ahead, count)):
            start(i)

    return begin, lambda: lax.fori_loop(0, count, body, 0)


def slab(i, size):
    return pl.ds(pl.multiple_of(i * size, size), size)


def pack_kernel(branch, mask_ref, slot_ref, index_ref, near_mask_ref, far_ref, *refs):
    basis_ref, transfer_ref, top_ref = refs[:3]
    out_ref, count_ref, list_ref, basis_out, transfer_out, top_out = refs[3:9]
    blocks, total, packed, basis, transfer, top, turned, lifting, row, arrived, left, came = refs[9:]
    leaves, entries, rank, _ = blocks.shape
    sources, _, width = packed.shape
    slots = width // rank
    near_entries = index_ref.shape[1]

    def fetch(leaf):
        return [pltpu.make_async_copy(far_ref.at[leaf], blocks.at[leaf], arrived.at[leaf])]

    def store(leaf):
        rows = slab(leaf, rank)
        return pltpu.make_async_copy(packed.at[:, rows], out_ref.at[:, rows], left.at[leaf])

    def work(leaf):
        total[...] = jnp.zeros(total.shape, F32)
        for f in range(entries):
            weight = mask_ref[leaf, f].astype(F32)
            total[slot_ref[leaf, f]] += blocks[leaf, f].astype(F32) * weight
        rows = slab(leaf, rank)
        for source in range(sources):
            sides = [total[source * slots + s] for s in range(slots)]
            packed[source, rows] = jnp.concatenate(sides, axis=1).astype(BF16)
        store(leaf).start()

    def list_one(i, count):
        leaf, n = i // near_entries, i % near_entries
        place = index_ref[leaf, n]
        hit = (near_mask_ref[leaf, n] != 0) & ((place < HW) | (place >= HW + leaves))
        list_ref[i] = 0

        @pl.when(hit)
        def _():
            list_ref[count] = i

        return count + hit.astype(jnp.int32)

    small = [
        pltpu.make_async_copy(basis_ref, basis, came.at[0]),
        pltpu.make_async_copy(transfer_ref, transfer, came.at[1]),
        pltpu.make_async_copy(top_ref, top, came.at[2]),
    ]
    for copy in small:
        copy.start()
    begin, run = windowed(leaves, AHEAD, fetch, work)
    begin()
    count_ref[0] = lax.fori_loop(0, list_ref.shape[0], list_one, 0)
    for copy in small:
        copy.wait()
    turn = lambda a: a.astype(F32).T.astype(BF16)
    for leaf in range(leaves):
        turned[leaf] = turn(basis[leaf])
    for pair in range(leaves // 2):
        columns = slice(pair * 2 * rank, (pair + 1) * 2 * rank)
        sides = [turn(transfer[2 * pair + j]) for j in range(2)]
        lifting[:, columns] = jnp.concatenate(sides, axis=1)
    for pair in range(top.shape[1] // 2):
        columns = slice(pair * 2 * rank, (pair + 1) * 2 * rank)
        sides = []
        for c in (2 * pair, 2 * pair + 1):
            sides.append(top[0, c] * (branch[0] != c).astype(F32).astype(BF16))
        row[:, columns] = jnp.concatenate(sides, axis=1)
    results = [
        pltpu.make_async_copy(turned, basis_out, came.at[0]),
        pltpu.make_async_copy(lifting, transfer_out, came.at[1]),
        pltpu.make_async_copy(row, top_out, came.at[2]),
    ]
    for copy in results:
        copy.start()
    run()
    for leaf in range(leaves):
        store(leaf).wait()
    for copy in results:
        copy.wait()


def pack(branch, basis, transfer, top_blocks, far_blocks, far_mask, far_slot, near_index, near_mask, inner, slots):
    leaves, entries, rank, _ = far_blocks.shape
    shape = (inner, leaves * rank, slots * rank)
    turned = (leaves, basis.shape[2], rank)
    lifting = (rank, leaves * rank)
    row = (rank, top_blocks.shape[1] * rank)
    return call(
        pack_kernel,
        (branch, far_mask, far_slot, near_index, near_mask, far_blocks, basis, transfer, top_blocks),
        (SMEM,) * 5 + (HBM,) * 4,
        [
            (shape, BF16, HBM),
            ((1,), jnp.int32, SMEM),
            ((near_index.size,), jnp.int32, SMEM),
            (turned, BF16, HBM),
            (lifting, BF16, HBM),
            (row, BF16, HBM),
        ],
        [
            pltpu.VMEM(far_blocks.shape, BF16),
            pltpu.VMEM((inner * slots, rank, rank), F32),
            pltpu.VMEM(shape, BF16),
            pltpu.VMEM(basis.shape, BF16),
            pltpu.VMEM(transfer.shape, BF16),
            pltpu.VMEM(top_blocks.shape, BF16),
            pltpu.VMEM(turned, BF16),
            pltpu.VMEM(lifting, BF16),
            pltpu.VMEM(row, BF16),
            semaphores(leaves),
            semaphores(leaves),
            semaphores(3),
        ],
        "pack",
        0,
        10 << 20,
    )


def near_kernel(index_ref, mask_ref, blocks_ref, own_ref, *refs):
    out_ref, blocks, own, result, arrived, came, left = refs[-7:]
    leaves, entries, size, _ = blocks.shape

    def fetch(leaf):
        halves = [pl.ds(j * (entries // 2), entries // 2) for j in range(2)]
        return [
            pltpu.make_async_copy(
                blocks_ref.at[leaf, half], blocks.at[leaf, half], arrived.at[leaf, j]
            )
            for j, half in enumerate(halves)
        ]

    def store(leaf):
        return pltpu.make_async_copy(
            result.at[leaf], out_ref.at[leaf], left.at[leaf]
        )

    def work(leaf):
        total = None
        for n in range(entries):
            place = index_ref[leaf, n] - HW
            inside = (place >= 0) & (place < leaves)
            weight = jnp.where(inside, mask_ref[leaf, n], 0).astype(F32).astype(BF16)
            values = own[jnp.clip(place, 0, leaves - 1)] * weight
            term = dot(blocks[leaf, n], values)
            total = term if total is None else total + term
        result[leaf] = total
        store(leaf).start()

    begin, run = windowed(leaves, AHEAD, fetch, work)
    copy = pltpu.make_async_copy(own_ref, own, came)
    copy.start()
    begin()
    copy.wait()
    run()
    for leaf in range(leaves):
        store(leaf).wait()


def near_field(near_index, near_mask, near_blocks, own, *earlier):
    leaves, _, size, _ = near_blocks.shape
    columns = own.shape[2]
    return call(
        near_kernel,
        (near_index, near_mask, near_blocks, own) + earlier,
        (SMEM, SMEM, HBM, HBM) + (AFTER,) * len(earlier),
        [((leaves, size, columns), F32, HBM)],
        [
            pltpu.VMEM(near_blocks.shape, BF16),
            pltpu.VMEM(own.shape, BF16),
            pltpu.VMEM((leaves, size, columns), F32),
            semaphores(leaves, 2),
            semaphores(),
            semaphores(leaves),
        ],
        "near_field",
        2 * near_blocks.size * columns,
        2 * near_blocks.size,
    )[0]


def gather_sum_kernel(recv, *refs, lead):
    out_ref, split = refs[-2:]
    rank = out_ref.shape[0] - DOT_ROWS
    total = recv[0, lead:].astype(F32)
    for i in range(1, recv.shape[0]):
        total = total + recv[i, lead:].astype(F32)
    store_split(split, jnp.concatenate(joined(total[rank:]), axis=0), 5)
    if rank > 0:
        out_ref[:rank] = total[:rank].astype(BF16)
    out_ref[rank:] = split[...].astype(BF16)


def gather_sum(recv, lead, earlier):
    _, rows, columns = recv.shape
    return call(
        functools.partial(gather_sum_kernel, lead=lead),
        (recv, earlier),
        (VMEM, AFTER),
        [((rows - lead, columns), BF16, VMEM)],
        [pltpu.VMEM((DOT_ROWS, columns), F32)],
        "gather_sum",
        1 << 20,
        1 << 19,
    )[0]


def stack_kernel(*refs):
    for i, ref in enumerate(refs[:-2]):
        refs[-1][i] = ref[...]


def over_branches(summed, outer, earlier, between):
    shifts = [[(o, (o + 2 * j) % outer) for o in range(outer)] for j in range(1, outer // 2)]
    parts = [summed] + [lax.ppermute(summed, "outer", shift) for shift in shifts]
    column = call(
        stack_kernel,
        parts + [earlier],
        [VMEM] * len(parts) + [AFTER_VMEM],
        [((len(parts),) + summed.shape, BF16, VMEM)],
        [],
        "stack",
        0,
        1 << 18,
    )[0]
    other = lax.ppermute(column, "outer", [(o, o ^ 1) for o in range(outer)])
    return column, other, between(column)


def in_order(branch, column, other, ups):
    count = ups.shape[0]
    for j in range(count // 2):
        ups[lax.rem(branch[0] + count - 2 * j, count)] = column[j]
        mate = branch[0] + 1 - 2 * lax.rem(branch[0], 2)
        ups[lax.rem(mate + count - 2 * j, count)] = other[j]


def far_kernel(count_ref, list_ref, recv, packed_ref, blocks_ref, *refs):
    held = (len(refs) - 7) // 2
    sources, (_, far, blocks), targets = refs[:held], refs[held : held + 3], refs[held + 3 : -4]
    packed, arrived, fetched, loaded = refs[-4:]
    share = packed.shape[0] // CHUNKS
    width = packed.shape[2]
    entries = blocks_ref.shape[1]
    count = count_ref[0]

    def fetch(i):
        some = slab(i, share)
        return [pltpu.make_async_copy(packed_ref.at[some], packed.at[some], arrived.at[i])]

    def block(i):
        entry = list_ref[i]
        return pltpu.make_async_copy(
            blocks_ref.at[entry // entries, entry % entries], blocks.at[i], fetched.at[i]
        )

    def ask(i, carry):
        block(i).start()
        return carry

    def have(i, carry):
        block(i).wait()
        return carry

    def work(i):
        term = None
        for j in range(share):
            source = i * share + j
            one = dot(packed[source], recv[source, :width])
            term = one if term is None else term + one

        @pl.when(i == 0)
        def _():
            far[...] = term

        @pl.when(i > 0)
        def _():
            far[...] += term

    loads = [
        pltpu.make_async_copy(source, target, loaded.at[i])
        for i, (source, target) in enumerate(zip(sources, targets))
    ]
    begin, run = windowed(CHUNKS, CHUNKS, fetch, work)
    begin()
    lax.fori_loop(0, count, ask, 0)
    for copy in loads:
        copy.start()
    run()
    lax.fori_loop(0, count, have, 0)
    for copy in loads:
        copy.wait()


def far_field(listed, recv, packed, near_blocks, held, earlier):
    sources, rows, _ = packed.shape
    leaves, entries, size, _ = near_blocks.shape
    outs = [((rows, recv.shape[2]), F32, VMEM), ((leaves * entries, size, size), BF16, VMEM)]
    far, blocks, *held = call(
        far_kernel,
        (*listed, recv, packed, near_blocks, *held, earlier),
        (SMEM, SMEM, VMEM, HBM, HBM) + (HBM,) * len(held) + (AFTER_VMEM,),
        outs + [(a.shape, a.dtype, VMEM) for a in held],
        [
            pltpu.VMEM(packed.shape, BF16),
            semaphores(CHUNKS),
            semaphores(leaves * entries),
            semaphores(len(held)),
        ],
        "far_field",
        2 * packed.size * recv.shape[2],
        2 * packed.size,
    )
    return far, blocks, held


def halo_kernel(count_ref, list_ref, index_ref, blocks, before, after, near_in, *refs):
    held = (len(refs) - 4) // 2
    sources, near, targets = refs[:held], refs[held + 1], refs[held + 2 : -2]
    halo, loaded = refs[-2:]
    loads = [
        pltpu.make_async_copy(source, target, loaded.at[i])
        for i, (source, target) in enumerate(zip(sources, targets))
    ]
    for copy in loads:
        copy.start()
    leaves, reach, entries = near.shape[0], before.shape[0], index_ref.shape[1]
    halo[:reach] = before[...]
    halo[reach:] = after[...]
    count = count_ref[0]
    at_once = 8

    def add(group, carry):
        terms = []
        for j in range(at_once):
            i = jnp.minimum(group * at_once + j, count - 1)
            weight = (group * at_once + j < count).astype(F32).astype(BF16)
            entry = list_ref[i]
            leaf = entry // entries
            place = index_ref[leaf, entry % entries]
            values = halo[jnp.where(place < reach, place, place - leaves)] * weight
            terms.append((leaf, dot(blocks[i], values)))
        for leaf, term in terms:
            near[leaf] += term
        return carry

    lax.fori_loop(0, (count + at_once - 1) // at_once, add, 0)
    for copy in loads:
        copy.wait()


def halo_part(listed, near_index, blocks, before, after, near, held, earlier):
    return call(
        halo_kernel,
        (*listed, near_index, blocks, before, after, near, *held, earlier),
        (SMEM, SMEM, SMEM, VMEM, VMEM, VMEM, VMEM) + (HBM,) * len(held) + (AFTER_VMEM,),
        [(a.shape, a.dtype, VMEM) for a in (near, *held)],
        [pltpu.VMEM((2 * before.shape[0],) + before.shape[1:], BF16), semaphores(len(held))],
        "halo_part",
        1 << 28,
        2 << 20,
        {6: 0},
    )


def sum_kernel(*refs, axis, stride):
    *parts, _, out, rows, split = refs
    count = len(parts)
    place = lax.rem(lax.axis_index(axis).astype(jnp.int32) // stride, count)
    for j, part in enumerate(parts):
        rows[lax.rem(place + count - j, count)] = part[...].astype(F32)
    total = rows[0]
    for i in range(1, count):
        total = total + rows[i]
    store_split(split, jnp.concatenate(joined(total), axis=0), 5)
    out[...] = split[...].astype(BF16)


def sum_over(dots, axis, stride, count, earlier, after):
    if count == 1:
        return dots
    size = lax.axis_size(axis)

    def moved(i, j):
        at = i // stride % count
        return i + ((at + j) % count - at) * stride

    parts = [dots]
    for j in range(1, count):
        parts.append(lax.ppermute(dots, axis, [(i, moved(i, j)) for i in range(size)]))
    return call(
        functools.partial(sum_kernel, axis=axis, stride=stride),
        (*parts, earlier),
        (VMEM,) * count + (after,),
        [(dots.shape, BF16, VMEM)],
        [pltpu.VMEM((count,) + dots.shape, F32), pltpu.VMEM((DOT_ROWS, dots.shape[1]), F32)],
        "sum_over",
        0,
        1 << 18,
    )[0]


def stage_kernel(*refs, k, points):
    refs = list(refs)
    take = lambda count: [refs.pop(0) for _ in range(count)]
    m = k - 1
    first, sends = k == 0, k < STEPS
    send_slot, branch = take(2)
    if first:
        z_any, basis_any, transfer_any = take(3)
    else:
        column, other, state, far, near, basis, turned, transfer, lifting, top = take(10)
        zs = take(k)
        (z_any,) = take(1)
    state_out, send = take(2)
    if sends:
        coarse_any, low_any, high_any = take(3)
    sums, split, arrived, left = take(4)
    if sends:
        coarse, skeletons, out = take(3)
    if first:
        basis, transfer, vectors, came = take(4)
    else:
        ups, result, coef, combined = take(4)

    leaves, rank, size = basis.shape
    group = leaves // CHUNKS

    def fetch(i):
        if not first:
            return []
        some = slab(i, group)
        return [pltpu.make_async_copy(z_any.at[some], vectors.at[some], arrived.at[i])]

    def stores(i):
        some = slab(i, group)
        pairs = []
        if not first:
            pairs.append((result.at[some], z_any.at[some]))
        if sends:
            pairs.append((coarse.at[some], coarse_any.at[some]))
        return [
            pltpu.make_async_copy(source, target, left.at[n, i])
            for n, (source, target) in enumerate(pairs)
        ]

    def work(i):
        for j in range(group):
            leaf = i * group + j
            if first:
                others = []
                z = vectors[leaf]
            else:
                others = [ref[leaf] for ref in zs]
                z = near[leaf] + dot(turned[leaf], combined[slab(leaf, rank)])
                for l in range(m):
                    z = z - coef[l : l + 1, :] * others[l + 1]
                z = z * coef[STEPS : STEPS + 1, :]
                result[leaf] = z
            if sends:
                rounded = z.astype(BF16)
                coarse[leaf] = rounded
                skeletons[slab(leaf, rank)] = dot(basis[leaf], rounded).astype(BF16)
            for l, vector in enumerate(others + [z]):
                sums[l] += jnp.sum((z * vector).reshape(size // 8, 8, z.shape[1]), axis=0)
        for copy in stores(i):
            copy.start()

    begin, run = windowed(CHUNKS, CHUNKS, fetch, work)
    if first:
        small = [
            pltpu.make_async_copy(basis_any, basis, came.at[0]),
            pltpu.make_async_copy(transfer_any, transfer, came.at[1]),
        ]
        for copy in small:
            copy.start()
    begin()
    sums[...] = jnp.zeros(sums.shape, F32)
    if first:
        state_out[...] = jnp.zeros(state_out.shape, F32)
        for copy in small:
            copy.wait()
    else:
        in_order(branch, column, other, ups)
        count, columns = ups.shape[0], ups.shape[2]
        incoming = dot(top[...], ups[:, :rank].reshape(count * rank, columns)).astype(BF16)
        down = dot(transfer[...].reshape(leaves * rank, rank), incoming)
        combined[...] = (far[...] + down).astype(BF16)
        grams = [row / points for row in from_branches(ups, rank)]
        state_out[...] = state[...]
        weights, inverse = coefficients(m, grams, state, state_out)
        for i, weight in enumerate(weights):
            coef[i : i + 1, :] = weight
        coef[STEPS : STEPS + 1, :] = inverse
    run()

    if sends:
        halos = [
            pltpu.make_async_copy(coarse.at[pl.ds(0, HW)], low_any, out.at[0]),
            pltpu.make_async_copy(coarse.at[pl.ds(leaves - HW, HW)], high_any, out.at[1]),
        ]
        for copy in halos:
            copy.start()
        if first:
            lifted = dot_first(transfer[...].reshape(leaves * rank, rank), skeletons[...])
        else:
            lifted = dot(lifting[...], skeletons[...])
        lifted = lifted.astype(BF16)
    products = [jnp.sum(sums[i], axis=0, keepdims=True) for i in range(k + 1)]
    products = jnp.concatenate(products + [jnp.zeros_like(products[0])] * (7 - k), axis=0)
    store_split(split, products, k + 1)
    dots = split[...].astype(BF16)
    if sends:
        slots, inner = send_slot.shape
        for r in range(inner):
            for s in range(slots):
                send[r, s * rank : (s + 1) * rank] = skeletons[slab(send_slot[s, r], rank)]
            send[r, slots * rank : (slots + 1) * rank] = lifted
            send[r, (slots + 1) * rank :] = dots
    else:
        send[...] = dots
    for i in range(CHUNKS):
        for copy in stores(i):
            copy.wait()
    if sends:
        for copy in halos:
            copy.wait()


def stage(k, points, send_slot, branch, rhs, basis, transfer, later):
    leaves, rank, size = basis.shape
    first, sends = k == 0, k < STEPS
    tall = rhs.shape
    columns = tall[2]
    slots, inner = send_slot.shape
    names, outs = [], []

    def get(name, shape, dtype, spec):
        names.append(name)
        outs.append((shape, dtype, spec))

    args, specs = [send_slot, branch], [SMEM, SMEM]
    if first:
        args += [rhs, basis, transfer]
        specs += [HBM] * 3
    else:
        args += later
        specs += [VMEM] * len(later)
        get("z", tall, F32, HBM if sends else VMEM)
    get("state", (STATE_ROWS, columns), F32, VMEM)
    rows = (slots + 1) * rank + DOT_ROWS
    get("send", (inner, rows, columns) if sends else (DOT_ROWS, columns), BF16, VMEM)
    if sends:
        get("coarse", tall, BF16, HBM)
        get("low", (HW, size, columns), BF16, LOOSE)
        get("high", (HW, size, columns), BF16, LOOSE)

    scratch = [
        pltpu.VMEM((STEPS + 1, 8, columns), F32),
        pltpu.VMEM((DOT_ROWS, columns), F32),
        semaphores(CHUNKS),
        semaphores(2, CHUNKS),
    ]
    if sends:
        scratch += [
            pltpu.VMEM(tall, BF16),
            pltpu.VMEM((leaves * rank, columns), BF16),
            semaphores(2),
        ]
    if first:
        scratch += [
            pltpu.VMEM(basis.shape, BF16),
            pltpu.VMEM(transfer.shape, BF16),
            pltpu.VMEM(tall, F32),
            semaphores(2),
        ]
    else:
        column = later[0].shape
        scratch += [
            pltpu.VMEM((2 * column[0],) + column[1:], BF16),
            pltpu.VMEM(tall, F32),
            pltpu.VMEM((8, columns), F32),
            pltpu.VMEM((leaves * rank, columns), BF16),
        ]
    results = call(
        functools.partial(stage_kernel, k=k, points=points),
        args,
        specs,
        outs,
        scratch,
        f"stage{k}",
        1 << 27,
        (k + 4) << 20,
    )
    return dict(zip(names, results))


def vectors_kernel(*refs, wanted, held, final, points):
    refs = list(refs)
    take = lambda count: [refs.pop(0) for _ in range(count)]
    (state,) = take(1)
    if final:
        branch, column, other = take(3)
    zs = take(wanted[-1] + 1)
    _, krylov = take(2)
    if final:
        (hess_out,) = take(1)
    result, left = take(2)
    if final:
        after, ups = take(2)
    else:
        after = state
    if not held:
        vectors, arrived = take(2)
    parts = left.shape[1]
    group = zs[0].shape[0] // parts

    def fetch(i):
        if held:
            return []
        some = slab(i, group)
        return [
            pltpu.make_async_copy(z.at[some], vectors.at[l, some], arrived.at[l, i])
            for l, z in enumerate(zs)
        ]

    def store(n, i):
        some = slab(i, group)
        return pltpu.make_async_copy(result.at[n, some], krylov.at[wanted[n], some], left.at[n, i])

    def work(i):
        for j in range(group):
            leaf = i * group + j
            for n, which in enumerate(wanted):
                vector = None
                for l in range(which + 1):
                    row = basis_row(which, l)
                    values = zs[l][leaf] if held else vectors[l, leaf]
                    term = after[row : row + 1, :] * values
                    vector = term if vector is None else vector + term
                result[n, leaf] = vector
        for n in range(len(wanted)):
            store(n, i).start()

    begin, run = windowed(parts, parts, fetch, work)
    begin()
    if final:
        in_order(branch, column, other, ups)
        grams = [row / points for row in from_branches(ups, 0)]
        after[...] = state[...]
        coefficients(STEPS, grams, state, after)
    run()
    if final:
        for i in range(STEPS + 1):
            for j in range(STEPS):
                row = i * STEPS + j
                if i <= j + 1:
                    hess_out[i, j : j + 1, :] = after[row : row + 1, :]
                else:
                    hess_out[i, j : j + 1, :] = jnp.zeros((1, hess_out.shape[2]), F32)
    for n in range(len(wanted)):
        for i in range(parts):
            store(n, i).wait()


def vectors(state, zs, wanted, before, parts, products=None, points=0):
    final = products is not None
    held = wanted[0] > 0
    tall = zs[0].shape
    count = wanted[-1] + 1
    shape = (STEPS + 1,) + tall
    scratch = [pltpu.VMEM((len(wanted),) + tall, F32), semaphores(len(wanted), parts)]
    outs = [(shape, F32, HBM)]
    args, specs = [state], [VMEM]
    if final:
        args += products
        specs += [SMEM, VMEM, VMEM]
        column = products[1].shape
        outs.append(((STEPS + 1, STEPS, tall[2]), F32, FREE))
        scratch += [
            pltpu.VMEM(state.shape, F32),
            pltpu.VMEM((2 * column[0],) + column[1:], BF16),
        ]
    args += zs[:count]
    specs += [VMEM if held else HBM] * count
    args.append(before)
    specs.append(HBM if held else AFTER)
    if not held:
        scratch += [pltpu.VMEM((count,) + tall, F32), semaphores(count, parts)]
    return call(
        functools.partial(
            vectors_kernel, wanted=wanted, held=held, final=final, points=points
        ),
        args,
        specs,
        outs,
        scratch,
        "last_vector" if final else "vectors",
        1 << 23,
        len(wanted) << 21,
        {len(args) - 1: 0} if held else {},
    )


def shards(
    rhs,
    near_blocks,
    near_index,
    near_mask,
    basis,
    far_blocks,
    far_slot,
    far_mask,
    send_slot,
    transfer,
    top_blocks,
):
    outer, inner = lax.axis_size("outer"), lax.axis_size("inner")
    points = outer * inner * rhs.shape[0]
    leaves, rank = basis.shape[:2]
    slots = send_slot.shape[2]
    branch = lax.axis_index("outer").astype(jnp.int32).reshape(1)
    up_pairs = [(i, i + 1) for i in range(inner - 1)]
    down_pairs = [(j, i) for i, j in up_pairs]
    wanted = send_slot[0].T

    def exchange(array, axis):
        return lax.all_to_all(array, axis, split_axis=0, concat_axis=0, tiled=True)

    zs = [rhs.reshape(leaves, -1, rhs.shape[1])]
    out = stage(0, points, wanted, branch, zs[0], basis, transfer, None)
    packed, count, entries, turned, lifting, top = pack(
        branch, basis, transfer, top_blocks, far_blocks, far_mask, far_slot, near_index, near_mask,
        inner, slots,
    )
    listed = (count, entries)
    state = out["state"]
    for k in range(1, STEPS + 1):
        recv = exchange(out["send"], "inner")
        before = lax.ppermute(out["high"], "inner", up_pairs)
        after = lax.ppermute(out["low"], "inner", down_pairs)
        earlier = (packed,) if k == 1 else ()
        near = near_field(near_index, near_mask, near_blocks, out["coarse"], *earlier)
        done = near
        if k == STEPS:
            krylov = done = vectors(state, zs, list(range(STEPS - 1)), near, CHUNKS)[0]
        summed = gather_sum(recv, slots * rank, done)
        local_far, blocks, (near,) = far_field(listed, recv, packed, near_blocks, (near,), summed)

        def between(column):
            held = (basis, turned, transfer, lifting, top, *zs)
            return halo_part(listed, near_index, blocks, before, after, near, held, column)

        column, other, (near, *held) = over_branches(summed, outer, local_far, between)
        later = [column, other, state, local_far, near, *held]
        out = stage(k, points, wanted, branch, zs[0], basis, transfer, later)
        state = out["state"]
        zs = zs + [out["z"]]
    low = 4 if inner % 4 == 0 else inner
    held = held[-STEPS:] + [out["z"]]
    krylov = vectors(state, held, [STEPS - 1], krylov, CHUNKS)[0]
    summed = sum_over(out["send"], "inner", 1, low, krylov, AFTER)
    summed = sum_over(summed, "inner", low, inner // low, summed, AFTER_VMEM)
    column, other, _ = over_branches(summed, outer, summed, lambda column: None)
    products = [branch, column, other]
    krylov, hessenberg = vectors(state, held, [STEPS], krylov, CHUNKS, products, points)
    return krylov.reshape(STEPS + 1, *rhs.shape), hessenberg


def solution(mesh):
    return jax.shard_map(
        shards,
        mesh=mesh,
        in_specs=(
            P(("outer", "inner"), None),
            P(("outer", "inner"), None, None, None),
            P(("outer", "inner"), None),
            P(("outer", "inner"), None),
            P(("outer", "inner"), None, None),
            P(("outer", "inner"), None, None, None),
            P(("outer", "inner"), None),
            P(("outer", "inner"), None),
            P(("outer", "inner"), None, None),
            P(("outer", "inner"), None, None),
            P("outer", None, None, None),
        ),
        out_specs=(P(None, ("outer", "inner"), None), P()),
        check_vma=False,
    )
```

```python
import functools

import jax
import jax.numpy as jnp
from jax import lax
from jax.experimental import pallas as pl
from jax.experimental.pallas import tpu as pltpu
from jax.sharding import PartitionSpec as P

HW = 2
STEPS = 4
EPS = 1e-06
PIECES = 3
DOT_ROWS = 16
STATE_ROWS = 64
VMEM_BYTES = 32 * 1024 * 1024
BF16 = jnp.bfloat16
F32 = jnp.float32


def dot(a, b):
    return jnp.dot(a, b, preferred_element_type=F32)


def dot_first(a, b):
    return lax.dot_general(a, b, (((0,), (0,)), ((), ())), preferred_element_type=F32)


def store_split(ref, values, count):
    rest = values
    ref[...] = jnp.zeros(ref.shape, F32)
    for piece in range(PIECES):
        part = rest.astype(BF16).astype(F32)
        ref[piece * 5 : piece * 5 + count, :] = part[:count]
        rest = rest - part


def joined(rows):
    return [rows[i : i + 1] + rows[5 + i : 6 + i] + rows[10 + i : 11 + i] for i in range(5)]


def entry_row(i, l):
    low, high = min(i, l), max(i, l)
    return 20 + high * (high + 1) // 2 + low


def basis_row(i, l):
    return 32 + i * (i + 1) // 2 + l


def coefficients(m, grams, state_in, state_out):
    last = m - 1
    entry = lambda i, l: state_in[entry_row(i, l) : entry_row(i, l) + 1, :]
    expand = lambda i, l: state_in[basis_row(i, l) : basis_row(i, l) + 1, :]

    def put(row, value):
        state_out[row : row + 1, :] = value

    dots = []
    for i in range(m):
        dots.append(sum(expand(i, l) * grams[l] for l in range(i + 1)))
    weights = [dots[i] + entry(i, last) for i in range(m)]
    spread = [sum(weights[l] * entry(i, l) for l in range(m)) for i in range(m)]
    square = grams[m]
    for i in range(m):
        square = square + weights[i] * (weights[i] + spread[i] - 2.0 * dots[i])
    total = jnp.maximum(square, 0.0) + EPS
    root = jnp.sqrt(total)
    inverse = 1.0 / root
    for l in range(m):
        value = sum(weights[i] * expand(i, l) for i in range(l, m))
        put(basis_row(m, l), -inverse * value)
    put(basis_row(m, m), inverse)
    for i in range(m):
        put(i * STEPS + last, weights[i] + (1.0 if i == last else 0.0))
    if m > 0:
        put(m * STEPS + last, root)
    if m < STEPS:
        for i in range(m):
            put(entry_row(i, m), (-entry(i, last) - spread[i]) * inverse)
        put(entry_row(m, m), -EPS / total)
    return weights, inverse


def from_branches(ups_ref, rank):
    rows = ups_ref[0, rank:].astype(F32)
    for c in range(1, ups_ref.shape[0]):
        rows = rows + ups_ref[c, rank:].astype(F32)
    return joined(rows)


SMEM = pl.BlockSpec(memory_space=pltpu.SMEM)
VMEM = pl.BlockSpec(memory_space=pltpu.VMEM)
HBM = pl.BlockSpec(memory_space=pl.ANY)
AFTER = pl.BlockSpec(memory_space=pl.ANY)
AFTER_VMEM = pl.BlockSpec(memory_space=pl.ANY)
LOOSE = pl.BlockSpec(memory_space=pl.ANY)
FREE = pl.BlockSpec(memory_space=pltpu.VMEM)
AHEAD = 3
CHUNKS = 4
PIN = True


def call(kernel, args, in_specs, outs, scratch, name, flops, moved, aliases={}):
    def pinned(array, spec):
        if not PIN or not any(spec is one for one in (VMEM, HBM, SMEM, AFTER, AFTER_VMEM)):
            return array
        in_vmem = spec is VMEM or spec is AFTER_VMEM
        return pltpu.with_memory_space_constraint(array, pltpu.VMEM if in_vmem else pltpu.HBM)

    def shape_of(shape, dtype, spec):
        if not PIN or not (spec is VMEM or spec is HBM):
            return jax.ShapeDtypeStruct(shape, dtype)
        return (pltpu.VMEM if spec is VMEM else pltpu.HBM)(shape, dtype)

    return pl.pallas_call(
        kernel,
        in_specs=list(in_specs),
        out_specs=[spec for _, _, spec in outs],
        out_shape=[shape_of(*out) for out in outs],
        scratch_shapes=scratch,
        input_output_aliases=aliases,
        compiler_params=pltpu.CompilerParams(vmem_limit_bytes=VMEM_BYTES),
        cost_estimate=pl.CostEstimate(flops=flops, bytes_accessed=moved, transcendentals=0),
        name=name,
    )(*[pinned(array, spec) for array, spec in zip(args, in_specs)])


def semaphores(*shape):
    return pltpu.SemaphoreType.DMA(shape)


def windowed(count, ahead, fetch, work):
    def start(i):
        for j, copy in enumerate(fetch(i)):
            copy.start(priority=j % 2)

    def body(i, carry):
        @pl.when(i + ahead < count)
        def _():
            start(i + ahead)

        for copy in fetch(i):
            copy.wait()
        work(i)
        return carry

    def begin():
        for i in range(min(ahead, count)):
            start(i)

    return begin, lambda: lax.fori_loop(0, count, body, 0)


def slab(i, size):
    return pl.ds(pl.multiple_of(i * size, size), size)


def pack_kernel(branch, mask_ref, slot_ref, index_ref, near_mask_ref, far_ref, *refs):
    basis_ref, transfer_ref, top_ref = refs[:3]
    out_ref, count_ref, list_ref, basis_out, transfer_out, top_out = refs[3:9]
    blocks, total, packed, basis, transfer, top, turned, lifting, row, arrived, left, came = refs[9:]
    leaves, entries, rank, _ = blocks.shape
    sources, _, width = packed.shape
    slots = width // rank
    near_entries = index_ref.shape[1]
    side = lax.broadcasted_iota(jnp.int32, (1, 2 * rank), 1) // rank

    def fetch(leaf):
        return [pltpu.make_async_copy(far_ref.at[leaf], blocks.at[leaf], arrived.at[leaf])]

    def store(leaf):
        rows = slab(leaf, rank)
        return pltpu.make_async_copy(packed.at[:, rows], out_ref.at[:, rows], left.at[leaf])

    def work(leaf):
        total[...] = jnp.zeros(total.shape, F32)
        for f in range(entries):
            slot = slot_ref[leaf, f]
            block = blocks[leaf, f].astype(F32)
            weight = jnp.where(side == slot % 2, mask_ref[leaf, f], 0).astype(F32)
            total[slot // 2] += jnp.concatenate([block, block], axis=1) * weight
        rows = slab(leaf, rank)
        pairs = slots // 2
        for source in range(sources):
            sides = [total[source * pairs + s] for s in range(pairs)]
            packed[source, rows] = jnp.concatenate(sides, axis=1).astype(BF16)
        store(leaf).start()

    def list_one(i, count):
        leaf, n = i // near_entries, i % near_entries
        place = index_ref[leaf, n]
        hit = (near_mask_ref[leaf, n] != 0) & ((place < HW) | (place >= HW + leaves))
        list_ref[i] = 0

        @pl.when(hit)
        def _():
            list_ref[count] = i

        return count + hit.astype(jnp.int32)

    small = [
        pltpu.make_async_copy(basis_ref, basis, came.at[0]),
        pltpu.make_async_copy(transfer_ref, transfer, came.at[1]),
        pltpu.make_async_copy(top_ref, top, came.at[2]),
    ]
    for copy in small:
        copy.start()
    begin, run = windowed(leaves, AHEAD, fetch, work)
    begin()
    count_ref[0] = lax.fori_loop(0, list_ref.shape[0], list_one, 0)
    for copy in small:
        copy.wait()
    turn = lambda a: a.astype(F32).T.astype(BF16)
    for leaf in range(leaves):
        turned[leaf] = turn(basis[leaf])
    for pair in range(leaves // 2):
        columns = slice(pair * 2 * rank, (pair + 1) * 2 * rank)
        sides = [turn(transfer[2 * pair + j]) for j in range(2)]
        lifting[:, columns] = jnp.concatenate(sides, axis=1)
    for pair in range(top.shape[1] // 2):
        columns = slice(pair * 2 * rank, (pair + 1) * 2 * rank)
        sides = []
        for c in (2 * pair, 2 * pair + 1):
            sides.append(top[0, c] * (branch[0] != c).astype(F32).astype(BF16))
        row[:, columns] = jnp.concatenate(sides, axis=1)
    results = [
        pltpu.make_async_copy(turned, basis_out, came.at[0]),
        pltpu.make_async_copy(lifting, transfer_out, came.at[1]),
        pltpu.make_async_copy(row, top_out, came.at[2]),
    ]
    for copy in results:
        copy.start()
    run()
    for leaf in range(leaves):
        store(leaf).wait()
    for copy in results:
        copy.wait()


def pack(branch, basis, transfer, top_blocks, far_blocks, far_mask, far_slot, near_index, near_mask, inner, slots):
    leaves, entries, rank, _ = far_blocks.shape
    shape = (inner, leaves * rank, slots * rank)
    turned = (leaves, basis.shape[2], rank)
    lifting = (rank, leaves * rank)
    row = (rank, top_blocks.shape[1] * rank)
    return call(
        pack_kernel,
        (branch, far_mask, far_slot, near_index, near_mask, far_blocks, basis, transfer, top_blocks),
        (SMEM,) * 5 + (HBM,) * 4,
        [
            (shape, BF16, HBM),
            ((1,), jnp.int32, SMEM),
            ((near_index.size,), jnp.int32, SMEM),
            (turned, BF16, HBM),
            (lifting, BF16, HBM),
            (row, BF16, HBM),
        ],
        [
            pltpu.VMEM(far_blocks.shape, BF16),
            pltpu.VMEM((inner * slots // 2, rank, 2 * rank), F32),
            pltpu.VMEM(shape, BF16),
            pltpu.VMEM(basis.shape, BF16),
            pltpu.VMEM(transfer.shape, BF16),
            pltpu.VMEM(top_blocks.shape, BF16),
            pltpu.VMEM(turned, BF16),
            pltpu.VMEM(lifting, BF16),
            pltpu.VMEM(row, BF16),
            semaphores(leaves),
            semaphores(leaves),
            semaphores(3),
        ],
        "pack",
        0,
        10 << 20,
    )


def near_kernel(index_ref, mask_ref, blocks_ref, own_ref, *refs):
    out_ref, blocks, own, result, arrived, came, left = refs[-7:]
    leaves, entries, size, _ = blocks.shape

    def fetch(leaf):
        halves = [pl.ds(j * (entries // 2), entries // 2) for j in range(2)]
        return [
            pltpu.make_async_copy(
                blocks_ref.at[leaf, half], blocks.at[leaf, half], arrived.at[leaf, j]
            )
            for j, half in enumerate(halves)
        ]

    def store(leaf):
        return pltpu.make_async_copy(
            result.at[leaf], out_ref.at[leaf], left.at[leaf]
        )

    def work(leaf):
        total = None
        for n in range(entries):
            place = index_ref[leaf, n] - HW
            inside = (place >= 0) & (place < leaves)
            weight = jnp.where(inside, mask_ref[leaf, n], 0).astype(F32).astype(BF16)
            values = own[jnp.clip(place, 0, leaves - 1)] * weight
            term = dot(blocks[leaf, n], values)
            total = term if total is None else total + term
        result[leaf] = total
        store(leaf).start()

    begin, run = windowed(leaves, AHEAD, fetch, work)
    copy = pltpu.make_async_copy(own_ref, own, came)
    copy.start()
    begin()
    copy.wait()
    run()
    for leaf in range(leaves):
        store(leaf).wait()


def near_field(near_index, near_mask, near_blocks, own, *earlier):
    leaves, _, size, _ = near_blocks.shape
    columns = own.shape[2]
    return call(
        near_kernel,
        (near_index, near_mask, near_blocks, own) + earlier,
        (SMEM, SMEM, HBM, HBM) + (AFTER,) * len(earlier),
        [((leaves, size, columns), F32, HBM)],
        [
            pltpu.VMEM(near_blocks.shape, BF16),
            pltpu.VMEM(own.shape, BF16),
            pltpu.VMEM((leaves, size, columns), F32),
            semaphores(leaves, 2),
            semaphores(),
            semaphores(leaves),
        ],
        "near_field",
        2 * near_blocks.size * columns,
        2 * near_blocks.size,
    )[0]


def gather_sum_kernel(recv, *refs, lead):
    out_ref, split = refs[-2:]
    rank = out_ref.shape[0] - DOT_ROWS
    total = recv[0, lead:].astype(F32)
    for i in range(1, recv.shape[0]):
        total = total + recv[i, lead:].astype(F32)
    store_split(split, jnp.concatenate(joined(total[rank:]), axis=0), 5)
    if rank > 0:
        out_ref[:rank] = total[:rank].astype(BF16)
    out_ref[rank:] = split[...].astype(BF16)


def gather_sum(recv, lead, earlier):
    _, rows, columns = recv.shape
    return call(
        functools.partial(gather_sum_kernel, lead=lead),
        (recv, earlier),
        (VMEM, AFTER),
        [((rows - lead, columns), BF16, VMEM)],
        [pltpu.VMEM((DOT_ROWS, columns), F32)],
        "gather_sum",
        1 << 20,
        1 << 19,
    )[0]


def stack_kernel(*refs):
    for i, ref in enumerate(refs[:-2]):
        refs[-1][i] = ref[...]


def over_branches(summed, outer, earlier, between):
    shifts = [[(o, (o + 2 * j) % outer) for o in range(outer)] for j in range(1, outer // 2)]
    parts = [summed] + [lax.ppermute(summed, "outer", shift) for shift in shifts]
    column = call(
        stack_kernel,
        parts + [earlier],
        [VMEM] * len(parts) + [AFTER_VMEM],
        [((len(parts),) + summed.shape, BF16, VMEM)],
        [],
        "stack",
        0,
        1 << 18,
    )[0]
    other = lax.ppermute(column, "outer", [(o, o ^ 1) for o in range(outer)])
    return column, other, between(column)


def in_order(branch, column, other, ups):
    count = ups.shape[0]
    for j in range(count // 2):
        ups[lax.rem(branch[0] + count - 2 * j, count)] = column[j]
        mate = branch[0] + 1 - 2 * lax.rem(branch[0], 2)
        ups[lax.rem(mate + count - 2 * j, count)] = other[j]


def far_kernel(count_ref, list_ref, recv, packed_ref, blocks_ref, *refs):
    held = (len(refs) - 7) // 2
    sources, (_, far, blocks), targets = refs[:held], refs[held : held + 3], refs[held + 3 : -4]
    packed, arrived, fetched, loaded = refs[-4:]
    share = packed.shape[0] // CHUNKS
    width = packed.shape[2]
    entries = blocks_ref.shape[1]
    count = count_ref[0]

    def fetch(i):
        some = slab(i, share)
        return [pltpu.make_async_copy(packed_ref.at[some], packed.at[some], arrived.at[i])]

    def block(i):
        entry = list_ref[i]
        return pltpu.make_async_copy(
            blocks_ref.at[entry // entries, entry % entries], blocks.at[i], fetched.at[i]
        )

    def ask(i, carry):
        block(i).start()
        return carry

    def have(i, carry):
        block(i).wait()
        return carry

    loads = [
        pltpu.make_async_copy(source, target, loaded.at[i])
        for i, (source, target) in enumerate(zip(sources, targets))
    ]

    def work(i):
        @pl.when(i == 0)
        def _():
            lax.fori_loop(0, count, ask, 0)
            for copy in loads:
                copy.start()

        term = None
        for j in range(share):
            source = i * share + j
            one = dot(packed[source], recv[source, :width])
            term = one if term is None else term + one

        @pl.when(i == 0)
        def _():
            far[...] = term

        @pl.when(i > 0)
        def _():
            far[...] += term

    begin, run = windowed(CHUNKS, CHUNKS, fetch, work)
    begin()
    run()
    lax.fori_loop(0, count, have, 0)
    for copy in loads:
        copy.wait()


def far_field(listed, recv, packed, near_blocks, held, earlier):
    sources, rows, _ = packed.shape
    leaves, entries, size, _ = near_blocks.shape
    outs = [((rows, recv.shape[2]), F32, VMEM), ((leaves * entries, size, size), BF16, VMEM)]
    far, blocks, *held = call(
        far_kernel,
        (*listed, recv, packed, near_blocks, *held, earlier),
        (SMEM, SMEM, VMEM, HBM, HBM) + (HBM,) * len(held) + (AFTER_VMEM,),
        outs + [(a.shape, a.dtype, VMEM) for a in held],
        [
            pltpu.VMEM(packed.shape, BF16),
            semaphores(CHUNKS),
            semaphores(leaves * entries),
            semaphores(len(held)),
        ],
        "far_field",
        2 * packed.size * recv.shape[2],
        2 * packed.size,
    )
    return far, blocks, held


def halo_kernel(count_ref, list_ref, index_ref, blocks, before, after, near_in, *refs):
    held = (len(refs) - 4) // 2
    sources, near, targets = refs[:held], refs[held + 1], refs[held + 2 : -2]
    halo, loaded = refs[-2:]
    loads = [
        pltpu.make_async_copy(source, target, loaded.at[i])
        for i, (source, target) in enumerate(zip(sources, targets))
    ]
    for copy in loads:
        copy.start()
    leaves, reach, entries = near.shape[0], before.shape[0], index_ref.shape[1]
    halo[:reach] = before[...]
    halo[reach:] = after[...]
    count = count_ref[0]
    at_once = 8

    def add(group, carry):
        terms = []
        for j in range(at_once):
            i = jnp.minimum(group * at_once + j, count - 1)
            weight = (group * at_once + j < count).astype(F32).astype(BF16)
            entry = list_ref[i]
            leaf = entry // entries
            place = index_ref[leaf, entry % entries]
            values = halo[jnp.where(place < reach, place, place - leaves)] * weight
            terms.append((leaf, dot(blocks[i], values)))
        for leaf, term in terms:
            near[leaf] += term
        return carry

    lax.fori_loop(0, (count + at_once - 1) // at_once, add, 0)
    for copy in loads:
        copy.wait()


def halo_part(listed, near_index, blocks, before, after, near, held, earlier):
    return call(
        halo_kernel,
        (*listed, near_index, blocks, before, after, near, *held, earlier),
        (SMEM, SMEM, SMEM, VMEM, VMEM, VMEM, VMEM) + (HBM,) * len(held) + (AFTER_VMEM,),
        [(a.shape, a.dtype, VMEM) for a in (near, *held)],
        [pltpu.VMEM((2 * before.shape[0],) + before.shape[1:], BF16), semaphores(len(held))],
        "halo_part",
        1 << 28,
        2 << 20,
        {6: 0},
    )


def sum_kernel(*refs, axis, stride):
    *parts, _, out, rows, split = refs
    count = len(parts)
    place = lax.rem(lax.axis_index(axis).astype(jnp.int32) // stride, count)
    for j, part in enumerate(parts):
        rows[lax.rem(place + count - j, count)] = part[...].astype(F32)
    total = rows[0]
    for i in range(1, count):
        total = total + rows[i]
    store_split(split, jnp.concatenate(joined(total), axis=0), 5)
    out[...] = split[...].astype(BF16)


def sum_over(dots, axis, stride, count, earlier, after):
    if count == 1:
        return dots
    size = lax.axis_size(axis)

    def moved(i, j):
        at = i // stride % count
        return i + ((at + j) % count - at) * stride

    parts = [dots]
    for j in range(1, count):
        parts.append(lax.ppermute(dots, axis, [(i, moved(i, j)) for i in range(size)]))
    return call(
        functools.partial(sum_kernel, axis=axis, stride=stride),
        (*parts, earlier),
        (VMEM,) * count + (after,),
        [(dots.shape, BF16, VMEM)],
        [pltpu.VMEM((count,) + dots.shape, F32), pltpu.VMEM((DOT_ROWS, dots.shape[1]), F32)],
        "sum_over",
        0,
        1 << 18,
    )[0]


def stage_kernel(*refs, k, points):
    refs = list(refs)
    take = lambda count: [refs.pop(0) for _ in range(count)]
    m = k - 1
    first, sends = k == 0, k < STEPS
    send_slot, branch = take(2)
    if first:
        z_any, basis_any, transfer_any = take(3)
    else:
        column, other, state, far, near, basis, turned, transfer, lifting, top = take(10)
        zs = take(k)
        (z_any,) = take(1)
    state_out, send = take(2)
    if sends:
        coarse_any, low_any, high_any = take(3)
    sums, split, arrived, left = take(4)
    if sends:
        coarse, skeletons, out = take(3)
    if first:
        basis, transfer, vectors, came = take(4)
    else:
        ups, result, coef, combined = take(4)
    streamed = zs if sends and not first else []
    if streamed:
        vectors = take(1)[0]

    leaves, rank, size = basis.shape
    group = leaves // CHUNKS

    def fetch(i):
        some = slab(i, group)
        if first:
            return [pltpu.make_async_copy(z_any.at[some], vectors.at[some], arrived.at[0, i])]
        return [
            pltpu.make_async_copy(z.at[some], vectors.at[l, some], arrived.at[l, i])
            for l, z in enumerate(streamed)
        ]

    def stores(leaf):
        pairs = []
        if not first:
            pairs.append((result.at[leaf], z_any.at[leaf]))
        if sends:
            pairs.append((coarse.at[leaf], coarse_any.at[leaf]))
        return [
            pltpu.make_async_copy(source, target, left.at[n, leaf])
            for n, (source, target) in enumerate(pairs)
        ]

    def work(i):
        for j in range(group):
            leaf = i * group + j
            if first:
                others = []
                z = vectors[leaf]
            else:
                others = [vectors[l, leaf] if streamed else zs[l][leaf] for l in range(k)]
                z = near[leaf] + dot(turned[leaf], combined[slab(leaf, rank)])
                for l in range(m):
                    z = z - coef[l : l + 1, :] * others[l + 1]
                z = z * coef[STEPS : STEPS + 1, :]
                result[leaf] = z
            if sends:
                rounded = z.astype(BF16)
                coarse[leaf] = rounded
                skeletons[slab(leaf, rank)] = dot(basis[leaf], rounded).astype(BF16)
            for l, vector in enumerate(others + [z]):
                sums[l] += jnp.sum((z * vector).reshape(size // 8, 8, z.shape[1]), axis=0)
        for j in range(group):
            for copy in stores(i * group + j):
                copy.start()

    begin, run = windowed(CHUNKS, CHUNKS, fetch, work)
    if first:
        small = [
            pltpu.make_async_copy(basis_any, basis, came.at[0]),
            pltpu.make_async_copy(transfer_any, transfer, came.at[1]),
        ]
        for copy in small:
            copy.start()
    begin()
    sums[...] = jnp.zeros(sums.shape, F32)
    if first:
        state_out[...] = jnp.zeros(state_out.shape, F32)
        for copy in small:
            copy.wait()
    else:
        in_order(branch, column, other, ups)
        count, columns = ups.shape[0], ups.shape[2]
        incoming = dot(top[...], ups[:, :rank].reshape(count * rank, columns)).astype(BF16)
        down = dot(transfer[...].reshape(leaves * rank, rank), incoming)
        combined[...] = (far[...] + down).astype(BF16)
        grams = [row / points for row in from_branches(ups, rank)]
        state_out[...] = state[...]
        weights, inverse = coefficients(m, grams, state, state_out)
        for i, weight in enumerate(weights):
            coef[i : i + 1, :] = weight
        coef[STEPS : STEPS + 1, :] = inverse
    run()

    if sends:
        halos = [
            pltpu.make_async_copy(coarse.at[pl.ds(0, HW)], low_any, out.at[0]),
            pltpu.make_async_copy(coarse.at[pl.ds(leaves - HW, HW)], high_any, out.at[1]),
        ]
        for copy in halos:
            copy.start()
        if first:
            lifted = dot_first(transfer[...].reshape(leaves * rank, rank), skeletons[...])
        else:
            lifted = dot(lifting[...], skeletons[...])
        lifted = lifted.astype(BF16)
    products = [jnp.sum(sums[i], axis=0, keepdims=True) for i in range(k + 1)]
    products = jnp.concatenate(products + [jnp.zeros_like(products[0])] * (7 - k), axis=0)
    store_split(split, products, k + 1)
    dots = split[...].astype(BF16)
    if sends:
        slots, inner = send_slot.shape
        for r in range(inner):
            for s in range(slots):
                send[r, s * rank : (s + 1) * rank] = skeletons[slab(send_slot[s, r], rank)]
            send[r, slots * rank : (slots + 1) * rank] = lifted
            send[r, (slots + 1) * rank :] = dots
    else:
        send[...] = dots
    for leaf in range(leaves):
        for copy in stores(leaf):
            copy.wait()
    if sends:
        for copy in halos:
            copy.wait()


def stage(k, points, send_slot, branch, rhs, basis, transfer, later):
    leaves, rank, size = basis.shape
    first, sends = k == 0, k < STEPS
    tall = rhs.shape
    columns = tall[2]
    slots, inner = send_slot.shape
    names, outs = [], []

    def get(name, shape, dtype, spec):
        names.append(name)
        outs.append((shape, dtype, spec))

    args, specs = [send_slot, branch], [SMEM, SMEM]
    if first:
        args += [rhs, basis, transfer]
        specs += [HBM] * 3
    else:
        args += later
        specs += [VMEM] * (len(later) - k) + [HBM if sends else VMEM] * k
        get("z", tall, F32, HBM if sends else VMEM)
    get("state", (STATE_ROWS, columns), F32, VMEM)
    rows = (slots + 1) * rank + DOT_ROWS
    get("send", (inner, rows, columns) if sends else (DOT_ROWS, columns), BF16, VMEM)
    if sends:
        get("coarse", tall, BF16, HBM)
        get("low", (HW, size, columns), BF16, LOOSE)
        get("high", (HW, size, columns), BF16, LOOSE)

    scratch = [
        pltpu.VMEM((STEPS + 1, 8, columns), F32),
        pltpu.VMEM((DOT_ROWS, columns), F32),
        semaphores(max(k, 1), CHUNKS),
        semaphores(2, leaves),
    ]
    if sends:
        scratch += [
            pltpu.VMEM(tall, BF16),
            pltpu.VMEM((leaves * rank, columns), BF16),
            semaphores(2),
        ]
    if first:
        scratch += [
            pltpu.VMEM(basis.shape, BF16),
            pltpu.VMEM(transfer.shape, BF16),
            pltpu.VMEM(tall, F32),
            semaphores(2),
        ]
    else:
        column = later[0].shape
        scratch += [
            pltpu.VMEM((2 * column[0],) + column[1:], BF16),
            pltpu.VMEM(tall, F32),
            pltpu.VMEM((8, columns), F32),
            pltpu.VMEM((leaves * rank, columns), BF16),
        ]
        if sends:
            scratch.append(pltpu.VMEM((k,) + tall, F32))
    results = call(
        functools.partial(stage_kernel, k=k, points=points),
        args,
        specs,
        outs,
        scratch,
        f"stage{k}",
        1 << 27,
        (k + 4) << 20,
    )
    return dict(zip(names, results))


def vectors_kernel(*refs, wanted, held, final, points):
    refs = list(refs)
    take = lambda count: [refs.pop(0) for _ in range(count)]
    (state,) = take(1)
    if final:
        branch, column, other = take(3)
    zs = take(wanted[-1] + 1)
    _, krylov = take(2)
    if final:
        (hess_out,) = take(1)
    result, left = take(2)
    if final:
        after, ups = take(2)
    else:
        after = state
    if not held:
        vectors, arrived = take(2)
    parts = left.shape[1]
    group = zs[0].shape[0] // parts

    def fetch(i):
        if held:
            return []
        some = slab(i, group)
        return [
            pltpu.make_async_copy(z.at[some], vectors.at[l, some], arrived.at[l, i])
            for l, z in enumerate(zs)
        ]

    def store(n, i):
        some = slab(i, group)
        return pltpu.make_async_copy(result.at[n, some], krylov.at[wanted[n], some], left.at[n, i])

    def work(i):
        for j in range(group):
            leaf = i * group + j
            for n, which in enumerate(wanted):
                vector = None
                for l in range(which + 1):
                    row = basis_row(which, l)
                    values = zs[l][leaf] if held else vectors[l, leaf]
                    term = after[row : row + 1, :] * values
                    vector = term if vector is None else vector + term
                result[n, leaf] = vector
        for n in range(len(wanted)):
            store(n, i).start()

    begin, run = windowed(parts, parts, fetch, work)
    begin()
    if final:
        in_order(branch, column, other, ups)
        grams = [row / points for row in from_branches(ups, 0)]
        after[...] = state[...]
        coefficients(STEPS, grams, state, after)
    run()
    if final:
        for i in range(STEPS + 1):
            for j in range(STEPS):
                row = i * STEPS + j
                if i <= j + 1:
                    hess_out[i, j : j + 1, :] = after[row : row + 1, :]
                else:
                    hess_out[i, j : j + 1, :] = jnp.zeros((1, hess_out.shape[2]), F32)
    for n in range(len(wanted)):
        for i in range(parts):
            store(n, i).wait()


def vectors(state, zs, wanted, before, parts, products=None, points=0):
    final = products is not None
    held = wanted[0] > 0
    tall = zs[0].shape
    count = wanted[-1] + 1
    shape = (STEPS + 1,) + tall
    scratch = [pltpu.VMEM((len(wanted),) + tall, F32), semaphores(len(wanted), parts)]
    outs = [(shape, F32, HBM)]
    args, specs = [state], [VMEM]
    if final:
        args += products
        specs += [SMEM, VMEM, VMEM]
        column = products[1].shape
        outs.append(((STEPS + 1, STEPS, tall[2]), F32, FREE))
        scratch += [
            pltpu.VMEM(state.shape, F32),
            pltpu.VMEM((2 * column[0],) + column[1:], BF16),
        ]
    args += zs[:count]
    specs += [VMEM if held else HBM] * count
    args.append(before)
    specs.append(HBM if held else AFTER)
    if not held:
        scratch += [pltpu.VMEM((count,) + tall, F32), semaphores(count, parts)]
    return call(
        functools.partial(
            vectors_kernel, wanted=wanted, held=held, final=final, points=points
        ),
        args,
        specs,
        outs,
        scratch,
        "last_vector" if final else "vectors",
        1 << 23,
        len(wanted) << 21,
        {len(args) - 1: 0} if held else {},
    )


def shards(
    rhs,
    near_blocks,
    near_index,
    near_mask,
    basis,
    far_blocks,
    far_slot,
    far_mask,
    send_slot,
    transfer,
    top_blocks,
):
    outer, inner = lax.axis_size("outer"), lax.axis_size("inner")
    points = outer * inner * rhs.shape[0]
    leaves, rank = basis.shape[:2]
    slots = send_slot.shape[2]
    branch = lax.axis_index("outer").astype(jnp.int32).reshape(1)
    up_pairs = [(i, i + 1) for i in range(inner - 1)]
    down_pairs = [(j, i) for i, j in up_pairs]
    wanted = send_slot[0].T

    def exchange(array, axis):
        return lax.all_to_all(array, axis, split_axis=0, concat_axis=0, tiled=True)

    zs = [rhs.reshape(leaves, -1, rhs.shape[1])]
    out = stage(0, points, wanted, branch, zs[0], basis, transfer, None)
    packed, count, entries, turned, lifting, top = pack(
        branch, basis, transfer, top_blocks, far_blocks, far_mask, far_slot, near_index, near_mask,
        inner, slots,
    )
    listed = (count, entries)
    state = out["state"]
    for k in range(1, STEPS + 1):
        recv = exchange(out["send"], "inner")
        before = lax.ppermute(out["high"], "inner", up_pairs)
        after = lax.ppermute(out["low"], "inner", down_pairs)
        earlier = (packed,) if k == 1 else ()
        near = near_field(near_index, near_mask, near_blocks, out["coarse"], *earlier)
        done = near
        if k == STEPS:
            krylov = done = vectors(state, zs, list(range(STEPS - 1)), near, CHUNKS)[0]
        summed = gather_sum(recv, slots * rank, done)
        local_far, blocks, (near,) = far_field(listed, recv, packed, near_blocks, (near,), summed)

        def between(column):
            held = (basis, turned, transfer, lifting, top) + (tuple(zs) if k == STEPS else ())
            return halo_part(listed, near_index, blocks, before, after, near, held, column)

        column, other, (near, *held) = over_branches(summed, outer, local_far, between)
        if k < STEPS:
            held = held + zs
        later = [column, other, state, local_far, near, *held]
        out = stage(k, points, wanted, branch, zs[0], basis, transfer, later)
        state = out["state"]
        zs = zs + [out["z"]]
    low = 4 if inner % 4 == 0 else inner
    held = held[-STEPS:] + [out["z"]]
    krylov = vectors(state, held, [STEPS - 1], krylov, CHUNKS)[0]
    summed = sum_over(out["send"], "inner", 1, low, krylov, AFTER)
    summed = sum_over(summed, "inner", low, inner // low, summed, AFTER_VMEM)
    column, other, _ = over_branches(summed, outer, summed, lambda column: None)
    products = [branch, column, other]
    krylov, hessenberg = vectors(state, held, [STEPS], krylov, CHUNKS, products, points)
    return krylov.reshape(STEPS + 1, *rhs.shape), hessenberg


def solution(mesh):
    return jax.shard_map(
        shards,
        mesh=mesh,
        in_specs=(
            P(("outer", "inner"), None),
            P(("outer", "inner"), None, None, None),
            P(("outer", "inner"), None),
            P(("outer", "inner"), None),
            P(("outer", "inner"), None, None),
            P(("outer", "inner"), None, None, None),
            P(("outer", "inner"), None),
            P(("outer", "inner"), None),
            P(("outer", "inner"), None, None),
            P(("outer", "inner"), None, None),
            P("outer", None, None, None),
        ),
        out_specs=(P(None, ("outer", "inner"), None), P()),
        check_vma=False,
    )
```

```python
import functools

import jax
import jax.numpy as jnp
from jax import lax
from jax.experimental import pallas as pl
from jax.experimental.pallas import tpu as pltpu
from jax.sharding import PartitionSpec as P

HW = 2
STEPS = 4
EPS = 1e-06
PIECES = 3
DOT_ROWS = 16
STATE_ROWS = 64
VMEM_BYTES = 32 * 1024 * 1024
BF16 = jnp.bfloat16
F32 = jnp.float32


def dot(a, b):
    return jnp.dot(a, b, preferred_element_type=F32)


def dot_first(a, b):
    return lax.dot_general(a, b, (((0,), (0,)), ((), ())), preferred_element_type=F32)


def store_split(ref, values, count):
    rest = values
    ref[...] = jnp.zeros(ref.shape, F32)
    for piece in range(PIECES):
        part = rest.astype(BF16).astype(F32)
        ref[piece * 5 : piece * 5 + count, :] = part[:count]
        rest = rest - part


def joined(rows):
    return [rows[i : i + 1] + rows[5 + i : 6 + i] + rows[10 + i : 11 + i] for i in range(5)]


def entry_row(i, l):
    low, high = min(i, l), max(i, l)
    return 20 + high * (high + 1) // 2 + low


def basis_row(i, l):
    return 32 + i * (i + 1) // 2 + l


def coefficients(m, grams, state_in, state_out):
    last = m - 1
    entry = lambda i, l: state_in[entry_row(i, l) : entry_row(i, l) + 1, :]
    expand = lambda i, l: state_in[basis_row(i, l) : basis_row(i, l) + 1, :]

    def put(row, value):
        state_out[row : row + 1, :] = value

    dots = []
    for i in range(m):
        dots.append(sum(expand(i, l) * grams[l] for l in range(i + 1)))
    weights = [dots[i] + entry(i, last) for i in range(m)]
    spread = [sum(weights[l] * entry(i, l) for l in range(m)) for i in range(m)]
    square = grams[m]
    for i in range(m):
        square = square + weights[i] * (weights[i] + spread[i] - 2.0 * dots[i])
    total = jnp.maximum(square, 0.0) + EPS
    root = jnp.sqrt(total)
    inverse = 1.0 / root
    for l in range(m):
        value = sum(weights[i] * expand(i, l) for i in range(l, m))
        put(basis_row(m, l), -inverse * value)
    put(basis_row(m, m), inverse)
    for i in range(m):
        put(i * STEPS + last, weights[i] + (1.0 if i == last else 0.0))
    if m > 0:
        put(m * STEPS + last, root)
    if m < STEPS:
        for i in range(m):
            put(entry_row(i, m), (-entry(i, last) - spread[i]) * inverse)
        put(entry_row(m, m), -EPS / total)
    return weights, inverse


def from_branches(ups_ref, rank):
    rows = ups_ref[0, rank:].astype(F32)
    for c in range(1, ups_ref.shape[0]):
        rows = rows + ups_ref[c, rank:].astype(F32)
    return joined(rows)


SMEM = pl.BlockSpec(memory_space=pltpu.SMEM)
VMEM = pl.BlockSpec(memory_space=pltpu.VMEM)
HBM = pl.BlockSpec(memory_space=pl.ANY)
AFTER = pl.BlockSpec(memory_space=pl.ANY)
AFTER_VMEM = pl.BlockSpec(memory_space=pl.ANY)
LOOSE = pl.BlockSpec(memory_space=pl.ANY)
FREE = pl.BlockSpec(memory_space=pltpu.VMEM)
AHEAD = 3
CHUNKS = 4
PIN = True


def call(kernel, args, in_specs, outs, scratch, name, flops, moved, aliases={}):
    def pinned(array, spec):
        if not PIN or not any(spec is one for one in (VMEM, HBM, SMEM, AFTER, AFTER_VMEM)):
            return array
        in_vmem = spec is VMEM or spec is AFTER_VMEM
        return pltpu.with_memory_space_constraint(array, pltpu.VMEM if in_vmem else pltpu.HBM)

    def shape_of(shape, dtype, spec):
        if not PIN or not (spec is VMEM or spec is HBM):
            return jax.ShapeDtypeStruct(shape, dtype)
        return (pltpu.VMEM if spec is VMEM else pltpu.HBM)(shape, dtype)

    return pl.pallas_call(
        kernel,
        in_specs=list(in_specs),
        out_specs=[spec for _, _, spec in outs],
        out_shape=[shape_of(*out) for out in outs],
        scratch_shapes=scratch,
        input_output_aliases=aliases,
        compiler_params=pltpu.CompilerParams(vmem_limit_bytes=VMEM_BYTES),
        cost_estimate=pl.CostEstimate(flops=flops, bytes_accessed=moved, transcendentals=0),
        name=name,
    )(*[pinned(array, spec) for array, spec in zip(args, in_specs)])


def semaphores(*shape):
    return pltpu.SemaphoreType.DMA(shape)


def windowed(count, ahead, fetch, work):
    def start(i):
        for j, copy in enumerate(fetch(i)):
            copy.start(priority=j % 2)

    def body(i, carry):
        @pl.when(i + ahead < count)
        def _():
            start(i + ahead)

        for copy in fetch(i):
            copy.wait()
        work(i)
        return carry

    def begin():
        for i in range(min(ahead, count)):
            start(i)

    return begin, lambda: lax.fori_loop(0, count, body, 0)


def slab(i, size):
    return pl.ds(pl.multiple_of(i * size, size), size)


def pack_kernel(branch, mask_ref, slot_ref, index_ref, near_mask_ref, far_ref, *refs):
    basis_ref, transfer_ref, top_ref, near_ref = refs[:4]
    out_ref, count_ref, list_ref, basis_out, transfer_out, top_out, listed_ref = refs[4:11]
    blocks, total, packed, basis, transfer, top, turned, lifting, row, chosen = refs[11:21]
    arrived, left, came, moved, given = refs[21:]
    leaves, entries, rank, _ = blocks.shape
    sources, _, width = packed.shape
    slots = width // rank
    near_entries = index_ref.shape[1]

    def fetch(leaf):
        return [pltpu.make_async_copy(far_ref.at[leaf], blocks.at[leaf], arrived.at[leaf])]

    def store(leaf):
        rows = slab(leaf, rank)
        return pltpu.make_async_copy(packed.at[:, rows], out_ref.at[:, rows], left.at[leaf])

    def work(leaf):
        total[...] = jnp.zeros(total.shape, F32)
        for f in range(entries):
            weight = mask_ref[leaf, f].astype(F32)
            total[slot_ref[leaf, f]] += blocks[leaf, f].astype(F32) * weight
        rows = slab(leaf, rank)
        for source in range(sources):
            sides = [total[source * slots + s] for s in range(slots)]
            packed[source, rows] = jnp.concatenate(sides, axis=1).astype(BF16)
        store(leaf).start()

    piece = chosen.shape[0] // given.shape[0]

    def move(leaf, n, i):
        return pltpu.make_async_copy(near_ref.at[leaf, n], chosen.at[i], moved.at[i])

    def moved_one(i, carry):
        entry = list_ref[i]
        move(entry // near_entries, entry % near_entries, i).wait()
        return carry

    def give(i):
        some = slab(i, piece)
        return pltpu.make_async_copy(chosen.at[some], listed_ref.at[some], given.at[i])

    def start_give(i, carry):
        give(i).start()
        return carry

    def end_give(i, carry):
        give(i).wait()
        return carry

    def list_one(i, count):
        leaf, n = i // near_entries, i % near_entries
        place = index_ref[leaf, n]
        hit = (near_mask_ref[leaf, n] != 0) & ((place < HW) | (place >= HW + leaves))
        list_ref[i] = 0

        @pl.when(hit)
        def _():
            list_ref[count] = i
            move(leaf, n, count).start()

        return count + hit.astype(jnp.int32)

    small = [
        pltpu.make_async_copy(basis_ref, basis, came.at[0]),
        pltpu.make_async_copy(transfer_ref, transfer, came.at[1]),
        pltpu.make_async_copy(top_ref, top, came.at[2]),
    ]
    for copy in small:
        copy.start()
    begin, run = windowed(leaves, leaves, fetch, work)
    begin()
    count = lax.fori_loop(0, list_ref.shape[0], list_one, 0)
    count_ref[0] = count
    for copy in small:
        copy.wait()
    turn = lambda a: a.astype(F32).T.astype(BF16)
    for leaf in range(leaves):
        turned[leaf] = turn(basis[leaf])
    for pair in range(leaves // 2):
        columns = slice(pair * 2 * rank, (pair + 1) * 2 * rank)
        sides = [turn(transfer[2 * pair + j]) for j in range(2)]
        lifting[:, columns] = jnp.concatenate(sides, axis=1)
    for pair in range(top.shape[1] // 2):
        columns = slice(pair * 2 * rank, (pair + 1) * 2 * rank)
        sides = []
        for c in (2 * pair, 2 * pair + 1):
            sides.append(top[0, c] * (branch[0] != c).astype(F32).astype(BF16))
        row[:, columns] = jnp.concatenate(sides, axis=1)
    results = [
        pltpu.make_async_copy(turned, basis_out, came.at[0]),
        pltpu.make_async_copy(lifting, transfer_out, came.at[1]),
        pltpu.make_async_copy(row, top_out, came.at[2]),
    ]
    for copy in results:
        copy.start()
    lax.fori_loop(0, count, moved_one, 0)
    pieces = (count + piece - 1) // piece
    lax.fori_loop(0, pieces, start_give, 0)
    run()
    for leaf in range(leaves):
        store(leaf).wait()
    for copy in results:
        copy.wait()
    lax.fori_loop(0, pieces, end_give, 0)


def pack(branch, basis, transfer, top_blocks, near_blocks, far_blocks, far_mask, far_slot, near_index, near_mask, inner, slots):
    leaves, entries, rank, _ = far_blocks.shape
    shape = (inner, leaves * rank, slots * rank)
    turned = (leaves, basis.shape[2], rank)
    lifting = (rank, leaves * rank)
    row = (rank, top_blocks.shape[1] * rank)
    listed = (near_index.size,) + near_blocks.shape[2:]
    return call(
        pack_kernel,
        (branch, far_mask, far_slot, near_index, near_mask, far_blocks, basis, transfer, top_blocks,
         near_blocks),
        (SMEM,) * 5 + (HBM,) * 5,
        [
            (shape, BF16, HBM),
            ((1,), jnp.int32, SMEM),
            ((near_index.size,), jnp.int32, SMEM),
            (turned, BF16, HBM),
            (lifting, BF16, HBM),
            (row, BF16, HBM),
            (listed, BF16, HBM),
        ],
        [
            pltpu.VMEM(far_blocks.shape, BF16),
            pltpu.VMEM((inner * slots, rank, rank), F32),
            pltpu.VMEM(shape, BF16),
            pltpu.VMEM(basis.shape, BF16),
            pltpu.VMEM(transfer.shape, BF16),
            pltpu.VMEM(top_blocks.shape, BF16),
            pltpu.VMEM(turned, BF16),
            pltpu.VMEM(lifting, BF16),
            pltpu.VMEM(row, BF16),
            pltpu.VMEM(listed, BF16),
            semaphores(leaves),
            semaphores(leaves),
            semaphores(3),
            semaphores(near_index.size),
            semaphores(near_index.size // 8),
        ],
        "pack",
        0,
        10 << 20,
    )


def near_kernel(index_ref, mask_ref, blocks_ref, own_ref, *refs):
    out_ref, blocks, own, result, arrived, came, left = refs[-7:]
    leaves, entries, size, _ = blocks.shape
    pair = leaves // CHUNKS

    def fetch(leaf):
        return [pltpu.make_async_copy(blocks_ref.at[leaf], blocks.at[leaf], arrived.at[leaf])]

    def store(i):
        some = slab(i, pair)
        return pltpu.make_async_copy(result.at[some], out_ref.at[some], left.at[i])

    def work(leaf):
        total = None
        for n in range(entries):
            place = index_ref[leaf, n] - HW
            inside = (place >= 0) & (place < leaves)
            weight = jnp.where(inside, mask_ref[leaf, n], 0).astype(F32).astype(BF16)
            values = own[jnp.clip(place, 0, leaves - 1)] * weight
            term = dot(blocks[leaf, n], values)
            total = term if total is None else total + term
        result[leaf] = total

        @pl.when(leaf % pair == pair - 1)
        def _():
            store(leaf // pair).start()

    begin, run = windowed(leaves, AHEAD, fetch, work)
    copy = pltpu.make_async_copy(own_ref, own, came)
    copy.start()
    begin()
    copy.wait()
    run()
    for i in range(CHUNKS):
        store(i).wait()


def near_field(near_index, near_mask, near_blocks, own, *earlier):
    leaves, _, size, _ = near_blocks.shape
    columns = own.shape[2]
    return call(
        near_kernel,
        (near_index, near_mask, near_blocks, own) + earlier,
        (SMEM, SMEM, HBM, HBM) + (AFTER,) * len(earlier),
        [((leaves, size, columns), F32, HBM)],
        [
            pltpu.VMEM(near_blocks.shape, BF16),
            pltpu.VMEM(own.shape, BF16),
            pltpu.VMEM((leaves, size, columns), F32),
            semaphores(leaves),
            semaphores(),
            semaphores(leaves),
        ],
        "near_field",
        2 * near_blocks.size * columns,
        2 * near_blocks.size,
    )[0]


def gather_sum_kernel(recv, *refs, lead):
    out_ref, split = refs[-2:]
    rank = out_ref.shape[0] - DOT_ROWS
    total = recv[0, lead:].astype(F32)
    for i in range(1, recv.shape[0]):
        total = total + recv[i, lead:].astype(F32)
    store_split(split, jnp.concatenate(joined(total[rank:]), axis=0), 5)
    if rank > 0:
        out_ref[:rank] = total[:rank].astype(BF16)
    out_ref[rank:] = split[...].astype(BF16)


def gather_sum(recv, lead, earlier):
    _, rows, columns = recv.shape
    return call(
        functools.partial(gather_sum_kernel, lead=lead),
        (recv, earlier),
        (VMEM, AFTER),
        [((rows - lead, columns), BF16, VMEM)],
        [pltpu.VMEM((DOT_ROWS, columns), F32)],
        "gather_sum",
        1 << 20,
        1 << 19,
    )[0]


def stack_kernel(*refs):
    for i, ref in enumerate(refs[:-2]):
        refs[-1][i] = ref[...]


def over_branches(summed, outer, earlier, between):
    shifts = [[(o, (o + 2 * j) % outer) for o in range(outer)] for j in range(1, outer // 2)]
    parts = [summed] + [lax.ppermute(summed, "outer", shift) for shift in shifts]
    column = call(
        stack_kernel,
        parts + [earlier],
        [VMEM] * len(parts) + [AFTER_VMEM],
        [((len(parts),) + summed.shape, BF16, VMEM)],
        [],
        "stack",
        0,
        1 << 18,
    )[0]
    other = lax.ppermute(column, "outer", [(o, o ^ 1) for o in range(outer)])
    return column, other, between(column)


def in_order(branch, column, other, ups):
    count = ups.shape[0]
    for j in range(count // 2):
        ups[lax.rem(branch[0] + count - 2 * j, count)] = column[j]
        mate = branch[0] + 1 - 2 * lax.rem(branch[0], 2)
        ups[lax.rem(mate + count - 2 * j, count)] = other[j]


def far_kernel(count_ref, recv, packed_ref, blocks_ref, *refs):
    held = (len(refs) - 7) // 2
    sources, (_, far, blocks), targets = refs[:held], refs[held : held + 3], refs[held + 3 : -4]
    packed, arrived, fetched, loaded = refs[-4:]
    share = packed.shape[0] // CHUNKS
    width = packed.shape[2]
    piece = blocks.shape[0] // fetched.shape[0]
    count = (count_ref[0] + piece - 1) // piece

    def fetch(i):
        some = slab(i, share)
        return [pltpu.make_async_copy(packed_ref.at[some], packed.at[some], arrived.at[i])]

    def block(i):
        some = slab(i, piece)
        return pltpu.make_async_copy(blocks_ref.at[some], blocks.at[some], fetched.at[i])

    def ask(i, carry):
        block(i).start()
        return carry

    def have(i, carry):
        block(i).wait()
        return carry

    def work(i):
        term = None
        for j in range(share):
            source = i * share + j
            one = dot(packed[source], recv[source, :width])
            term = one if term is None else term + one

        @pl.when(i == 0)
        def _():
            far[...] = term

        @pl.when(i > 0)
        def _():
            far[...] += term

    loads = [
        pltpu.make_async_copy(source, target, loaded.at[i])
        for i, (source, target) in enumerate(zip(sources, targets))
    ]
    begin, run = windowed(CHUNKS, CHUNKS, fetch, work)
    begin()
    lax.fori_loop(0, count, ask, 0)
    for copy in loads:
        copy.start()
    run()
    lax.fori_loop(0, count, have, 0)
    for copy in loads:
        copy.wait()


def far_field(count, recv, packed, blocks, held, earlier):
    sources, rows, _ = packed.shape
    outs = [((rows, recv.shape[2]), F32, VMEM), (blocks.shape, BF16, VMEM)]
    far, blocks, *held = call(
        far_kernel,
        (count, recv, packed, blocks, *held, earlier),
        (SMEM, VMEM, HBM, HBM) + (HBM,) * len(held) + (AFTER_VMEM,),
        outs + [(a.shape, a.dtype, VMEM) for a in held],
        [
            pltpu.VMEM(packed.shape, BF16),
            semaphores(CHUNKS),
            semaphores(blocks.shape[0] // 8),
            semaphores(len(held)),
        ],
        "far_field",
        2 * packed.size * recv.shape[2],
        2 * packed.size,
    )
    return far, blocks, held


def halo_kernel(count_ref, list_ref, index_ref, blocks, before, after, near_in, *refs):
    held = (len(refs) - 4) // 2
    sources, near, targets = refs[:held], refs[held + 1], refs[held + 2 : -2]
    halo, loaded = refs[-2:]
    loads = [
        pltpu.make_async_copy(source, target, loaded.at[i])
        for i, (source, target) in enumerate(zip(sources, targets))
    ]
    for copy in loads:
        copy.start()
    leaves, reach, entries = near.shape[0], before.shape[0], index_ref.shape[1]
    halo[:reach] = before[...]
    halo[reach:] = after[...]
    count = count_ref[0]
    at_once = 8

    def add(group, carry):
        terms = []
        for j in range(at_once):
            i = jnp.minimum(group * at_once + j, count - 1)
            weight = (group * at_once + j < count).astype(F32).astype(BF16)
            entry = list_ref[i]
            leaf = entry // entries
            place = index_ref[leaf, entry % entries]
            values = halo[jnp.where(place < reach, place, place - leaves)] * weight
            terms.append((leaf, dot(blocks[i], values)))
        for leaf, term in terms:
            near[leaf] += term
        return carry

    lax.fori_loop(0, (count + at_once - 1) // at_once, add, 0)
    for copy in loads:
        copy.wait()


def halo_part(listed, near_index, blocks, before, after, near, held, earlier):
    return call(
        halo_kernel,
        (*listed, near_index, blocks, before, after, near, *held, earlier),
        (SMEM, SMEM, SMEM, VMEM, VMEM, VMEM, VMEM) + (HBM,) * len(held) + (AFTER_VMEM,),
        [(a.shape, a.dtype, VMEM) for a in (near, *held)],
        [pltpu.VMEM((2 * before.shape[0],) + before.shape[1:], BF16), semaphores(len(held))],
        "halo_part",
        1 << 28,
        2 << 20,
        {6: 0},
    )


def sum_kernel(*refs, axis, stride):
    *parts, _, out, rows, split = refs
    count = len(parts)
    place = lax.rem(lax.axis_index(axis).astype(jnp.int32) // stride, count)
    for j, part in enumerate(parts):
        rows[lax.rem(place + count - j, count)] = part[...].astype(F32)
    total = rows[0]
    for i in range(1, count):
        total = total + rows[i]
    store_split(split, jnp.concatenate(joined(total), axis=0), 5)
    out[...] = split[...].astype(BF16)


def sum_over(dots, axis, stride, count, earlier, after):
    if count == 1:
        return dots
    size = lax.axis_size(axis)

    def moved(i, j):
        at = i // stride % count
        return i + ((at + j) % count - at) * stride

    parts = [dots]
    for j in range(1, count):
        parts.append(lax.ppermute(dots, axis, [(i, moved(i, j)) for i in range(size)]))
    return call(
        functools.partial(sum_kernel, axis=axis, stride=stride),
        (*parts, earlier),
        (VMEM,) * count + (after,),
        [(dots.shape, BF16, VMEM)],
        [pltpu.VMEM((count,) + dots.shape, F32), pltpu.VMEM((DOT_ROWS, dots.shape[1]), F32)],
        "sum_over",
        0,
        1 << 18,
    )[0]


def stage_kernel(*refs, k, points):
    refs = list(refs)
    take = lambda count: [refs.pop(0) for _ in range(count)]
    m = k - 1
    first, sends = k == 0, k < STEPS
    send_slot, branch = take(2)
    if first:
        z_any, basis_any, transfer_any = take(3)
    else:
        column, other, state, far, near, basis, turned, transfer, lifting, top = take(10)
        zs = take(k)
        (z_any,) = take(1)
    state_out, send = take(2)
    if sends:
        coarse_any, low, high = take(3)
    sums, split, arrived, left = take(4)
    if sends:
        coarse, skeletons = take(2)
    if first:
        basis, transfer, vectors, came = take(4)
    else:
        ups, result, coef, combined = take(4)

    leaves, rank, size = basis.shape
    group = leaves // CHUNKS

    def fetch(i):
        if not first:
            return []
        some = slab(i, group)
        return [pltpu.make_async_copy(z_any.at[some], vectors.at[some], arrived.at[i])]

    pieces = 2

    def stores(i):
        some = slab(i, leaves // pieces)
        pairs = []
        if not first and sends:
            pairs.append((result.at[some], z_any.at[some]))
        if sends:
            pairs.append((coarse.at[some], coarse_any.at[some]))
        return [
            pltpu.make_async_copy(source, target, left.at[n, i])
            for n, (source, target) in enumerate(pairs)
        ]

    def work(i):
        for j in range(group):
            leaf = i * group + j
            if first:
                others = []
                z = vectors[leaf]
            else:
                others = [ref[leaf] for ref in zs]
                z = near[leaf] + dot(turned[leaf], combined[slab(leaf, rank)])
                for l in range(m):
                    z = z - coef[l : l + 1, :] * others[l + 1]
                z = z * coef[STEPS : STEPS + 1, :]
                if sends:
                    result[leaf] = z
                else:
                    z_any[leaf] = z
            if sends:
                rounded = z.astype(BF16)
                coarse[leaf] = rounded
                skeletons[slab(leaf, rank)] = dot(basis[leaf], rounded).astype(BF16)
            for l, vector in enumerate(others + [z]):
                sums[l] += jnp.sum((z * vector).reshape(size // 8, 8, z.shape[1]), axis=0)
        share = CHUNKS // pieces

        @pl.when(i % share == share - 1)
        def _():
            for copy in stores(i // share):
                copy.start()

    begin, run = windowed(CHUNKS, CHUNKS, fetch, work)
    if first:
        small = [
            pltpu.make_async_copy(basis_any, basis, came.at[0]),
            pltpu.make_async_copy(transfer_any, transfer, came.at[1]),
        ]
        for copy in small:
            copy.start()
    begin()
    sums[...] = jnp.zeros(sums.shape, F32)
    if first:
        state_out[...] = jnp.zeros(state_out.shape, F32)
        for copy in small:
            copy.wait()
    else:
        in_order(branch, column, other, ups)
        count, columns = ups.shape[0], ups.shape[2]
        incoming = dot(top[...], ups[:, :rank].reshape(count * rank, columns)).astype(BF16)
        down = dot(transfer[...].reshape(leaves * rank, rank), incoming)
        combined[...] = (far[...] + down).astype(BF16)
        grams = [row / points for row in from_branches(ups, rank)]
        state_out[...] = state[...]
        weights, inverse = coefficients(m, grams, state, state_out)
        for i, weight in enumerate(weights):
            coef[i : i + 1, :] = weight
        coef[STEPS : STEPS + 1, :] = inverse
    run()

    if sends:
        low[...] = coarse[:HW]
        high[...] = coarse[leaves - HW :]
        if first:
            lifted = dot_first(transfer[...].reshape(leaves * rank, rank), skeletons[...])
        else:
            lifted = dot(lifting[...], skeletons[...])
        lifted = lifted.astype(BF16)
    products = [jnp.sum(sums[i], axis=0, keepdims=True) for i in range(k + 1)]
    products = jnp.concatenate(products + [jnp.zeros_like(products[0])] * (7 - k), axis=0)
    store_split(split, products, k + 1)
    dots = split[...].astype(BF16)
    if sends:
        slots, inner = send_slot.shape
        for r in range(inner):
            for s in range(slots):
                send[r, s * rank : (s + 1) * rank] = skeletons[slab(send_slot[s, r], rank)]
            send[r, slots * rank : (slots + 1) * rank] = lifted
            send[r, (slots + 1) * rank :] = dots
    else:
        send[...] = dots
    for i in range(pieces):
        for copy in stores(i):
            copy.wait()


def stage(k, points, send_slot, branch, rhs, basis, transfer, later):
    leaves, rank, size = basis.shape
    first, sends = k == 0, k < STEPS
    tall = rhs.shape
    columns = tall[2]
    slots, inner = send_slot.shape
    names, outs = [], []

    def get(name, shape, dtype, spec):
        names.append(name)
        outs.append((shape, dtype, spec))

    args, specs = [send_slot, branch], [SMEM, SMEM]
    if first:
        args += [rhs, basis, transfer]
        specs += [HBM] * 3
    else:
        args += later
        specs += [VMEM] * len(later)
        get("z", tall, F32, HBM if sends else VMEM)
    get("state", (STATE_ROWS, columns), F32, VMEM)
    rows = (slots + 1) * rank + DOT_ROWS
    get("send", (inner, rows, columns) if sends else (DOT_ROWS, columns), BF16, VMEM)
    if sends:
        get("coarse", tall, BF16, HBM)
        get("low", (HW, size, columns), BF16, VMEM)
        get("high", (HW, size, columns), BF16, VMEM)

    scratch = [
        pltpu.VMEM((STEPS + 1, 8, columns), F32),
        pltpu.VMEM((DOT_ROWS, columns), F32),
        semaphores(CHUNKS),
        semaphores(2, CHUNKS),
    ]
    if sends:
        scratch += [
            pltpu.VMEM(tall, BF16),
            pltpu.VMEM((leaves * rank, columns), BF16),
        ]
    if first:
        scratch += [
            pltpu.VMEM(basis.shape, BF16),
            pltpu.VMEM(transfer.shape, BF16),
            pltpu.VMEM(tall, F32),
            semaphores(2),
        ]
    else:
        column = later[0].shape
        scratch += [
            pltpu.VMEM((2 * column[0],) + column[1:], BF16),
            pltpu.VMEM(tall, F32),
            pltpu.VMEM((8, columns), F32),
            pltpu.VMEM((leaves * rank, columns), BF16),
        ]
    results = call(
        functools.partial(stage_kernel, k=k, points=points),
        args,
        specs,
        outs,
        scratch,
        f"stage{k}",
        1 << 27,
        (k + 4) << 20,
    )
    return dict(zip(names, results))


def vectors_kernel(*refs, wanted, held, final, points):
    refs = list(refs)
    take = lambda count: [refs.pop(0) for _ in range(count)]
    (state,) = take(1)
    if final:
        branch, column, other = take(3)
    zs = take(wanted[-1] + 1)
    _, krylov = take(2)
    if final:
        (hess_out,) = take(1)
    result, left = take(2)
    if final:
        after, ups = take(2)
    else:
        after = state
    if not held:
        vectors, arrived = take(2)
    parts = left.shape[1]
    group = zs[0].shape[0] // parts

    def fetch(i):
        if held:
            return []
        some = slab(i, group)
        return [
            pltpu.make_async_copy(z.at[some], vectors.at[l, some], arrived.at[l, i])
            for l, z in enumerate(zs)
        ]

    def store(n, i):
        some = slab(i, group)
        return pltpu.make_async_copy(result.at[n, some], krylov.at[wanted[n], some], left.at[n, i])

    def work(i):
        for j in range(group):
            leaf = i * group + j
            for n, which in enumerate(wanted):
                vector = None
                for l in range(which + 1):
                    row = basis_row(which, l)
                    values = zs[l][leaf] if held else vectors[l, leaf]
                    term = after[row : row + 1, :] * values
                    vector = term if vector is None else vector + term
                result[n, leaf] = vector
        for n in range(len(wanted)):
            store(n, i).start()

    begin, run = windowed(parts, parts, fetch, work)
    begin()
    if final:
        in_order(branch, column, other, ups)
        grams = [row / points for row in from_branches(ups, 0)]
        after[...] = state[...]
        coefficients(STEPS, grams, state, after)
    run()
    if final:
        for i in range(STEPS + 1):
            for j in range(STEPS):
                row = i * STEPS + j
                if i <= j + 1:
                    hess_out[i, j : j + 1, :] = after[row : row + 1, :]
                else:
                    hess_out[i, j : j + 1, :] = jnp.zeros((1, hess_out.shape[2]), F32)
    for n in range(len(wanted)):
        for i in range(parts):
            store(n, i).wait()


def vectors(state, zs, wanted, before, parts, products=None, points=0):
    final = products is not None
    held = wanted[0] > 0
    tall = zs[0].shape
    count = wanted[-1] + 1
    shape = (STEPS + 1,) + tall
    scratch = [pltpu.VMEM((len(wanted),) + tall, F32), semaphores(len(wanted), parts)]
    outs = [(shape, F32, HBM)]
    args, specs = [state], [VMEM]
    if final:
        args += products
        specs += [SMEM, VMEM, VMEM]
        column = products[1].shape
        outs.append(((STEPS + 1, STEPS, tall[2]), F32, FREE))
        scratch += [
            pltpu.VMEM(state.shape, F32),
            pltpu.VMEM((2 * column[0],) + column[1:], BF16),
        ]
    args += zs[:count]
    specs += [VMEM if held else HBM] * count
    args.append(before)
    specs.append(HBM if held else AFTER)
    if not held:
        scratch += [pltpu.VMEM((count,) + tall, F32), semaphores(count, parts)]
    return call(
        functools.partial(
            vectors_kernel, wanted=wanted, held=held, final=final, points=points
        ),
        args,
        specs,
        outs,
        scratch,
        "last_vector" if final else "vectors",
        1 << 23,
        len(wanted) << 21,
        {len(args) - 1: 0} if held else {},
    )


def shards(
    rhs,
    near_blocks,
    near_index,
    near_mask,
    basis,
    far_blocks,
    far_slot,
    far_mask,
    send_slot,
    transfer,
    top_blocks,
):
    outer, inner = lax.axis_size("outer"), lax.axis_size("inner")
    points = outer * inner * rhs.shape[0]
    leaves, rank = basis.shape[:2]
    slots = send_slot.shape[2]
    branch = lax.axis_index("outer").astype(jnp.int32).reshape(1)
    up_pairs = [(i, i + 1) for i in range(inner - 1)]
    down_pairs = [(j, i) for i, j in up_pairs]
    wanted = send_slot[0].T

    def exchange(array, axis):
        return lax.all_to_all(array, axis, split_axis=0, concat_axis=0, tiled=True)

    zs = [rhs.reshape(leaves, -1, rhs.shape[1])]
    out = stage(0, points, wanted, branch, zs[0], basis, transfer, None)
    packed, count, entries, turned, lifting, top, listed_blocks = pack(
        branch, basis, transfer, top_blocks, near_blocks, far_blocks, far_mask, far_slot, near_index, near_mask,
        inner, slots,
    )
    listed = (count, entries)
    state = out["state"]
    for k in range(1, STEPS + 1):
        recv = exchange(out["send"], "inner")
        before = lax.ppermute(out["high"], "inner", up_pairs)
        after = lax.ppermute(out["low"], "inner", down_pairs)
        earlier = (packed,) if k == 1 else ()
        near = near_field(near_index, near_mask, near_blocks, out["coarse"], *earlier)
        done = near
        if k == STEPS:
            krylov = done = vectors(state, zs, list(range(STEPS - 1)), near, CHUNKS)[0]
        summed = gather_sum(recv, slots * rank, done)
        local_far, blocks, (near,) = far_field(
            count, recv, packed, listed_blocks, (near,), summed
        )

        def between(column):
            held = (basis, turned, transfer, lifting, top, *zs)
            return halo_part(listed, near_index, blocks, before, after, near, held, column)

        column, other, (near, *held) = over_branches(summed, outer, local_far, between)
        later = [column, other, state, local_far, near, *held]
        out = stage(k, points, wanted, branch, zs[0], basis, transfer, later)
        state = out["state"]
        zs = zs + [out["z"]]
    low = 4 if inner % 4 == 0 else inner
    held = held[-STEPS:] + [out["z"]]
    krylov = vectors(state, held, [STEPS - 1], krylov, 2)[0]
    summed = sum_over(out["send"], "inner", 1, low, krylov, AFTER)
    summed = sum_over(summed, "inner", low, inner // low, summed, AFTER_VMEM)
    column, other, _ = over_branches(summed, outer, summed, lambda column: None)
    products = [branch, column, other]
    krylov, hessenberg = vectors(state, held, [STEPS], krylov, 2, products, points)
    return krylov.reshape(STEPS + 1, *rhs.shape), hessenberg


def solution(mesh):
    return jax.shard_map(
        shards,
        mesh=mesh,
        in_specs=(
            P(("outer", "inner"), None),
            P(("outer", "inner"), None, None, None),
            P(("outer", "inner"), None),
            P(("outer", "inner"), None),
            P(("outer", "inner"), None, None),
            P(("outer", "inner"), None, None, None),
            P(("outer", "inner"), None),
            P(("outer", "inner"), None),
            P(("outer", "inner"), None, None),
            P(("outer", "inner"), None, None),
            P("outer", None, None, None),
        ),
        out_specs=(P(None, ("outer", "inner"), None), P()),
        check_vma=False,
    )
```

```python
import functools

import jax
import jax.numpy as jnp
from jax import lax
from jax.experimental import pallas as pl
from jax.experimental.pallas import tpu as pltpu
from jax.sharding import PartitionSpec as P

HW = 2
STEPS = 4
EPS = 1e-06
PIECES = 3
DOT_ROWS = 16
STATE_ROWS = 64
VMEM_BYTES = 32 * 1024 * 1024
BF16 = jnp.bfloat16
F32 = jnp.float32


def dot(a, b):
    return jnp.dot(a, b, preferred_element_type=F32)


def dot_first(a, b):
    return lax.dot_general(a, b, (((0,), (0,)), ((), ())), preferred_element_type=F32)


def store_split(ref, values, count):
    rest = values
    ref[...] = jnp.zeros(ref.shape, F32)
    for piece in range(PIECES):
        part = rest.astype(BF16).astype(F32)
        ref[piece * 5 : piece * 5 + count, :] = part[:count]
        rest = rest - part


def joined(rows):
    return [rows[i : i + 1] + rows[5 + i : 6 + i] + rows[10 + i : 11 + i] for i in range(5)]


def entry_row(i, l):
    low, high = min(i, l), max(i, l)
    return 20 + high * (high + 1) // 2 + low


def basis_row(i, l):
    return 32 + i * (i + 1) // 2 + l


def coefficients(m, grams, state_in, state_out):
    last = m - 1
    entry = lambda i, l: state_in[entry_row(i, l) : entry_row(i, l) + 1, :]
    expand = lambda i, l: state_in[basis_row(i, l) : basis_row(i, l) + 1, :]

    def put(row, value):
        state_out[row : row + 1, :] = value

    dots = []
    for i in range(m):
        dots.append(sum(expand(i, l) * grams[l] for l in range(i + 1)))
    weights = [dots[i] + entry(i, last) for i in range(m)]
    spread = [sum(weights[l] * entry(i, l) for l in range(m)) for i in range(m)]
    square = grams[m]
    for i in range(m):
        square = square + weights[i] * (weights[i] + spread[i] - 2.0 * dots[i])
    total = jnp.maximum(square, 0.0) + EPS
    root = jnp.sqrt(total)
    inverse = 1.0 / root
    for l in range(m):
        value = sum(weights[i] * expand(i, l) for i in range(l, m))
        put(basis_row(m, l), -inverse * value)
    put(basis_row(m, m), inverse)
    for i in range(m):
        put(i * STEPS + last, weights[i] + (1.0 if i == last else 0.0))
    if m > 0:
        put(m * STEPS + last, root)
    if m < STEPS:
        for i in range(m):
            put(entry_row(i, m), (-entry(i, last) - spread[i]) * inverse)
        put(entry_row(m, m), -EPS / total)
    return weights, inverse


def from_branches(ups_ref, rank):
    rows = ups_ref[0, rank:].astype(F32)
    for c in range(1, ups_ref.shape[0]):
        rows = rows + ups_ref[c, rank:].astype(F32)
    return joined(rows)


SMEM = pl.BlockSpec(memory_space=pltpu.SMEM)
VMEM = pl.BlockSpec(memory_space=pltpu.VMEM)
HBM = pl.BlockSpec(memory_space=pl.ANY)
AFTER = pl.BlockSpec(memory_space=pl.ANY)
AFTER_VMEM = pl.BlockSpec(memory_space=pl.ANY)
LOOSE = pl.BlockSpec(memory_space=pl.ANY)
FREE = pl.BlockSpec(memory_space=pltpu.VMEM)
AHEAD = 3
CHUNKS = 4
PIN = True


def call(kernel, args, in_specs, outs, scratch, name, flops, moved, aliases={}):
    def pinned(array, spec):
        if not PIN or not any(spec is one for one in (VMEM, HBM, SMEM, AFTER, AFTER_VMEM)):
            return array
        in_vmem = spec is VMEM or spec is AFTER_VMEM
        return pltpu.with_memory_space_constraint(array, pltpu.VMEM if in_vmem else pltpu.HBM)

    def shape_of(shape, dtype, spec):
        if not PIN or not (spec is VMEM or spec is HBM):
            return jax.ShapeDtypeStruct(shape, dtype)
        return (pltpu.VMEM if spec is VMEM else pltpu.HBM)(shape, dtype)

    return pl.pallas_call(
        kernel,
        in_specs=list(in_specs),
        out_specs=[spec for _, _, spec in outs],
        out_shape=[shape_of(*out) for out in outs],
        scratch_shapes=scratch,
        input_output_aliases=aliases,
        compiler_params=pltpu.CompilerParams(vmem_limit_bytes=VMEM_BYTES),
        cost_estimate=pl.CostEstimate(flops=flops, bytes_accessed=moved, transcendentals=0),
        name=name,
    )(*[pinned(array, spec) for array, spec in zip(args, in_specs)])


def semaphores(*shape):
    return pltpu.SemaphoreType.DMA(shape)


def windowed(count, ahead, fetch, work):
    def start(i):
        for j, copy in enumerate(fetch(i)):
            copy.start(priority=j % 2)

    def body(i, carry):
        @pl.when(i + ahead < count)
        def _():
            start(i + ahead)

        for copy in fetch(i):
            copy.wait()
        work(i)
        return carry

    def begin():
        for i in range(min(ahead, count)):
            start(i)

    return begin, lambda: lax.fori_loop(0, count, body, 0)


def slab(i, size):
    return pl.ds(pl.multiple_of(i * size, size), size)


def pack_kernel(branch, mask_ref, slot_ref, index_ref, near_mask_ref, far_ref, *refs):
    basis_ref, transfer_ref, top_ref = refs[:3]
    out_ref, count_ref, list_ref, basis_out, transfer_out, top_out = refs[3:9]
    blocks, total, packed, basis, transfer, top, turned, lifting, row = refs[9:18]
    arrived, left, came = refs[18:]
    leaves, entries, rank, _ = blocks.shape
    sources, _, width = packed.shape
    slots = width // rank
    near_entries = index_ref.shape[1]

    def fetch(leaf):
        return [pltpu.make_async_copy(far_ref.at[leaf], blocks.at[leaf], arrived.at[leaf])]

    def store(leaf):
        rows = slab(leaf, rank)
        return pltpu.make_async_copy(packed.at[:, rows], out_ref.at[:, rows], left.at[leaf])

    def work(leaf):
        total[...] = jnp.zeros(total.shape, F32)
        for f in range(entries):
            weight = mask_ref[leaf, f].astype(F32)
            total[slot_ref[leaf, f]] += blocks[leaf, f].astype(F32) * weight
        rows = slab(leaf, rank)
        for source in range(sources):
            sides = [total[source * slots + s] for s in range(slots)]
            packed[source, rows] = jnp.concatenate(sides, axis=1).astype(BF16)
        store(leaf).start()

    def list_one(i, count):
        leaf, n = i // near_entries, i % near_entries
        place = index_ref[leaf, n]
        hit = (near_mask_ref[leaf, n] != 0) & ((place < HW) | (place >= HW + leaves))
        list_ref[i] = 0

        @pl.when(hit)
        def _():
            list_ref[count] = i

        return count + hit.astype(jnp.int32)

    small = [
        pltpu.make_async_copy(basis_ref, basis, came.at[0]),
        pltpu.make_async_copy(transfer_ref, transfer, came.at[1]),
        pltpu.make_async_copy(top_ref, top, came.at[2]),
    ]
    for copy in small:
        copy.start()
    begin, run = windowed(leaves, leaves, fetch, work)
    begin()
    count = lax.fori_loop(0, list_ref.shape[0], list_one, 0)
    count_ref[0] = count
    for copy in small:
        copy.wait()
    turn = lambda a: a.astype(F32).T.astype(BF16)
    for leaf in range(leaves):
        turned[leaf] = turn(basis[leaf])
    for pair in range(leaves // 2):
        columns = slice(pair * 2 * rank, (pair + 1) * 2 * rank)
        sides = [turn(transfer[2 * pair + j]) for j in range(2)]
        lifting[:, columns] = jnp.concatenate(sides, axis=1)
    for pair in range(top.shape[1] // 2):
        columns = slice(pair * 2 * rank, (pair + 1) * 2 * rank)
        sides = []
        for c in (2 * pair, 2 * pair + 1):
            sides.append(top[0, c] * (branch[0] != c).astype(F32).astype(BF16))
        row[:, columns] = jnp.concatenate(sides, axis=1)
    results = [
        pltpu.make_async_copy(turned, basis_out, came.at[0]),
        pltpu.make_async_copy(lifting, transfer_out, came.at[1]),
        pltpu.make_async_copy(row, top_out, came.at[2]),
    ]
    for copy in results:
        copy.start()
    run()
    for leaf in range(leaves):
        store(leaf).wait()
    for copy in results:
        copy.wait()


def pack(branch, basis, transfer, top_blocks, far_blocks, far_mask, far_slot, near_index, near_mask, inner, slots):
    leaves, entries, rank, _ = far_blocks.shape
    shape = (inner, leaves * rank, slots * rank)
    turned = (leaves, basis.shape[2], rank)
    lifting = (rank, leaves * rank)
    row = (rank, top_blocks.shape[1] * rank)
    return call(
        pack_kernel,
        (branch, far_mask, far_slot, near_index, near_mask, far_blocks, basis, transfer, top_blocks),
        (SMEM,) * 5 + (HBM,) * 4,
        [
            (shape, BF16, HBM),
            ((1,), jnp.int32, SMEM),
            ((near_index.size,), jnp.int32, SMEM),
            (turned, BF16, HBM),
            (lifting, BF16, HBM),
            (row, BF16, HBM),
        ],
        [
            pltpu.VMEM(far_blocks.shape, BF16),
            pltpu.VMEM((inner * slots, rank, rank), F32),
            pltpu.VMEM(shape, BF16),
            pltpu.VMEM(basis.shape, BF16),
            pltpu.VMEM(transfer.shape, BF16),
            pltpu.VMEM(top_blocks.shape, BF16),
            pltpu.VMEM(turned, BF16),
            pltpu.VMEM(lifting, BF16),
            pltpu.VMEM(row, BF16),
            semaphores(leaves),
            semaphores(leaves),
            semaphores(3),
        ],
        "pack",
        0,
        10 << 20,
    )


def choose_kernel(count_ref, list_ref, near_ref, _, out_ref, chosen, moved, given):
    piece = chosen.shape[0] // given.shape[0]
    entries = near_ref.shape[1]
    count = count_ref[0]

    def move(i):
        entry = list_ref[i]
        source = near_ref.at[entry // entries, entry % entries]
        return pltpu.make_async_copy(source, chosen.at[i], moved.at[i])

    def give(i):
        some = slab(i, piece)
        return pltpu.make_async_copy(chosen.at[some], out_ref.at[some], given.at[i])

    def each(number, do):
        def body(i, carry):
            do(i)
            return carry

        lax.fori_loop(0, number, body, 0)

    pieces = (count + piece - 1) // piece
    each(count, lambda i: move(i).start())
    each(count, lambda i: move(i).wait())
    each(pieces, lambda i: give(i).start())
    each(pieces, lambda i: give(i).wait())


def choose(listed, near_blocks, earlier):
    leaves, entries, size, _ = near_blocks.shape
    shape = (leaves * entries, size, size)
    return call(
        choose_kernel,
        (*listed, near_blocks, earlier),
        (SMEM, SMEM, HBM, AFTER),
        [(shape, BF16, HBM)],
        [pltpu.VMEM(shape, BF16), semaphores(shape[0]), semaphores(shape[0] // 8)],
        "choose",
        0,
        5 << 20,
    )[0]


def near_kernel(index_ref, mask_ref, blocks_ref, own_ref, *refs):
    out_ref, blocks, own, result, arrived, came, left = refs[-7:]
    leaves, entries, size, _ = blocks.shape
    pair = leaves // CHUNKS

    def fetch(leaf):
        return [pltpu.make_async_copy(blocks_ref.at[leaf], blocks.at[leaf], arrived.at[leaf])]

    def store(i):
        some = slab(i, pair)
        return pltpu.make_async_copy(result.at[some], out_ref.at[some], left.at[i])

    def work(leaf):
        total = None
        for n in range(entries):
            place = index_ref[leaf, n] - HW
            inside = (place >= 0) & (place < leaves)
            weight = jnp.where(inside, mask_ref[leaf, n], 0).astype(F32).astype(BF16)
            values = own[jnp.clip(place, 0, leaves - 1)] * weight
            term = dot(blocks[leaf, n], values)
            total = term if total is None else total + term
        result[leaf] = total

        @pl.when(leaf % pair == pair - 1)
        def _():
            store(leaf // pair).start()

    begin, run = windowed(leaves, AHEAD, fetch, work)
    copy = pltpu.make_async_copy(own_ref, own, came)
    copy.start()
    begin()
    copy.wait()
    run()
    for i in range(CHUNKS):
        store(i).wait()


def near_field(near_index, near_mask, near_blocks, own, *earlier):
    leaves, _, size, _ = near_blocks.shape
    columns = own.shape[2]
    return call(
        near_kernel,
        (near_index, near_mask, near_blocks, own) + earlier,
        (SMEM, SMEM, HBM, HBM) + (AFTER,) * len(earlier),
        [((leaves, size, columns), F32, HBM)],
        [
            pltpu.VMEM(near_blocks.shape, BF16),
            pltpu.VMEM(own.shape, BF16),
            pltpu.VMEM((leaves, size, columns), F32),
            semaphores(leaves),
            semaphores(),
            semaphores(leaves),
        ],
        "near_field",
        2 * near_blocks.size * columns,
        2 * near_blocks.size,
    )[0]


def gather_sum_kernel(recv, *refs, lead):
    out_ref, split = refs[-2:]
    rank = out_ref.shape[0] - DOT_ROWS
    total = recv[0, lead:].astype(F32)
    for i in range(1, recv.shape[0]):
        total = total + recv[i, lead:].astype(F32)
    store_split(split, jnp.concatenate(joined(total[rank:]), axis=0), 5)
    if rank > 0:
        out_ref[:rank] = total[:rank].astype(BF16)
    out_ref[rank:] = split[...].astype(BF16)


def gather_sum(recv, lead, earlier):
    _, rows, columns = recv.shape
    return call(
        functools.partial(gather_sum_kernel, lead=lead),
        (recv, earlier),
        (VMEM, AFTER),
        [((rows - lead, columns), BF16, VMEM)],
        [pltpu.VMEM((DOT_ROWS, columns), F32)],
        "gather_sum",
        1 << 20,
        1 << 19,
    )[0]


def stack_kernel(*refs):
    for i, ref in enumerate(refs[:-2]):
        refs[-1][i] = ref[...]


def over_branches(summed, outer, earlier, between):
    shifts = [[(o, (o + 2 * j) % outer) for o in range(outer)] for j in range(1, outer // 2)]
    parts = [summed] + [lax.ppermute(summed, "outer", shift) for shift in shifts]
    column = call(
        stack_kernel,
        parts + [earlier],
        [VMEM] * len(parts) + [AFTER_VMEM],
        [((len(parts),) + summed.shape, BF16, VMEM)],
        [],
        "stack",
        0,
        1 << 18,
    )[0]
    other = lax.ppermute(column, "outer", [(o, o ^ 1) for o in range(outer)])
    return column, other, between(column)


def in_order(branch, column, other, ups):
    count = ups.shape[0]
    for j in range(count // 2):
        ups[lax.rem(branch[0] + count - 2 * j, count)] = column[j]
        mate = branch[0] + 1 - 2 * lax.rem(branch[0], 2)
        ups[lax.rem(mate + count - 2 * j, count)] = other[j]


def far_kernel(count_ref, list_ref, recv, packed_ref, blocks_ref, *refs):
    held = (len(refs) - 7) // 2
    sources, (_, far, blocks), targets = refs[:held], refs[held : held + 3], refs[held + 3 : -4]
    packed, arrived, fetched, loaded = refs[-4:]
    share = packed.shape[0] // CHUNKS
    width = packed.shape[2]
    chosen = len(blocks_ref.shape) == 3
    piece = blocks.shape[0] // fetched.shape[0]
    count = (count_ref[0] + piece - 1) // piece

    def fetch(i):
        some = slab(i, share)
        return [pltpu.make_async_copy(packed_ref.at[some], packed.at[some], arrived.at[i])]

    def block(i):
        if chosen:
            some = slab(i, piece)
            return pltpu.make_async_copy(blocks_ref.at[some], blocks.at[some], fetched.at[i])
        entry, entries = list_ref[i], blocks_ref.shape[1]
        source = blocks_ref.at[entry // entries, entry % entries]
        return pltpu.make_async_copy(source, blocks.at[i], fetched.at[i])

    def ask(i, carry):
        block(i).start()
        return carry

    def have(i, carry):
        block(i).wait()
        return carry

    def work(i):
        term = None
        for j in range(share):
            source = i * share + j
            one = dot(packed[source], recv[source, :width])
            term = one if term is None else term + one

        @pl.when(i == 0)
        def _():
            far[...] = term

        @pl.when(i > 0)
        def _():
            far[...] += term

    loads = [
        pltpu.make_async_copy(source, target, loaded.at[i])
        for i, (source, target) in enumerate(zip(sources, targets))
    ]
    begin, run = windowed(CHUNKS, CHUNKS, fetch, work)
    begin()
    lax.fori_loop(0, count, ask, 0)
    for copy in loads:
        copy.start()
    run()
    lax.fori_loop(0, count, have, 0)
    for copy in loads:
        copy.wait()


def far_field(listed, recv, packed, near_blocks, held, earlier):
    sources, rows, _ = packed.shape
    size = near_blocks.shape[-1]
    number = near_blocks.size // size**2
    pieces = number // 8 if near_blocks.ndim == 3 else number
    outs = [((rows, recv.shape[2]), F32, VMEM), ((number, size, size), BF16, VMEM)]
    far, blocks, *held = call(
        far_kernel,
        (*listed, recv, packed, near_blocks, *held, earlier),
        (SMEM, SMEM, VMEM, HBM, HBM) + (HBM,) * len(held) + (AFTER_VMEM,),
        outs + [(a.shape, a.dtype, VMEM) for a in held],
        [
            pltpu.VMEM(packed.shape, BF16),
            semaphores(CHUNKS),
            semaphores(pieces),
            semaphores(len(held)),
        ],
        "far_field",
        2 * packed.size * recv.shape[2],
        2 * packed.size,
    )
    return far, blocks, held


def halo_kernel(count_ref, list_ref, index_ref, blocks, before, after, near_in, *refs):
    held = (len(refs) - 4) // 2
    sources, near, targets = refs[:held], refs[held + 1], refs[held + 2 : -2]
    halo, loaded = refs[-2:]
    loads = [
        pltpu.make_async_copy(source, target, loaded.at[i])
        for i, (source, target) in enumerate(zip(sources, targets))
    ]
    for copy in loads:
        copy.start()
    leaves, reach, entries = near.shape[0], before.shape[0], index_ref.shape[1]
    halo[:reach] = before[...]
    halo[reach:] = after[...]
    count = count_ref[0]
    at_once = 8

    def add(group, carry):
        terms = []
        for j in range(at_once):
            i = jnp.minimum(group * at_once + j, count - 1)
            weight = (group * at_once + j < count).astype(F32).astype(BF16)
            entry = list_ref[i]
            leaf = entry // entries
            place = index_ref[leaf, entry % entries]
            values = halo[jnp.where(place < reach, place, place - leaves)] * weight
            terms.append((leaf, dot(blocks[i], values)))
        for leaf, term in terms:
            near[leaf] += term
        return carry

    lax.fori_loop(0, (count + at_once - 1) // at_once, add, 0)
    for copy in loads:
        copy.wait()


def halo_part(listed, near_index, blocks, before, after, near, held, earlier):
    return call(
        halo_kernel,
        (*listed, near_index, blocks, before, after, near, *held, earlier),
        (SMEM, SMEM, SMEM, VMEM, VMEM, VMEM, VMEM) + (HBM,) * len(held) + (AFTER_VMEM,),
        [(a.shape, a.dtype, VMEM) for a in (near, *held)],
        [pltpu.VMEM((2 * before.shape[0],) + before.shape[1:], BF16), semaphores(len(held))],
        "halo_part",
        1 << 28,
        2 << 20,
        {6: 0},
    )


def sum_kernel(*refs, axis, stride):
    *parts, _, out, rows, split = refs
    count = len(parts)
    place = lax.rem(lax.axis_index(axis).astype(jnp.int32) // stride, count)
    for j, part in enumerate(parts):
        rows[lax.rem(place + count - j, count)] = part[...].astype(F32)
    total = rows[0]
    for i in range(1, count):
        total = total + rows[i]
    store_split(split, jnp.concatenate(joined(total), axis=0), 5)
    out[...] = split[...].astype(BF16)


def sum_over(dots, axis, stride, count, earlier, after):
    if count == 1:
        return dots
    size = lax.axis_size(axis)

    def moved(i, j):
        at = i // stride % count
        return i + ((at + j) % count - at) * stride

    parts = [dots]
    for j in range(1, count):
        parts.append(lax.ppermute(dots, axis, [(i, moved(i, j)) for i in range(size)]))
    return call(
        functools.partial(sum_kernel, axis=axis, stride=stride),
        (*parts, earlier),
        (VMEM,) * count + (after,),
        [(dots.shape, BF16, VMEM)],
        [pltpu.VMEM((count,) + dots.shape, F32), pltpu.VMEM((DOT_ROWS, dots.shape[1]), F32)],
        "sum_over",
        0,
        1 << 18,
    )[0]


def stage_kernel(*refs, k, points):
    refs = list(refs)
    take = lambda count: [refs.pop(0) for _ in range(count)]
    m = k - 1
    first, sends = k == 0, k < STEPS
    send_slot, branch = take(2)
    if first:
        z_any, basis_any, transfer_any = take(3)
    else:
        column, other, state, far, near, basis, turned, transfer, lifting, top = take(10)
        zs = take(k)
        (z_any,) = take(1)
    state_out, send = take(2)
    if sends:
        coarse_any, low, high = take(3)
    sums, split, arrived, left = take(4)
    if sends:
        coarse, skeletons = take(2)
    if first:
        basis, transfer, vectors, came = take(4)
    else:
        ups, result, coef, combined = take(4)

    leaves, rank, size = basis.shape
    group = leaves // CHUNKS

    def fetch(i):
        if not first:
            return []
        some = slab(i, group)
        return [pltpu.make_async_copy(z_any.at[some], vectors.at[some], arrived.at[i])]

    pieces = CHUNKS

    def stores(i):
        some = slab(i, leaves // pieces)
        pairs = []
        if not first and sends:
            pairs.append((result.at[some], z_any.at[some]))
        if sends:
            pairs.append((coarse.at[some], coarse_any.at[some]))
        return [
            pltpu.make_async_copy(source, target, left.at[n, i])
            for n, (source, target) in enumerate(pairs)
        ]

    def work(i):
        for j in range(group):
            leaf = i * group + j
            if first:
                others = []
                z = vectors[leaf]
            else:
                others = [ref[leaf] for ref in zs]
                z = near[leaf] + dot(turned[leaf], combined[slab(leaf, rank)])
                for l in range(m):
                    z = z - coef[l : l + 1, :] * others[l + 1]
                z = z * coef[STEPS : STEPS + 1, :]
                if sends:
                    result[leaf] = z
                else:
                    z_any[leaf] = z
            if sends:
                rounded = z.astype(BF16)
                coarse[leaf] = rounded
                skeletons[slab(leaf, rank)] = dot(basis[leaf], rounded).astype(BF16)
            for l, vector in enumerate(others + [z]):
                sums[l] += jnp.sum((z * vector).reshape(size // 8, 8, z.shape[1]), axis=0)
        for copy in stores(i):
            copy.start()

    begin, run = windowed(CHUNKS, CHUNKS, fetch, work)
    if first:
        small = [
            pltpu.make_async_copy(basis_any, basis, came.at[0]),
            pltpu.make_async_copy(transfer_any, transfer, came.at[1]),
        ]
        for copy in small:
            copy.start()
    begin()
    sums[...] = jnp.zeros(sums.shape, F32)
    if first:
        state_out[...] = jnp.zeros(state_out.shape, F32)
        for copy in small:
            copy.wait()
    else:
        in_order(branch, column, other, ups)
        count, columns = ups.shape[0], ups.shape[2]
        incoming = dot(top[...], ups[:, :rank].reshape(count * rank, columns)).astype(BF16)
        down = dot(transfer[...].reshape(leaves * rank, rank), incoming)
        combined[...] = (far[...] + down).astype(BF16)
        grams = [row / points for row in from_branches(ups, rank)]
        state_out[...] = state[...]
        weights, inverse = coefficients(m, grams, state, state_out)
        for i, weight in enumerate(weights):
            coef[i : i + 1, :] = weight
        coef[STEPS : STEPS + 1, :] = inverse
    if first:
        run()
    else:
        for i in range(CHUNKS):
            work(i)

    if sends:
        low[...] = coarse[:HW]
        high[...] = coarse[leaves - HW :]
        if first:
            lifted = dot_first(transfer[...].reshape(leaves * rank, rank), skeletons[...])
        else:
            lifted = dot(lifting[...], skeletons[...])
        lifted = lifted.astype(BF16)
    products = [jnp.sum(sums[i], axis=0, keepdims=True) for i in range(k + 1)]
    products = jnp.concatenate(products + [jnp.zeros_like(products[0])] * (7 - k), axis=0)
    store_split(split, products, k + 1)
    dots = split[...].astype(BF16)
    if sends:
        slots, inner = send_slot.shape
        for r in range(inner):
            for s in range(slots):
                send[r, s * rank : (s + 1) * rank] = skeletons[slab(send_slot[s, r], rank)]
            send[r, slots * rank : (slots + 1) * rank] = lifted
            send[r, (slots + 1) * rank :] = dots
    else:
        send[...] = dots
    for i in range(pieces):
        for copy in stores(i):
            copy.wait()


def stage(k, points, send_slot, branch, rhs, basis, transfer, later):
    leaves, rank, size = basis.shape
    first, sends = k == 0, k < STEPS
    tall = rhs.shape
    columns = tall[2]
    slots, inner = send_slot.shape
    names, outs = [], []

    def get(name, shape, dtype, spec):
        names.append(name)
        outs.append((shape, dtype, spec))

    args, specs = [send_slot, branch], [SMEM, SMEM]
    if first:
        args += [rhs, basis, transfer]
        specs += [HBM] * 3
    else:
        args += later
        specs += [VMEM] * len(later)
        get("z", tall, F32, HBM if sends else VMEM)
    get("state", (STATE_ROWS, columns), F32, VMEM)
    rows = (slots + 1) * rank + DOT_ROWS
    get("send", (inner, rows, columns) if sends else (DOT_ROWS, columns), BF16, VMEM)
    if sends:
        get("coarse", tall, BF16, HBM)
        get("low", (HW, size, columns), BF16, VMEM)
        get("high", (HW, size, columns), BF16, VMEM)

    scratch = [
        pltpu.VMEM((STEPS + 1, 8, columns), F32),
        pltpu.VMEM((DOT_ROWS, columns), F32),
        semaphores(CHUNKS),
        semaphores(2, CHUNKS),
    ]
    if sends:
        scratch += [
            pltpu.VMEM(tall, BF16),
            pltpu.VMEM((leaves * rank, columns), BF16),
        ]
    if first:
        scratch += [
            pltpu.VMEM(basis.shape, BF16),
            pltpu.VMEM(transfer.shape, BF16),
            pltpu.VMEM(tall, F32),
            semaphores(2),
        ]
    else:
        column = later[0].shape
        scratch += [
            pltpu.VMEM((2 * column[0],) + column[1:], BF16),
            pltpu.VMEM(tall, F32),
            pltpu.VMEM((8, columns), F32),
            pltpu.VMEM((leaves * rank, columns), BF16),
        ]
    results = call(
        functools.partial(stage_kernel, k=k, points=points),
        args,
        specs,
        outs,
        scratch,
        f"stage{k}",
        1 << 27,
        (k + 4) << 20,
    )
    return dict(zip(names, results))


def vectors_kernel(*refs, wanted, held, final, points):
    refs = list(refs)
    take = lambda count: [refs.pop(0) for _ in range(count)]
    (state,) = take(1)
    if final:
        branch, column, other = take(3)
    zs = take(wanted[-1] + 1)
    _, krylov = take(2)
    if final:
        (hess_out,) = take(1)
    result, left = take(2)
    if final:
        after, ups = take(2)
    else:
        after = state
    if not held:
        vectors, arrived = take(2)
    parts = left.shape[1]
    group = zs[0].shape[0] // parts

    def fetch(i):
        if held:
            return []
        some = slab(i, group)
        return [
            pltpu.make_async_copy(z.at[some], vectors.at[l, some], arrived.at[l, i])
            for l, z in enumerate(zs)
        ]

    def store(n, i):
        some = slab(i, group)
        return pltpu.make_async_copy(result.at[n, some], krylov.at[wanted[n], some], left.at[n, i])

    def work(i):
        for j in range(group):
            leaf = i * group + j
            for n, which in enumerate(wanted):
                vector = None
                for l in range(which + 1):
                    row = basis_row(which, l)
                    values = zs[l][leaf] if held else vectors[l, leaf]
                    term = after[row : row + 1, :] * values
                    vector = term if vector is None else vector + term
                result[n, leaf] = vector
        for n in range(len(wanted)):
            store(n, i).start()

    begin, run = windowed(parts, parts, fetch, work)
    begin()
    if final:
        in_order(branch, column, other, ups)
        grams = [row / points for row in from_branches(ups, 0)]
        after[...] = state[...]
        coefficients(STEPS, grams, state, after)
    run()
    if final:
        for i in range(STEPS + 1):
            for j in range(STEPS):
                row = i * STEPS + j
                if i <= j + 1:
                    hess_out[i, j : j + 1, :] = after[row : row + 1, :]
                else:
                    hess_out[i, j : j + 1, :] = jnp.zeros((1, hess_out.shape[2]), F32)
    for n in range(len(wanted)):
        for i in range(parts):
            store(n, i).wait()


def vectors(state, zs, wanted, before, parts, products=None, points=0):
    final = products is not None
    held = wanted[0] > 0
    tall = zs[0].shape
    count = wanted[-1] + 1
    shape = (STEPS + 1,) + tall
    scratch = [pltpu.VMEM((len(wanted),) + tall, F32), semaphores(len(wanted), parts)]
    outs = [(shape, F32, HBM)]
    args, specs = [state], [VMEM]
    if final:
        args += products
        specs += [SMEM, VMEM, VMEM]
        column = products[1].shape
        outs.append(((STEPS + 1, STEPS, tall[2]), F32, FREE))
        scratch += [
            pltpu.VMEM(state.shape, F32),
            pltpu.VMEM((2 * column[0],) + column[1:], BF16),
        ]
    args += zs[:count]
    specs += [VMEM if held else HBM] * count
    args.append(before)
    specs.append(HBM if held else AFTER)
    if not held:
        scratch += [pltpu.VMEM((count,) + tall, F32), semaphores(count, parts)]
    return call(
        functools.partial(
            vectors_kernel, wanted=wanted, held=held, final=final, points=points
        ),
        args,
        specs,
        outs,
        scratch,
        "last_vector" if final else "vectors",
        1 << 23,
        len(wanted) << 21,
        {len(args) - 1: 0} if held else {},
    )


def shards(
    rhs,
    near_blocks,
    near_index,
    near_mask,
    basis,
    far_blocks,
    far_slot,
    far_mask,
    send_slot,
    transfer,
    top_blocks,
):
    outer, inner = lax.axis_size("outer"), lax.axis_size("inner")
    points = outer * inner * rhs.shape[0]
    leaves, rank = basis.shape[:2]
    slots = send_slot.shape[2]
    branch = lax.axis_index("outer").astype(jnp.int32).reshape(1)
    up_pairs = [(i, i + 1) for i in range(inner - 1)]
    down_pairs = [(j, i) for i, j in up_pairs]
    wanted = send_slot[0].T

    def exchange(array, axis):
        return lax.all_to_all(array, axis, split_axis=0, concat_axis=0, tiled=True)

    zs = [rhs.reshape(leaves, -1, rhs.shape[1])]
    out = stage(0, points, wanted, branch, zs[0], basis, transfer, None)
    packed, count, entries, turned, lifting, top = pack(
        branch, basis, transfer, top_blocks, far_blocks, far_mask, far_slot, near_index, near_mask,
        inner, slots,
    )
    listed = (count, entries)
    state = out["state"]
    for k in range(1, STEPS + 1):
        recv = exchange(out["send"], "inner")
        before = lax.ppermute(out["high"], "inner", up_pairs)
        after = lax.ppermute(out["low"], "inner", down_pairs)
        earlier = (packed,) if k == 1 else ()
        near = near_field(near_index, near_mask, near_blocks, out["coarse"], *earlier)
        done = near
        if k == 1:
            chosen = near_blocks
        elif k == 2:
            chosen = done = choose(listed, near_blocks, near)
        if k == STEPS:
            krylov = done = vectors(state, zs, list(range(STEPS - 1)), near, CHUNKS)[0]
        summed = gather_sum(recv, slots * rank, done)
        local_far, blocks, (near,) = far_field(
            listed, recv, packed, chosen, (near,), summed
        )

        def between(column):
            held = (basis, turned, transfer, lifting, top, *zs)
            return halo_part(listed, near_index, blocks, before, after, near, held, column)

        column, other, (near, *held) = over_branches(summed, outer, local_far, between)
        later = [column, other, state, local_far, near, *held]
        out = stage(k, points, wanted, branch, zs[0], basis, transfer, later)
        state = out["state"]
        zs = zs + [out["z"]]
    low = 4 if inner % 4 == 0 else inner
    held = held[-STEPS:] + [out["z"]]
    krylov = vectors(state, held, [STEPS - 1], krylov, 2)[0]
    summed = sum_over(out["send"], "inner", 1, low, krylov, AFTER)
    summed = sum_over(summed, "inner", low, inner // low, summed, AFTER_VMEM)
    column, other, _ = over_branches(summed, outer, summed, lambda column: None)
    products = [branch, column, other]
    krylov, hessenberg = vectors(state, held, [STEPS], krylov, 2, products, points)
    return krylov.reshape(STEPS + 1, *rhs.shape), hessenberg


def solution(mesh):
    return jax.shard_map(
        shards,
        mesh=mesh,
        in_specs=(
            P(("outer", "inner"), None),
            P(("outer", "inner"), None, None, None),
            P(("outer", "inner"), None),
            P(("outer", "inner"), None),
            P(("outer", "inner"), None, None),
            P(("outer", "inner"), None, None, None),
            P(("outer", "inner"), None),
            P(("outer", "inner"), None),
            P(("outer", "inner"), None, None),
            P(("outer", "inner"), None, None),
            P("outer", None, None, None),
        ),
        out_specs=(P(None, ("outer", "inner"), None), P()),
        check_vma=False,
    )
```

```python
import functools

import jax
import jax.numpy as jnp
from jax import lax
from jax.experimental import pallas as pl
from jax.experimental.pallas import tpu as pltpu
from jax.sharding import PartitionSpec as P

HW = 2
STEPS = 4
EPS = 1e-06
PIECES = 3
DOT_ROWS = 16
STATE_ROWS = 64
VMEM_BYTES = 32 * 1024 * 1024
BF16 = jnp.bfloat16
F32 = jnp.float32


def dot(a, b):
    return jnp.dot(a, b, preferred_element_type=F32)


def dot_first(a, b):
    return lax.dot_general(a, b, (((0,), (0,)), ((), ())), preferred_element_type=F32)


def store_split(ref, values, count):
    rest = values
    ref[...] = jnp.zeros(ref.shape, F32)
    for piece in range(PIECES):
        part = rest.astype(BF16).astype(F32)
        ref[piece * 5 : piece * 5 + count, :] = part[:count]
        rest = rest - part


def joined(rows):
    return [rows[i : i + 1] + rows[5 + i : 6 + i] + rows[10 + i : 11 + i] for i in range(5)]


def entry_row(i, l):
    low, high = min(i, l), max(i, l)
    return 20 + high * (high + 1) // 2 + low


def basis_row(i, l):
    return 32 + i * (i + 1) // 2 + l


def coefficients(m, grams, state_in, state_out):
    last = m - 1
    entry = lambda i, l: state_in[entry_row(i, l) : entry_row(i, l) + 1, :]
    expand = lambda i, l: state_in[basis_row(i, l) : basis_row(i, l) + 1, :]

    def put(row, value):
        state_out[row : row + 1, :] = value

    dots = []
    for i in range(m):
        dots.append(sum(expand(i, l) * grams[l] for l in range(i + 1)))
    weights = [dots[i] + entry(i, last) for i in range(m)]
    spread = [sum(weights[l] * entry(i, l) for l in range(m)) for i in range(m)]
    square = grams[m]
    for i in range(m):
        square = square + weights[i] * (weights[i] + spread[i] - 2.0 * dots[i])
    total = jnp.maximum(square, 0.0) + EPS
    root = jnp.sqrt(total)
    inverse = 1.0 / root
    for l in range(m):
        value = sum(weights[i] * expand(i, l) for i in range(l, m))
        put(basis_row(m, l), -inverse * value)
    put(basis_row(m, m), inverse)
    for i in range(m):
        put(i * STEPS + last, weights[i] + (1.0 if i == last else 0.0))
    if m > 0:
        put(m * STEPS + last, root)
    if m < STEPS:
        for i in range(m):
            put(entry_row(i, m), (-entry(i, last) - spread[i]) * inverse)
        put(entry_row(m, m), -EPS / total)
    return weights, inverse


def from_branches(ups_ref, rank):
    rows = ups_ref[0, rank:].astype(F32)
    for c in range(1, ups_ref.shape[0]):
        rows = rows + ups_ref[c, rank:].astype(F32)
    return joined(rows)


SMEM = pl.BlockSpec(memory_space=pltpu.SMEM)
INDEX = pl.BlockSpec(memory_space=pltpu.SMEM)
VMEM = pl.BlockSpec(memory_space=pltpu.VMEM)
HBM = pl.BlockSpec(memory_space=pl.ANY)
AFTER = pl.BlockSpec(memory_space=pl.ANY)
AFTER_VMEM = pl.BlockSpec(memory_space=pl.ANY)
LOOSE = pl.BlockSpec(memory_space=pl.ANY)
FREE = pl.BlockSpec(memory_space=pltpu.VMEM)
AHEAD = 3
LISTED, PLACE, OWN, INDICES = 64, 128, 192, 256
CHUNKS = 4
PIN = True


def call(kernel, args, in_specs, outs, scratch, name, flops, moved, aliases={}):
    def pinned(array, spec):
        if not PIN or not any(spec is one for one in (VMEM, HBM, SMEM, AFTER, AFTER_VMEM)):
            return array
        in_vmem = spec is VMEM or spec is AFTER_VMEM
        return pltpu.with_memory_space_constraint(array, pltpu.VMEM if in_vmem else pltpu.HBM)

    def shape_of(shape, dtype, spec):
        if not PIN or not (spec is VMEM or spec is HBM):
            return jax.ShapeDtypeStruct(shape, dtype)
        return (pltpu.VMEM if spec is VMEM else pltpu.HBM)(shape, dtype)

    return pl.pallas_call(
        kernel,
        in_specs=list(in_specs),
        out_specs=[spec for _, _, spec in outs],
        out_shape=[shape_of(*out) for out in outs],
        scratch_shapes=scratch,
        input_output_aliases=aliases,
        compiler_params=pltpu.CompilerParams(vmem_limit_bytes=VMEM_BYTES),
        cost_estimate=pl.CostEstimate(flops=flops, bytes_accessed=moved, transcendentals=0),
        name=name,
    )(*[pinned(array, spec) for array, spec in zip(args, in_specs)])


def semaphores(*shape):
    return pltpu.SemaphoreType.DMA(shape)


def windowed(count, ahead, fetch, work):
    def start(i):
        for j, copy in enumerate(fetch(i)):
            copy.start(priority=j % 2)

    def body(i, carry):
        @pl.when(i + ahead < count)
        def _():
            start(i + ahead)

        for copy in fetch(i):
            copy.wait()
        work(i)
        return carry

    def begin():
        for i in range(min(ahead, count)):
            start(i)

    return begin, lambda: lax.fori_loop(0, count, body, 0)


def slab(i, size):
    return pl.ds(pl.multiple_of(i * size, size), size)


def pack_kernel(branch, mask_ref, slot_ref, index_ref, near_mask_ref, far_ref, *refs):
    basis_ref, transfer_ref, top_ref = refs[:3]
    out_ref, index_out, basis_out, transfer_out, top_out = refs[3:8]
    blocks, total, packed, basis, transfer, top, turned, lifting, row = refs[8:17]
    arrived, left, came = refs[17:]
    leaves, entries, rank, _ = blocks.shape
    sources, _, width = packed.shape
    slots = width // rank
    near_entries = index_ref.shape[1]

    def fetch(leaf):
        return [pltpu.make_async_copy(far_ref.at[leaf], blocks.at[leaf], arrived.at[leaf])]

    def store(leaf):
        rows = slab(leaf, rank)
        return pltpu.make_async_copy(packed.at[:, rows], out_ref.at[:, rows], left.at[leaf])

    def work(leaf):
        total[...] = jnp.zeros(total.shape, F32)
        for f in range(entries):
            weight = mask_ref[leaf, f].astype(F32)
            total[slot_ref[leaf, f]] += blocks[leaf, f].astype(F32) * weight
        rows = slab(leaf, rank)
        for source in range(sources):
            sides = [total[source * slots + s] for s in range(slots)]
            packed[source, rows] = jnp.concatenate(sides, axis=1).astype(BF16)
        store(leaf).start()

    def list_one(i, count):
        leaf, n = i // near_entries, i % near_entries
        place = index_ref[leaf, n]
        hit = (near_mask_ref[leaf, n] != 0) & ((place < HW) | (place >= HW + leaves))
        own = (place >= HW) & (place < HW + leaves) & (near_mask_ref[leaf, n] != 0)
        index_out[OWN + i] = jnp.where(own, place - HW + 1, 0)
        index_out[LISTED + i] = 0
        index_out[PLACE + i] = 0

        @pl.when(hit)
        def _():
            index_out[LISTED + count] = i
            index_out[PLACE + count] = jnp.where(place < HW, place, place - leaves)

        return count + hit.astype(jnp.int32)

    small = [
        pltpu.make_async_copy(basis_ref, basis, came.at[0]),
        pltpu.make_async_copy(transfer_ref, transfer, came.at[1]),
        pltpu.make_async_copy(top_ref, top, came.at[2]),
    ]
    for copy in small:
        copy.start()
    begin, run = windowed(leaves, AHEAD, fetch, work)
    begin()
    index_out[0] = lax.fori_loop(0, leaves * near_entries, list_one, 0)
    for copy in small:
        copy.wait()
    turn = lambda a: a.astype(F32).T.astype(BF16)
    for leaf in range(leaves):
        turned[leaf] = turn(basis[leaf])
    for pair in range(leaves // 2):
        columns = slice(pair * 2 * rank, (pair + 1) * 2 * rank)
        sides = [turn(transfer[2 * pair + j]) for j in range(2)]
        lifting[:, columns] = jnp.concatenate(sides, axis=1)
    for pair in range(top.shape[1] // 2):
        columns = slice(pair * 2 * rank, (pair + 1) * 2 * rank)
        sides = []
        for c in (2 * pair, 2 * pair + 1):
            sides.append(top[0, c] * (branch[0] != c).astype(F32).astype(BF16))
        row[:, columns] = jnp.concatenate(sides, axis=1)
    results = [
        pltpu.make_async_copy(turned, basis_out, came.at[0]),
        pltpu.make_async_copy(lifting, transfer_out, came.at[1]),
        pltpu.make_async_copy(row, top_out, came.at[2]),
    ]
    for copy in results:
        copy.start()
    run()
    for leaf in range(leaves):
        store(leaf).wait()
    for copy in results:
        copy.wait()


def pack(branch, basis, transfer, top_blocks, far_blocks, far_mask, far_slot, near_index, near_mask, inner, slots):
    leaves, entries, rank, _ = far_blocks.shape
    shape = (inner, leaves * rank, slots * rank)
    turned = (leaves, basis.shape[2], rank)
    lifting = (rank, leaves * rank)
    row = (rank, top_blocks.shape[1] * rank)
    return call(
        pack_kernel,
        (branch, far_mask, far_slot, near_index, near_mask, far_blocks, basis, transfer, top_blocks),
        (SMEM,) * 5 + (HBM,) * 4,
        [
            (shape, BF16, HBM),
            ((INDICES,), jnp.int32, INDEX),
            (turned, BF16, HBM),
            (lifting, BF16, HBM),
            (row, BF16, HBM),
        ],
        [
            pltpu.VMEM(far_blocks.shape, BF16),
            pltpu.VMEM((inner * slots, rank, rank), F32),
            pltpu.VMEM(shape, BF16),
            pltpu.VMEM(basis.shape, BF16),
            pltpu.VMEM(transfer.shape, BF16),
            pltpu.VMEM(top_blocks.shape, BF16),
            pltpu.VMEM(turned, BF16),
            pltpu.VMEM(lifting, BF16),
            pltpu.VMEM(row, BF16),
            semaphores(leaves),
            semaphores(leaves),
            semaphores(3),
        ],
        "pack",
        0,
        10 << 20,
    )


def choose_kernel(index_ref, near_ref, _, out_ref, chosen, moved, given):
    piece = chosen.shape[0] // given.shape[0]
    entries = near_ref.shape[1]
    count = index_ref[0]

    def move(i):
        entry = index_ref[LISTED + i]
        source = near_ref.at[entry // entries, entry % entries]
        return pltpu.make_async_copy(source, chosen.at[i], moved.at[i])

    def give(i):
        some = slab(i, piece)
        return pltpu.make_async_copy(chosen.at[some], out_ref.at[some], given.at[i])

    def each(number, do):
        def body(i, carry):
            do(i)
            return carry

        lax.fori_loop(0, number, body, 0)

    pieces = (count + piece - 1) // piece
    each(count, lambda i: move(i).start())
    each(count, lambda i: move(i).wait())
    each(pieces, lambda i: give(i).start())
    each(pieces, lambda i: give(i).wait())


def choose(index, near_blocks, earlier):
    leaves, entries, size, _ = near_blocks.shape
    shape = (leaves * entries, size, size)
    return call(
        choose_kernel,
        (index, near_blocks, earlier),
        (INDEX, HBM, AFTER),
        [(shape, BF16, HBM)],
        [pltpu.VMEM(shape, BF16), semaphores(shape[0]), semaphores(shape[0] // 8)],
        "choose",
        0,
        5 << 20,
    )[0]


def near_kernel(index_ref, blocks_ref, own_ref, *refs):
    out_ref, blocks, own, result, arrived, came, left = refs[-7:]
    leaves, entries, size, _ = blocks.shape
    pair = leaves // CHUNKS

    def fetch(leaf):
        return [pltpu.make_async_copy(blocks_ref.at[leaf], blocks.at[leaf], arrived.at[leaf])]

    def store(i):
        some = slab(i, pair)
        return pltpu.make_async_copy(result.at[some], out_ref.at[some], left.at[i])

    def work(leaf):
        total = None
        for n in range(entries):
            place = index_ref[OWN + leaf * entries + n]
            weight = (place > 0).astype(F32).astype(BF16)
            values = own[jnp.maximum(place - 1, 0)] * weight
            term = dot(blocks[leaf, n], values)
            total = term if total is None else total + term
        result[leaf] = total

        @pl.when(leaf % pair == pair - 1)
        def _():
            store(leaf // pair).start()

    begin, run = windowed(leaves, AHEAD, fetch, work)
    copy = pltpu.make_async_copy(own_ref, own, came)
    copy.start()
    begin()
    copy.wait()
    run()
    for i in range(CHUNKS):
        store(i).wait()


def near_field(index, near_blocks, own, *earlier):
    leaves, _, size, _ = near_blocks.shape
    columns = own.shape[2]
    return call(
        near_kernel,
        (index, near_blocks, own) + earlier,
        (INDEX, HBM, HBM) + (AFTER,) * len(earlier),
        [((leaves, size, columns), F32, HBM)],
        [
            pltpu.VMEM(near_blocks.shape, BF16),
            pltpu.VMEM(own.shape, BF16),
            pltpu.VMEM((leaves, size, columns), F32),
            semaphores(leaves),
            semaphores(),
            semaphores(leaves),
        ],
        "near_field",
        2 * near_blocks.size * columns,
        2 * near_blocks.size,
    )[0]


def gather_sum_kernel(recv, *refs, lead):
    out_ref, split = refs[-2:]
    rank = out_ref.shape[0] - DOT_ROWS
    total = recv[0, lead:].astype(F32)
    for i in range(1, recv.shape[0]):
        total = total + recv[i, lead:].astype(F32)
    store_split(split, jnp.concatenate(joined(total[rank:]), axis=0), 5)
    if rank > 0:
        out_ref[:rank] = total[:rank].astype(BF16)
    out_ref[rank:] = split[...].astype(BF16)


def gather_sum(recv, lead, earlier):
    _, rows, columns = recv.shape
    return call(
        functools.partial(gather_sum_kernel, lead=lead),
        (recv, earlier),
        (VMEM, AFTER),
        [((rows - lead, columns), BF16, VMEM)],
        [pltpu.VMEM((DOT_ROWS, columns), F32)],
        "gather_sum",
        1 << 20,
        1 << 19,
    )[0]


def stack_kernel(*refs):
    for i, ref in enumerate(refs[:-2]):
        refs[-1][i] = ref[...]


def over_branches(summed, outer, earlier, between):
    shifts = [[(o, (o + 2 * j) % outer) for o in range(outer)] for j in range(1, outer // 2)]
    parts = [summed] + [lax.ppermute(summed, "outer", shift) for shift in shifts]
    column = call(
        stack_kernel,
        parts + [earlier],
        [VMEM] * len(parts) + [AFTER_VMEM],
        [((len(parts),) + summed.shape, BF16, VMEM)],
        [],
        "stack",
        0,
        1 << 18,
    )[0]
    other = lax.ppermute(column, "outer", [(o, o ^ 1) for o in range(outer)])
    return column, other, between(column)


def in_order(branch, column, other, ups):
    count = ups.shape[0]
    for j in range(count // 2):
        ups[lax.rem(branch[0] + count - 2 * j, count)] = column[j]
        mate = branch[0] + 1 - 2 * lax.rem(branch[0], 2)
        ups[lax.rem(mate + count - 2 * j, count)] = other[j]


def far_kernel(index_ref, recv, packed_ref, blocks_ref, *refs):
    held = (len(refs) - 7) // 2
    sources, (_, far, blocks), targets = refs[:held], refs[held : held + 3], refs[held + 3 : -4]
    packed, arrived, fetched, loaded = refs[-4:]
    share = packed.shape[0] // CHUNKS
    width = packed.shape[2]
    chosen = len(blocks_ref.shape) == 3
    piece = blocks.shape[0] // fetched.shape[0]
    count = (index_ref[0] + piece - 1) // piece

    def fetch(i):
        some = slab(i, share)
        return [pltpu.make_async_copy(packed_ref.at[some], packed.at[some], arrived.at[i])]

    def block(i):
        if chosen:
            some = slab(i, piece)
            return pltpu.make_async_copy(blocks_ref.at[some], blocks.at[some], fetched.at[i])
        entry, entries = index_ref[LISTED + i], blocks_ref.shape[1]
        source = blocks_ref.at[entry // entries, entry % entries]
        return pltpu.make_async_copy(source, blocks.at[i], fetched.at[i])

    def ask(i, carry):
        block(i).start()
        return carry

    def have(i, carry):
        block(i).wait()
        return carry

    def work(i):
        term = None
        for j in range(share):
            source = i * share + j
            one = dot(packed[source], recv[source, :width])
            term = one if term is None else term + one

        @pl.when(i == 0)
        def _():
            far[...] = term

        @pl.when(i > 0)
        def _():
            far[...] += term

    loads = [
        pltpu.make_async_copy(source, target, loaded.at[i])
        for i, (source, target) in enumerate(zip(sources, targets))
    ]
    begin, run = windowed(CHUNKS, CHUNKS, fetch, work)
    begin()
    lax.fori_loop(0, count, ask, 0)
    for copy in loads:
        copy.start()
    run()
    lax.fori_loop(0, count, have, 0)
    for copy in loads:
        copy.wait()


def far_field(index, recv, packed, near_blocks, held, earlier):
    sources, rows, _ = packed.shape
    size = near_blocks.shape[-1]
    number = near_blocks.size // size**2
    pieces = number // 8 if near_blocks.ndim == 3 else number
    outs = [((rows, recv.shape[2]), F32, VMEM), ((number, size, size), BF16, VMEM)]
    far, blocks, *held = call(
        far_kernel,
        (index, recv, packed, near_blocks, *held, earlier),
        (INDEX, VMEM, HBM, HBM) + (HBM,) * len(held) + (AFTER_VMEM,),
        outs + [(a.shape, a.dtype, VMEM) for a in held],
        [
            pltpu.VMEM(packed.shape, BF16),
            semaphores(CHUNKS),
            semaphores(pieces),
            semaphores(len(held)),
        ],
        "far_field",
        2 * packed.size * recv.shape[2],
        2 * packed.size,
    )
    return far, blocks, held


def halo_kernel(index_ref, blocks, before, after, near_in, *refs):
    held = (len(refs) - 4) // 2
    sources, near, targets = refs[:held], refs[held + 1], refs[held + 2 : -2]
    halo, loaded = refs[-2:]
    loads = [
        pltpu.make_async_copy(source, target, loaded.at[i])
        for i, (source, target) in enumerate(zip(sources, targets))
    ]
    for copy in loads:
        copy.start()
    reach = before.shape[0]
    entries = blocks.shape[0] // near.shape[0]
    halo[:reach] = before[...]
    halo[reach:] = after[...]
    count = index_ref[0]
    at_once = 8

    def add(group, carry):
        terms = []
        for j in range(at_once):
            i = jnp.minimum(group * at_once + j, count - 1)
            weight = (group * at_once + j < count).astype(F32).astype(BF16)
            leaf = index_ref[LISTED + i] // entries
            values = halo[index_ref[PLACE + i]] * weight
            terms.append((leaf, dot(blocks[i], values)))
        for leaf, term in terms:
            near[leaf] += term
        return carry

    lax.fori_loop(0, (count + at_once - 1) // at_once, add, 0)
    for copy in loads:
        copy.wait()


def halo_part(index, blocks, before, after, near, held, earlier):
    return call(
        halo_kernel,
        (index, blocks, before, after, near, *held, earlier),
        (INDEX, VMEM, VMEM, VMEM, VMEM) + (HBM,) * len(held) + (AFTER_VMEM,),
        [(a.shape, a.dtype, VMEM) for a in (near, *held)],
        [pltpu.VMEM((2 * before.shape[0],) + before.shape[1:], BF16), semaphores(len(held))],
        "halo_part",
        1 << 28,
        2 << 20,
        {4: 0},
    )


def sum_kernel(*refs, axis, stride):
    *parts, _, out, rows, split = refs
    count = len(parts)
    place = lax.rem(lax.axis_index(axis).astype(jnp.int32) // stride, count)
    for j, part in enumerate(parts):
        rows[lax.rem(place + count - j, count)] = part[...].astype(F32)
    total = rows[0]
    for i in range(1, count):
        total = total + rows[i]
    store_split(split, jnp.concatenate(joined(total), axis=0), 5)
    out[...] = split[...].astype(BF16)


def sum_over(dots, axis, stride, count, earlier, after):
    if count == 1:
        return dots
    size = lax.axis_size(axis)

    def moved(i, j):
        at = i // stride % count
        return i + ((at + j) % count - at) * stride

    parts = [dots]
    for j in range(1, count):
        parts.append(lax.ppermute(dots, axis, [(i, moved(i, j)) for i in range(size)]))
    return call(
        functools.partial(sum_kernel, axis=axis, stride=stride),
        (*parts, earlier),
        (VMEM,) * count + (after,),
        [(dots.shape, BF16, VMEM)],
        [pltpu.VMEM((count,) + dots.shape, F32), pltpu.VMEM((DOT_ROWS, dots.shape[1]), F32)],
        "sum_over",
        0,
        1 << 18,
    )[0]


def stage_kernel(*refs, k, points):
    refs = list(refs)
    take = lambda count: [refs.pop(0) for _ in range(count)]
    m = k - 1
    first, sends = k == 0, k < STEPS
    send_slot, branch = take(2)
    if first:
        z_any, basis_any, transfer_any = take(3)
    else:
        column, other, state, far, near, basis, turned, transfer, lifting, top = take(10)
        zs = take(k)
        (z_any,) = take(1)
    state_out, send = take(2)
    if sends:
        coarse_any, low, high = take(3)
    sums, split, arrived, left = take(4)
    if sends:
        coarse, skeletons = take(2)
    if first:
        basis, transfer, vectors, came = take(4)
    else:
        ups, result, coef, combined = take(4)

    leaves, rank, size = basis.shape
    group = leaves // CHUNKS

    def fetch(i):
        if not first:
            return []
        some = slab(i, group)
        return [pltpu.make_async_copy(z_any.at[some], vectors.at[some], arrived.at[i])]

    pieces = CHUNKS

    def stores(i):
        some = slab(i, leaves // pieces)
        pairs = []
        if not first and sends:
            pairs.append((result.at[some], z_any.at[some]))
        if sends:
            pairs.append((coarse.at[some], coarse_any.at[some]))
        return [
            pltpu.make_async_copy(source, target, left.at[n, i])
            for n, (source, target) in enumerate(pairs)
        ]

    def work(i):
        for j in range(group):
            leaf = i * group + j
            if first:
                others = []
                z = vectors[leaf]
            else:
                others = [ref[leaf] for ref in zs]
                z = near[leaf] + dot(turned[leaf], combined[slab(leaf, rank)])
                for l in range(m):
                    z = z - coef[l : l + 1, :] * others[l + 1]
                z = z * coef[STEPS : STEPS + 1, :]
                if sends:
                    result[leaf] = z
                else:
                    z_any[leaf] = z
            if sends:
                rounded = z.astype(BF16)
                coarse[leaf] = rounded
                skeletons[slab(leaf, rank)] = dot(basis[leaf], rounded).astype(BF16)
            for l, vector in enumerate(others + [z]):
                sums[l] += jnp.sum((z * vector).reshape(size // 8, 8, z.shape[1]), axis=0)
        for copy in stores(i):
            copy.start()

    begin, run = windowed(CHUNKS, CHUNKS, fetch, work)
    if first:
        small = [
            pltpu.make_async_copy(basis_any, basis, came.at[0]),
            pltpu.make_async_copy(transfer_any, transfer, came.at[1]),
        ]
        for copy in small:
            copy.start()
    begin()
    sums[...] = jnp.zeros(sums.shape, F32)
    if first:
        state_out[...] = jnp.zeros(state_out.shape, F32)
        for copy in small:
            copy.wait()
    else:
        in_order(branch, column, other, ups)
        count, columns = ups.shape[0], ups.shape[2]
        incoming = dot(top[...], ups[:, :rank].reshape(count * rank, columns)).astype(BF16)
        down = dot(transfer[...].reshape(leaves * rank, rank), incoming)
        combined[...] = (far[...] + down).astype(BF16)
        grams = [row / points for row in from_branches(ups, rank)]
        state_out[...] = state[...]
        weights, inverse = coefficients(m, grams, state, state_out)
        for i, weight in enumerate(weights):
            coef[i : i + 1, :] = weight
        coef[STEPS : STEPS + 1, :] = inverse
    if first:
        run()
    else:
        for i in range(CHUNKS):
            work(i)

    if sends:
        low[...] = coarse[:HW]
        high[...] = coarse[leaves - HW :]
        if first:
            lifted = dot_first(transfer[...].reshape(leaves * rank, rank), skeletons[...])
        else:
            lifted = dot(lifting[...], skeletons[...])
        lifted = lifted.astype(BF16)
    products = [jnp.sum(sums[i], axis=0, keepdims=True) for i in range(k + 1)]
    products = jnp.concatenate(products + [jnp.zeros_like(products[0])] * (7 - k), axis=0)
    store_split(split, products, k + 1)
    dots = split[...].astype(BF16)
    if sends:
        slots, inner = send_slot.shape
        for r in range(inner):
            for s in range(slots):
                send[r, s * rank : (s + 1) * rank] = skeletons[slab(send_slot[s, r], rank)]
            send[r, slots * rank : (slots + 1) * rank] = lifted
            send[r, (slots + 1) * rank :] = dots
    else:
        send[...] = dots
    for i in range(pieces):
        for copy in stores(i):
            copy.wait()


def stage(k, points, send_slot, branch, rhs, basis, transfer, later):
    leaves, rank, size = basis.shape
    first, sends = k == 0, k < STEPS
    tall = rhs.shape
    columns = tall[2]
    slots, inner = send_slot.shape
    names, outs = [], []

    def get(name, shape, dtype, spec):
        names.append(name)
        outs.append((shape, dtype, spec))

    args, specs = [send_slot, branch], [SMEM, SMEM]
    if first:
        args += [rhs, basis, transfer]
        specs += [HBM] * 3
    else:
        args += later
        specs += [VMEM] * len(later)
        get("z", tall, F32, HBM if sends else VMEM)
    get("state", (STATE_ROWS, columns), F32, VMEM)
    rows = (slots + 1) * rank + DOT_ROWS
    get("send", (inner, rows, columns) if sends else (DOT_ROWS, columns), BF16, VMEM)
    if sends:
        get("coarse", tall, BF16, HBM)
        get("low", (HW, size, columns), BF16, VMEM)
        get("high", (HW, size, columns), BF16, VMEM)

    scratch = [
        pltpu.VMEM((STEPS + 1, 8, columns), F32),
        pltpu.VMEM((DOT_ROWS, columns), F32),
        semaphores(CHUNKS),
        semaphores(2, CHUNKS),
    ]
    if sends:
        scratch += [
            pltpu.VMEM(tall, BF16),
            pltpu.VMEM((leaves * rank, columns), BF16),
        ]
    if first:
        scratch += [
            pltpu.VMEM(basis.shape, BF16),
            pltpu.VMEM(transfer.shape, BF16),
            pltpu.VMEM(tall, F32),
            semaphores(2),
        ]
    else:
        column = later[0].shape
        scratch += [
            pltpu.VMEM((2 * column[0],) + column[1:], BF16),
            pltpu.VMEM(tall, F32),
            pltpu.VMEM((8, columns), F32),
            pltpu.VMEM((leaves * rank, columns), BF16),
        ]
    results = call(
        functools.partial(stage_kernel, k=k, points=points),
        args,
        specs,
        outs,
        scratch,
        f"stage{k}",
        1 << 27,
        (k + 4) << 20,
    )
    return dict(zip(names, results))


def vectors_kernel(*refs, wanted, held, final, points):
    refs = list(refs)
    take = lambda count: [refs.pop(0) for _ in range(count)]
    (state,) = take(1)
    if final:
        branch, column, other = take(3)
    zs = take(wanted[-1] + 1)
    _, krylov = take(2)
    if final:
        (hess_out,) = take(1)
    result, left = take(2)
    if final:
        after, ups = take(2)
    else:
        after = state
    if not held:
        vectors, arrived = take(2)
    parts = left.shape[1]
    group = zs[0].shape[0] // parts

    def fetch(i):
        if held:
            return []
        some = slab(i, group)
        return [
            pltpu.make_async_copy(z.at[some], vectors.at[l, some], arrived.at[l, i])
            for l, z in enumerate(zs)
        ]

    def store(n, i):
        some = slab(i, group)
        return pltpu.make_async_copy(result.at[n, some], krylov.at[wanted[n], some], left.at[n, i])

    def work(i):
        for j in range(group):
            leaf = i * group + j
            for n, which in enumerate(wanted):
                vector = None
                for l in range(which + 1):
                    row = basis_row(which, l)
                    values = zs[l][leaf] if held else vectors[l, leaf]
                    term = after[row : row + 1, :] * values
                    vector = term if vector is None else vector + term
                result[n, leaf] = vector
        for n in range(len(wanted)):
            store(n, i).start()

    begin, run = windowed(parts, parts, fetch, work)
    begin()
    if final:
        in_order(branch, column, other, ups)
        grams = [row / points for row in from_branches(ups, 0)]
        after[...] = state[...]
        coefficients(STEPS, grams, state, after)
    run()
    if final:
        for i in range(STEPS + 1):
            for j in range(STEPS):
                row = i * STEPS + j
                if i <= j + 1:
                    hess_out[i, j : j + 1, :] = after[row : row + 1, :]
                else:
                    hess_out[i, j : j + 1, :] = jnp.zeros((1, hess_out.shape[2]), F32)
    for n in range(len(wanted)):
        for i in range(parts):
            store(n, i).wait()


def vectors(state, zs, wanted, before, parts, products=None, points=0):
    final = products is not None
    held = wanted[0] > 0
    tall = zs[0].shape
    count = wanted[-1] + 1
    shape = (STEPS + 1,) + tall
    scratch = [pltpu.VMEM((len(wanted),) + tall, F32), semaphores(len(wanted), parts)]
    outs = [(shape, F32, HBM)]
    args, specs = [state], [VMEM]
    if final:
        args += products
        specs += [SMEM, VMEM, VMEM]
        column = products[1].shape
        outs.append(((STEPS + 1, STEPS, tall[2]), F32, FREE))
        scratch += [
            pltpu.VMEM(state.shape, F32),
            pltpu.VMEM((2 * column[0],) + column[1:], BF16),
        ]
    args += zs[:count]
    specs += [VMEM if held else HBM] * count
    args.append(before)
    specs.append(HBM if held else AFTER)
    if not held:
        scratch += [pltpu.VMEM((count,) + tall, F32), semaphores(count, parts)]
    return call(
        functools.partial(
            vectors_kernel, wanted=wanted, held=held, final=final, points=points
        ),
        args,
        specs,
        outs,
        scratch,
        "last_vector" if final else "vectors",
        1 << 23,
        len(wanted) << 21,
        {len(args) - 1: 0} if held else {},
    )


def shards(
    rhs,
    near_blocks,
    near_index,
    near_mask,
    basis,
    far_blocks,
    far_slot,
    far_mask,
    send_slot,
    transfer,
    top_blocks,
):
    outer, inner = lax.axis_size("outer"), lax.axis_size("inner")
    points = outer * inner * rhs.shape[0]
    leaves, rank = basis.shape[:2]
    slots = send_slot.shape[2]
    branch = lax.axis_index("outer").astype(jnp.int32).reshape(1)
    up_pairs = [(i, i + 1) for i in range(inner - 1)]
    down_pairs = [(j, i) for i, j in up_pairs]
    wanted = send_slot[0].T

    def exchange(array, axis):
        return lax.all_to_all(array, axis, split_axis=0, concat_axis=0, tiled=True)

    zs = [rhs.reshape(leaves, -1, rhs.shape[1])]
    out = stage(0, points, wanted, branch, zs[0], basis, transfer, None)
    packed, index, turned, lifting, top = pack(
        branch, basis, transfer, top_blocks, far_blocks, far_mask, far_slot, near_index, near_mask,
        inner, slots,
    )
    state = out["state"]
    for k in range(1, STEPS + 1):
        recv = exchange(out["send"], "inner")
        before = lax.ppermute(out["high"], "inner", up_pairs)
        after = lax.ppermute(out["low"], "inner", down_pairs)
        earlier = (packed,) if k == 1 else ()
        near = near_field(index, near_blocks, out["coarse"], *earlier)
        done = near
        if k == 1:
            chosen = near_blocks
        elif k == 2:
            chosen = done = choose(index, near_blocks, near)
        if k == STEPS:
            krylov = done = vectors(state, zs, list(range(STEPS - 1)), near, CHUNKS)[0]
        summed = gather_sum(recv, slots * rank, done)
        local_far, blocks, (near,) = far_field(
            index, recv, packed, chosen, (near,), summed
        )

        def between(column):
            held = (basis, turned, transfer, lifting, top, *zs)
            return halo_part(index, blocks, before, after, near, held, column)

        column, other, (near, *held) = over_branches(summed, outer, local_far, between)
        later = [column, other, state, local_far, near, *held]
        out = stage(k, points, wanted, branch, zs[0], basis, transfer, later)
        state = out["state"]
        zs = zs + [out["z"]]
    low = 4 if inner % 4 == 0 else inner
    held = held[-STEPS:] + [out["z"]]
    krylov = vectors(state, held, [STEPS - 1], krylov, 2)[0]
    summed = sum_over(out["send"], "inner", 1, low, krylov, AFTER)
    summed = sum_over(summed, "inner", low, inner // low, summed, AFTER_VMEM)
    column, other, _ = over_branches(summed, outer, summed, lambda column: None)
    products = [branch, column, other]
    krylov, hessenberg = vectors(state, held, [STEPS], krylov, 2, products, points)
    return krylov.reshape(STEPS + 1, *rhs.shape), hessenberg


def solution(mesh):
    return jax.shard_map(
        shards,
        mesh=mesh,
        in_specs=(
            P(("outer", "inner"), None),
            P(("outer", "inner"), None, None, None),
            P(("outer", "inner"), None),
            P(("outer", "inner"), None),
            P(("outer", "inner"), None, None),
            P(("outer", "inner"), None, None, None),
            P(("outer", "inner"), None),
            P(("outer", "inner"), None),
            P(("outer", "inner"), None, None),
            P(("outer", "inner"), None, None),
            P("outer", None, None, None),
        ),
        out_specs=(P(None, ("outer", "inner"), None), P()),
        check_vma=False,
    )
```

```python
import functools

import jax
import jax.numpy as jnp
from jax import lax
from jax.experimental import pallas as pl
from jax.experimental.pallas import tpu as pltpu
from jax.sharding import PartitionSpec as P

HW = 2
STEPS = 4
EPS = 1e-06
PIECES = 3
DOT_ROWS = 16
STATE_ROWS = 64
VMEM_BYTES = 32 * 1024 * 1024
BF16 = jnp.bfloat16
F32 = jnp.float32


def dot(a, b):
    return jnp.dot(a, b, preferred_element_type=F32)


def dot_first(a, b):
    return lax.dot_general(a, b, (((0,), (0,)), ((), ())), preferred_element_type=F32)


def store_split(ref, values, count):
    rest = values
    ref[...] = jnp.zeros(ref.shape, F32)
    for piece in range(PIECES):
        part = rest.astype(BF16).astype(F32)
        ref[piece * 5 : piece * 5 + count, :] = part[:count]
        rest = rest - part


def joined(rows):
    return [rows[i : i + 1] + rows[5 + i : 6 + i] + rows[10 + i : 11 + i] for i in range(5)]


def entry_row(i, l):
    low, high = min(i, l), max(i, l)
    return 20 + high * (high + 1) // 2 + low


def basis_row(i, l):
    return 32 + i * (i + 1) // 2 + l


def coefficients(m, grams, state_in, state_out):
    last = m - 1
    entry = lambda i, l: state_in[entry_row(i, l) : entry_row(i, l) + 1, :]
    expand = lambda i, l: state_in[basis_row(i, l) : basis_row(i, l) + 1, :]

    def put(row, value):
        state_out[row : row + 1, :] = value

    dots = []
    for i in range(m):
        dots.append(sum(expand(i, l) * grams[l] for l in range(i + 1)))
    weights = [dots[i] + entry(i, last) for i in range(m)]
    spread = [sum(weights[l] * entry(i, l) for l in range(m)) for i in range(m)]
    square = grams[m]
    for i in range(m):
        square = square + weights[i] * (weights[i] + spread[i] - 2.0 * dots[i])
    total = jnp.maximum(square, 0.0) + EPS
    root = jnp.sqrt(total)
    inverse = 1.0 / root
    for l in range(m):
        value = sum(weights[i] * expand(i, l) for i in range(l, m))
        put(basis_row(m, l), -inverse * value)
    put(basis_row(m, m), inverse)
    for i in range(m):
        put(i * STEPS + last, weights[i] + (1.0 if i == last else 0.0))
    if m > 0:
        put(m * STEPS + last, root)
    if m < STEPS:
        for i in range(m):
            put(entry_row(i, m), (-entry(i, last) - spread[i]) * inverse)
        put(entry_row(m, m), -EPS / total)
    return weights, inverse


def from_branches(ups_ref, rank):
    rows = ups_ref[0, rank:].astype(F32)
    for c in range(1, ups_ref.shape[0]):
        rows = rows + ups_ref[c, rank:].astype(F32)
    return joined(rows)


SMEM = pl.BlockSpec(memory_space=pltpu.SMEM)
INDEX = pl.BlockSpec(memory_space=pltpu.SMEM)
VMEM = pl.BlockSpec(memory_space=pltpu.VMEM)
HBM = pl.BlockSpec(memory_space=pl.ANY)
AFTER = pl.BlockSpec(memory_space=pl.ANY)
AFTER_VMEM = pl.BlockSpec(memory_space=pl.ANY)
LOOSE = pl.BlockSpec(memory_space=pl.ANY)
FREE = pl.BlockSpec(memory_space=pltpu.VMEM)
AHEAD = 3
LISTED, PLACE, OWN, INDICES = 64, 128, 192, 256
CHUNKS = 4
PIN = True


def call(kernel, args, in_specs, outs, scratch, name, flops, moved, aliases={}):
    def pinned(array, spec):
        if not PIN or not any(spec is one for one in (VMEM, HBM, SMEM, AFTER, AFTER_VMEM)):
            return array
        in_vmem = spec is VMEM or spec is AFTER_VMEM
        return pltpu.with_memory_space_constraint(array, pltpu.VMEM if in_vmem else pltpu.HBM)

    def shape_of(shape, dtype, spec):
        if not PIN or not (spec is VMEM or spec is HBM):
            return jax.ShapeDtypeStruct(shape, dtype)
        return (pltpu.VMEM if spec is VMEM else pltpu.HBM)(shape, dtype)

    return pl.pallas_call(
        kernel,
        in_specs=list(in_specs),
        out_specs=[spec for _, _, spec in outs],
        out_shape=[shape_of(*out) for out in outs],
        scratch_shapes=scratch,
        input_output_aliases=aliases,
        compiler_params=pltpu.CompilerParams(vmem_limit_bytes=VMEM_BYTES),
        cost_estimate=pl.CostEstimate(flops=flops, bytes_accessed=moved, transcendentals=0),
        name=name,
    )(*[pinned(array, spec) for array, spec in zip(args, in_specs)])


def semaphores(*shape):
    return pltpu.SemaphoreType.DMA(shape)


def windowed(count, ahead, fetch, work):
    def start(i):
        for j, copy in enumerate(fetch(i)):
            copy.start(priority=j % 2)

    def body(i, carry):
        @pl.when(i + ahead < count)
        def _():
            start(i + ahead)

        for copy in fetch(i):
            copy.wait()
        work(i)
        return carry

    def begin():
        for i in range(min(ahead, count)):
            start(i)

    return begin, lambda: lax.fori_loop(0, count, body, 0)


def slab(i, size):
    return pl.ds(pl.multiple_of(i * size, size), size)


def pack_kernel(branch, mask_ref, slot_ref, index_ref, near_mask_ref, far_ref, *refs):
    basis_ref, transfer_ref, top_ref = refs[:3]
    out_ref, index_out, basis_out, transfer_out, top_out = refs[3:8]
    blocks, total, packed, basis, transfer, top, turned, lifting, row = refs[8:17]
    arrived, left, came = refs[17:]
    leaves, entries, rank, _ = blocks.shape
    sources, _, width = packed.shape
    slots = width // rank
    near_entries = index_ref.shape[1]

    def fetch(leaf):
        return [pltpu.make_async_copy(far_ref.at[leaf], blocks.at[leaf], arrived.at[leaf])]

    def store(leaf):
        rows = slab(leaf, rank)
        return pltpu.make_async_copy(packed.at[:, rows], out_ref.at[:, rows], left.at[leaf])

    def work(leaf):
        total[...] = jnp.zeros(total.shape, F32)
        for f in range(entries):
            weight = mask_ref[leaf, f].astype(F32)
            total[slot_ref[leaf, f]] += blocks[leaf, f].astype(F32) * weight
        rows = slab(leaf, rank)
        for source in range(sources):
            sides = [total[source * slots + s] for s in range(slots)]
            packed[source, rows] = jnp.concatenate(sides, axis=1).astype(BF16)
        store(leaf).start()

    def list_one(i, count):
        leaf, n = i // near_entries, i % near_entries
        place = index_ref[leaf, n]
        hit = (near_mask_ref[leaf, n] != 0) & ((place < HW) | (place >= HW + leaves))
        own = (place >= HW) & (place < HW + leaves) & (near_mask_ref[leaf, n] != 0)
        index_out[OWN + i] = jnp.where(own, place - HW + 1, 0)
        index_out[LISTED + i] = 0
        index_out[PLACE + i] = 0

        @pl.when(hit)
        def _():
            index_out[LISTED + count] = i
            index_out[PLACE + count] = jnp.where(place < HW, place, place - leaves)

        return count + hit.astype(jnp.int32)

    small = [
        pltpu.make_async_copy(basis_ref, basis, came.at[0]),
        pltpu.make_async_copy(transfer_ref, transfer, came.at[1]),
        pltpu.make_async_copy(top_ref, top, came.at[2]),
    ]
    for copy in small:
        copy.start()
    begin, run = windowed(leaves, AHEAD, fetch, work)
    begin()
    index_out[0] = lax.fori_loop(0, leaves * near_entries, list_one, 0)
    for copy in small:
        copy.wait()
    turn = lambda a: a.astype(F32).T.astype(BF16)
    for leaf in range(leaves):
        turned[leaf] = turn(basis[leaf])
    for pair in range(leaves // 2):
        columns = slice(pair * 2 * rank, (pair + 1) * 2 * rank)
        sides = [turn(transfer[2 * pair + j]) for j in range(2)]
        lifting[:, columns] = jnp.concatenate(sides, axis=1)
    for pair in range(top.shape[1] // 2):
        columns = slice(pair * 2 * rank, (pair + 1) * 2 * rank)
        sides = []
        for c in (2 * pair, 2 * pair + 1):
            sides.append(top[0, c] * (branch[0] != c).astype(F32).astype(BF16))
        row[:, columns] = jnp.concatenate(sides, axis=1)
    results = [
        pltpu.make_async_copy(turned, basis_out, came.at[0]),
        pltpu.make_async_copy(lifting, transfer_out, came.at[1]),
        pltpu.make_async_copy(row, top_out, came.at[2]),
    ]
    for copy in results:
        copy.start()
    run()
    for leaf in range(leaves):
        store(leaf).wait()
    for copy in results:
        copy.wait()


def pack(branch, basis, transfer, top_blocks, far_blocks, far_mask, far_slot, near_index, near_mask, inner, slots):
    leaves, entries, rank, _ = far_blocks.shape
    shape = (inner, leaves * rank, slots * rank)
    turned = (leaves, basis.shape[2], rank)
    lifting = (rank, leaves * rank)
    row = (rank, top_blocks.shape[1] * rank)
    return call(
        pack_kernel,
        (branch, far_mask, far_slot, near_index, near_mask, far_blocks, basis, transfer, top_blocks),
        (SMEM,) * 5 + (HBM,) * 4,
        [
            (shape, BF16, HBM),
            ((INDICES,), jnp.int32, INDEX),
            (turned, BF16, HBM),
            (lifting, BF16, HBM),
            (row, BF16, HBM),
        ],
        [
            pltpu.VMEM(far_blocks.shape, BF16),
            pltpu.VMEM((inner * slots, rank, rank), F32),
            pltpu.VMEM(shape, BF16),
            pltpu.VMEM(basis.shape, BF16),
            pltpu.VMEM(transfer.shape, BF16),
            pltpu.VMEM(top_blocks.shape, BF16),
            pltpu.VMEM(turned, BF16),
            pltpu.VMEM(lifting, BF16),
            pltpu.VMEM(row, BF16),
            semaphores(leaves),
            semaphores(leaves),
            semaphores(3),
        ],
        "pack",
        0,
        10 << 20,
    )


def choose_kernel(index_ref, near_ref, _, out_ref, chosen, moved, given):
    piece = chosen.shape[0] // given.shape[0]
    entries = near_ref.shape[1]
    count = index_ref[0]

    def move(i):
        entry = index_ref[LISTED + i]
        source = near_ref.at[entry // entries, entry % entries]
        return pltpu.make_async_copy(source, chosen.at[i], moved.at[i])

    def give(i):
        some = slab(i, piece)
        return pltpu.make_async_copy(chosen.at[some], out_ref.at[some], given.at[i])

    def each(number, do):
        def body(i, carry):
            do(i)
            return carry

        lax.fori_loop(0, number, body, 0)

    pieces = (count + piece - 1) // piece
    each(count, lambda i: move(i).start())
    each(count, lambda i: move(i).wait())
    each(pieces, lambda i: give(i).start())
    each(pieces, lambda i: give(i).wait())


def choose(index, near_blocks, earlier):
    leaves, entries, size, _ = near_blocks.shape
    shape = (leaves * entries, size, size)
    return call(
        choose_kernel,
        (index, near_blocks, earlier),
        (INDEX, HBM, AFTER),
        [(shape, BF16, HBM)],
        [pltpu.VMEM(shape, BF16), semaphores(shape[0]), semaphores(shape[0] // 8)],
        "choose",
        0,
        5 << 20,
    )[0]


def near_kernel(index_ref, blocks_ref, own_ref, *refs):
    out_ref, blocks, own, result, arrived, came, left = refs[-7:]
    leaves, entries, size, _ = blocks.shape
    pair = leaves // CHUNKS

    def fetch(leaf):
        return [pltpu.make_async_copy(blocks_ref.at[leaf], blocks.at[leaf], arrived.at[leaf])]

    def store(i):
        some = slab(i, pair)
        return pltpu.make_async_copy(result.at[some], out_ref.at[some], left.at[i])

    def work(leaf):
        total = None
        for n in range(entries):
            place = index_ref[OWN + leaf * entries + n]
            weight = (place > 0).astype(F32).astype(BF16)
            values = own[jnp.maximum(place - 1, 0)] * weight
            term = dot(blocks[leaf, n], values)
            total = term if total is None else total + term
        result[leaf] = total

        @pl.when(leaf % pair == pair - 1)
        def _():
            store(leaf // pair).start()

    begin, run = windowed(leaves, AHEAD, fetch, work)
    copy = pltpu.make_async_copy(own_ref, own, came)
    copy.start()
    begin()
    copy.wait()
    run()
    for i in range(CHUNKS):
        store(i).wait()


def near_field(index, near_blocks, own, *earlier):
    leaves, _, size, _ = near_blocks.shape
    columns = own.shape[2]
    return call(
        near_kernel,
        (index, near_blocks, own) + earlier,
        (INDEX, HBM, HBM) + (AFTER,) * len(earlier),
        [((leaves, size, columns), F32, HBM)],
        [
            pltpu.VMEM(near_blocks.shape, BF16),
            pltpu.VMEM(own.shape, BF16),
            pltpu.VMEM((leaves, size, columns), F32),
            semaphores(leaves),
            semaphores(),
            semaphores(leaves),
        ],
        "near_field",
        2 * near_blocks.size * columns,
        2 * near_blocks.size,
    )[0]


def gather_sum_kernel(recv, *refs, lead):
    out_ref, split = refs[-2:]
    rank = out_ref.shape[0] - DOT_ROWS
    total = recv[0, lead:].astype(F32)
    for i in range(1, recv.shape[0]):
        total = total + recv[i, lead:].astype(F32)
    store_split(split, jnp.concatenate(joined(total[rank:]), axis=0), 5)
    if rank > 0:
        out_ref[:rank] = total[:rank].astype(BF16)
    out_ref[rank:] = split[...].astype(BF16)


def gather_sum(recv, lead, earlier):
    _, rows, columns = recv.shape
    return call(
        functools.partial(gather_sum_kernel, lead=lead),
        (recv, earlier),
        (VMEM, AFTER),
        [((rows - lead, columns), BF16, VMEM)],
        [pltpu.VMEM((DOT_ROWS, columns), F32)],
        "gather_sum",
        1 << 20,
        1 << 19,
    )[0]


def stack_kernel(*refs):
    for i, ref in enumerate(refs[:-2]):
        refs[-1][i] = ref[...]


def over_branches(summed, outer, earlier, between):
    shifts = [[(o, (o + 2 * j) % outer) for o in range(outer)] for j in range(1, outer // 2)]
    parts = [summed] + [lax.ppermute(summed, "outer", shift) for shift in shifts]
    column = call(
        stack_kernel,
        parts + [earlier],
        [VMEM] * len(parts) + [AFTER_VMEM],
        [((len(parts),) + summed.shape, BF16, VMEM)],
        [],
        "stack",
        0,
        1 << 18,
    )[0]
    other = lax.ppermute(column, "outer", [(o, o ^ 1) for o in range(outer)])
    return column, other, between(column)


def in_order(branch, column, other, ups):
    count = ups.shape[0]
    for j in range(count // 2):
        ups[lax.rem(branch[0] + count - 2 * j, count)] = column[j]
        mate = branch[0] + 1 - 2 * lax.rem(branch[0], 2)
        ups[lax.rem(mate + count - 2 * j, count)] = other[j]


def far_kernel(index_ref, recv, packed_ref, blocks_ref, *refs):
    held = (len(refs) - 7) // 2
    sources, (_, far, blocks), targets = refs[:held], refs[held : held + 3], refs[held + 3 : -4]
    packed, arrived, fetched, loaded = refs[-4:]
    share = packed.shape[0] // CHUNKS
    width = packed.shape[2]
    chosen = len(blocks_ref.shape) == 3
    piece = blocks.shape[0] // fetched.shape[0]
    count = (index_ref[0] + piece - 1) // piece

    def fetch(i):
        some = slab(i, share)
        return [pltpu.make_async_copy(packed_ref.at[some], packed.at[some], arrived.at[i])]

    def block(i):
        if chosen:
            some = slab(i, piece)
            return pltpu.make_async_copy(blocks_ref.at[some], blocks.at[some], fetched.at[i])
        entry, entries = index_ref[LISTED + i], blocks_ref.shape[1]
        source = blocks_ref.at[entry // entries, entry % entries]
        return pltpu.make_async_copy(source, blocks.at[i], fetched.at[i])

    def ask(i, carry):
        block(i).start()
        return carry

    def have(i, carry):
        block(i).wait()
        return carry

    def work(i):
        term = None
        for j in range(share):
            source = i * share + j
            one = dot(packed[source], recv[source, :width])
            term = one if term is None else term + one

        @pl.when(i == 0)
        def _():
            far[...] = term

        @pl.when(i > 0)
        def _():
            far[...] += term

    loads = [
        pltpu.make_async_copy(source, target, loaded.at[i])
        for i, (source, target) in enumerate(zip(sources, targets))
    ]
    begin, run = windowed(CHUNKS, CHUNKS, fetch, work)
    begin()
    lax.fori_loop(0, count, ask, 0)
    for copy in loads:
        copy.start()
    run()
    lax.fori_loop(0, count, have, 0)
    for copy in loads:
        copy.wait()


def far_field(index, recv, packed, near_blocks, held, earlier):
    sources, rows, _ = packed.shape
    size = near_blocks.shape[-1]
    number = near_blocks.size // size**2
    pieces = number // 8 if near_blocks.ndim == 3 else number
    outs = [((rows, recv.shape[2]), F32, VMEM), ((number, size, size), BF16, VMEM)]
    far, blocks, *held = call(
        far_kernel,
        (index, recv, packed, near_blocks, *held, earlier),
        (INDEX, VMEM, HBM, HBM) + (HBM,) * len(held) + (AFTER_VMEM,),
        outs + [(a.shape, a.dtype, VMEM) for a in held],
        [
            pltpu.VMEM(packed.shape, BF16),
            semaphores(CHUNKS),
            semaphores(pieces),
            semaphores(len(held)),
        ],
        "far_field",
        2 * packed.size * recv.shape[2],
        2 * packed.size,
    )
    return far, blocks, held


def halo_kernel(index_ref, blocks, before, after, near_in, *refs):
    held = (len(refs) - 4) // 2
    sources, near, targets = refs[:held], refs[held + 1], refs[held + 2 : -2]
    halo, loaded = refs[-2:]
    loads = [
        pltpu.make_async_copy(source, target, loaded.at[i])
        for i, (source, target) in enumerate(zip(sources, targets))
    ]
    for copy in loads:
        copy.start()
    reach = before.shape[0]
    entries = blocks.shape[0] // near.shape[0]
    halo[:reach] = before[...]
    halo[reach:] = after[...]
    count = index_ref[0]
    at_once = 8

    def add(group, carry):
        terms = []
        for j in range(at_once):
            i = jnp.minimum(group * at_once + j, count - 1)
            weight = (group * at_once + j < count).astype(F32).astype(BF16)
            leaf = index_ref[LISTED + i] // entries
            values = halo[index_ref[PLACE + i]] * weight
            terms.append((leaf, dot(blocks[i], values)))
        for leaf, term in terms:
            near[leaf] += term
        return carry

    lax.fori_loop(0, (count + at_once - 1) // at_once, add, 0)
    for copy in loads:
        copy.wait()


def halo_part(index, blocks, before, after, near, held, earlier):
    return call(
        halo_kernel,
        (index, blocks, before, after, near, *held, earlier),
        (INDEX, VMEM, VMEM, VMEM, VMEM) + (HBM,) * len(held) + (AFTER_VMEM,),
        [(a.shape, a.dtype, VMEM) for a in (near, *held)],
        [pltpu.VMEM((2 * before.shape[0],) + before.shape[1:], BF16), semaphores(len(held))],
        "halo_part",
        1 << 28,
        2 << 20,
        {4: 0},
    )


def sum_kernel(*refs, axis, stride):
    *parts, _, out, rows, split = refs
    count = len(parts)
    place = lax.rem(lax.axis_index(axis).astype(jnp.int32) // stride, count)
    for j, part in enumerate(parts):
        rows[lax.rem(place + count - j, count)] = part[...].astype(F32)
    total = rows[0]
    for i in range(1, count):
        total = total + rows[i]
    store_split(split, jnp.concatenate(joined(total), axis=0), 5)
    out[...] = split[...].astype(BF16)


def sum_over(dots, axis, stride, count, earlier, after):
    if count == 1:
        return dots
    size = lax.axis_size(axis)

    def moved(i, j):
        at = i // stride % count
        return i + ((at + j) % count - at) * stride

    parts = [dots]
    for j in range(1, count):
        parts.append(lax.ppermute(dots, axis, [(i, moved(i, j)) for i in range(size)]))
    return call(
        functools.partial(sum_kernel, axis=axis, stride=stride),
        (*parts, earlier),
        (VMEM,) * count + (after,),
        [(dots.shape, BF16, VMEM)],
        [pltpu.VMEM((count,) + dots.shape, F32), pltpu.VMEM((DOT_ROWS, dots.shape[1]), F32)],
        "sum_over",
        0,
        1 << 18,
    )[0]


def stage_kernel(*refs, k, points):
    refs = list(refs)
    take = lambda count: [refs.pop(0) for _ in range(count)]
    m = k - 1
    first, sends = k == 0, k < STEPS
    send_slot, branch = take(2)
    if first:
        z_any, basis_any, transfer_any = take(3)
    else:
        column, other, state, far, near, basis, turned, transfer, lifting, top = take(10)
        zs = take(k)
        (z_any,) = take(1)
    state_out, send = take(2)
    if sends:
        coarse_any, low, high = take(3)
    sums, split, arrived, left = take(4)
    if sends:
        coarse, skeletons = take(2)
    if first:
        basis, transfer, vectors, came = take(4)
    else:
        ups, result, coef, combined = take(4)

    leaves, rank, size = basis.shape
    group = leaves // CHUNKS

    def fetch(i):
        if not first:
            return []
        some = slab(i, group)
        return [pltpu.make_async_copy(z_any.at[some], vectors.at[some], arrived.at[i])]

    pieces = CHUNKS

    def stores(i):
        some = slab(i, leaves // pieces)
        pairs = []
        if not first and sends:
            pairs.append((result.at[some], z_any.at[some]))
        if sends:
            pairs.append((coarse.at[some], coarse_any.at[some]))
        return [
            pltpu.make_async_copy(source, target, left.at[n, i])
            for n, (source, target) in enumerate(pairs)
        ]

    def work(i):
        for j in range(group):
            leaf = i * group + j
            if first:
                others = []
                z = vectors[leaf]
            else:
                others = [ref[leaf] for ref in zs]
                z = near[leaf] + dot(turned[leaf], combined[slab(leaf, rank)])
                for l in range(m):
                    z = z - coef[l : l + 1, :] * others[l + 1]
                z = z * coef[STEPS : STEPS + 1, :]
                if sends:
                    result[leaf] = z
                else:
                    z_any[leaf] = z
            if sends:
                rounded = z.astype(BF16)
                coarse[leaf] = rounded
                skeletons[slab(leaf, rank)] = dot(basis[leaf], rounded).astype(BF16)
            for l, vector in enumerate(others + [z]):
                sums[l] += jnp.sum((z * vector).reshape(size // 8, 8, z.shape[1]), axis=0)
        for copy in stores(i):
            copy.start()

    begin, run = windowed(CHUNKS, CHUNKS, fetch, work)
    if first:
        small = [
            pltpu.make_async_copy(basis_any, basis, came.at[0]),
            pltpu.make_async_copy(transfer_any, transfer, came.at[1]),
        ]
        for copy in small:
            copy.start()
    begin()
    sums[...] = jnp.zeros(sums.shape, F32)
    if first:
        state_out[...] = jnp.zeros(state_out.shape, F32)
        for copy in small:
            copy.wait()
    else:
        in_order(branch, column, other, ups)
        count, columns = ups.shape[0], ups.shape[2]
        incoming = dot(top[...], ups[:, :rank].reshape(count * rank, columns)).astype(BF16)
        down = dot(transfer[...].reshape(leaves * rank, rank), incoming)
        combined[...] = (far[...] + down).astype(BF16)
        grams = [row / points for row in from_branches(ups, rank)]
        state_out[...] = state[...]
        weights, inverse = coefficients(m, grams, state, state_out)
        for i, weight in enumerate(weights):
            coef[i : i + 1, :] = weight
        coef[STEPS : STEPS + 1, :] = inverse
    if first:
        run()
    else:
        for i in range(CHUNKS):
            work(i)

    if sends:
        low[...] = coarse[:HW]
        high[...] = coarse[leaves - HW :]
        if first:
            lifted = dot_first(transfer[...].reshape(leaves * rank, rank), skeletons[...])
        else:
            lifted = dot(lifting[...], skeletons[...])
        lifted = lifted.astype(BF16)
    products = [jnp.sum(sums[i], axis=0, keepdims=True) for i in range(k + 1)]
    products = jnp.concatenate(products + [jnp.zeros_like(products[0])] * (7 - k), axis=0)
    store_split(split, products, k + 1)
    dots = split[...].astype(BF16)
    if sends:
        slots, inner = send_slot.shape
        for r in range(inner):
            for s in range(slots):
                send[r, s * rank : (s + 1) * rank] = skeletons[slab(send_slot[s, r], rank)]
            send[r, slots * rank : (slots + 1) * rank] = lifted
            send[r, (slots + 1) * rank :] = dots
    else:
        send[...] = dots
    for i in range(pieces):
        for copy in stores(i):
            copy.wait()


def stage(k, points, send_slot, branch, rhs, basis, transfer, later):
    leaves, rank, size = basis.shape
    first, sends = k == 0, k < STEPS
    tall = rhs.shape
    columns = tall[2]
    slots, inner = send_slot.shape
    names, outs = [], []

    def get(name, shape, dtype, spec):
        names.append(name)
        outs.append((shape, dtype, spec))

    args, specs = [send_slot, branch], [SMEM, SMEM]
    if first:
        args += [rhs, basis, transfer]
        specs += [HBM] * 3
    else:
        args += later
        specs += [VMEM] * len(later)
        get("z", tall, F32, HBM if sends else VMEM)
    get("state", (STATE_ROWS, columns), F32, VMEM)
    rows = (slots + 1) * rank + DOT_ROWS
    get("send", (inner, rows, columns) if sends else (DOT_ROWS, columns), BF16, VMEM)
    if sends:
        get("coarse", tall, BF16, HBM)
        get("low", (HW, size, columns), BF16, VMEM)
        get("high", (HW, size, columns), BF16, VMEM)

    scratch = [
        pltpu.VMEM((STEPS + 1, 8, columns), F32),
        pltpu.VMEM((DOT_ROWS, columns), F32),
        semaphores(CHUNKS),
        semaphores(2, CHUNKS),
    ]
    if sends:
        scratch += [
            pltpu.VMEM(tall, BF16),
            pltpu.VMEM((leaves * rank, columns), BF16),
        ]
    if first:
        scratch += [
            pltpu.VMEM(basis.shape, BF16),
            pltpu.VMEM(transfer.shape, BF16),
            pltpu.VMEM(tall, F32),
            semaphores(2),
        ]
    else:
        column = later[0].shape
        scratch += [
            pltpu.VMEM((2 * column[0],) + column[1:], BF16),
            pltpu.VMEM(tall, F32),
            pltpu.VMEM((8, columns), F32),
            pltpu.VMEM((leaves * rank, columns), BF16),
        ]
    results = call(
        functools.partial(stage_kernel, k=k, points=points),
        args,
        specs,
        outs,
        scratch,
        f"stage{k}",
        1 << 27,
        (k + 4) << 20,
    )
    return dict(zip(names, results))


def vectors_kernel(*refs, wanted, held, final, points):
    refs = list(refs)
    take = lambda count: [refs.pop(0) for _ in range(count)]
    (state,) = take(1)
    if final:
        (dots,) = take(1)
    zs = take(wanted[-1] + 1)
    _, krylov = take(2)
    if final:
        (hess_out,) = take(1)
    result, left = take(2)
    if final:
        (after,) = take(1)
    else:
        after = state
    if not held:
        vectors, arrived = take(2)
    parts = left.shape[1]
    group = zs[0].shape[0] // parts

    def fetch(i):
        if held:
            return []
        some = slab(i, group)
        return [
            pltpu.make_async_copy(z.at[some], vectors.at[l, some], arrived.at[l, i])
            for l, z in enumerate(zs)
        ]

    def store(n, i):
        some = slab(i, group)
        return pltpu.make_async_copy(result.at[n, some], krylov.at[wanted[n], some], left.at[n, i])

    def work(i):
        for j in range(group):
            leaf = i * group + j
            for n, which in enumerate(wanted):
                vector = None
                for l in range(which + 1):
                    row = basis_row(which, l)
                    values = zs[l][leaf] if held else vectors[l, leaf]
                    term = after[row : row + 1, :] * values
                    vector = term if vector is None else vector + term
                result[n, leaf] = vector
        for n in range(len(wanted)):
            store(n, i).start()

    begin, run = windowed(parts, parts, fetch, work)
    begin()
    if final:
        grams = [row / points for row in joined(dots[...].astype(F32))]
        after[...] = state[...]
        coefficients(STEPS, grams, state, after)
    run()
    if final:
        for i in range(STEPS + 1):
            for j in range(STEPS):
                row = i * STEPS + j
                if i <= j + 1:
                    hess_out[i, j : j + 1, :] = after[row : row + 1, :]
                else:
                    hess_out[i, j : j + 1, :] = jnp.zeros((1, hess_out.shape[2]), F32)
    for n in range(len(wanted)):
        for i in range(parts):
            store(n, i).wait()


def vectors(state, zs, wanted, before, parts, products=None, points=0):
    final = products is not None
    held = wanted[0] > 0
    tall = zs[0].shape
    count = wanted[-1] + 1
    shape = (STEPS + 1,) + tall
    scratch = [pltpu.VMEM((len(wanted),) + tall, F32), semaphores(len(wanted), parts)]
    outs = [(shape, F32, HBM)]
    args, specs = [state], [VMEM]
    if final:
        args.append(products)
        specs.append(VMEM)
        outs.append(((STEPS + 1, STEPS, tall[2]), F32, FREE))
        scratch.append(pltpu.VMEM(state.shape, F32))
    args += zs[:count]
    specs += [VMEM if held else HBM] * count
    args.append(before)
    specs.append(HBM if held else AFTER)
    if not held:
        scratch += [pltpu.VMEM((count,) + tall, F32), semaphores(count, parts)]
    return call(
        functools.partial(
            vectors_kernel, wanted=wanted, held=held, final=final, points=points
        ),
        args,
        specs,
        outs,
        scratch,
        "last_vector" if final else "vectors",
        1 << 23,
        len(wanted) << 21,
        {len(args) - 1: 0} if held else {},
    )


def shards(
    rhs,
    near_blocks,
    near_index,
    near_mask,
    basis,
    far_blocks,
    far_slot,
    far_mask,
    send_slot,
    transfer,
    top_blocks,
):
    outer, inner = lax.axis_size("outer"), lax.axis_size("inner")
    points = outer * inner * rhs.shape[0]
    leaves, rank = basis.shape[:2]
    slots = send_slot.shape[2]
    branch = lax.axis_index("outer").astype(jnp.int32).reshape(1)
    up_pairs = [(i, i + 1) for i in range(inner - 1)]
    down_pairs = [(j, i) for i, j in up_pairs]
    wanted = send_slot[0].T

    def exchange(array, axis):
        return lax.all_to_all(array, axis, split_axis=0, concat_axis=0, tiled=True)

    zs = [rhs.reshape(leaves, -1, rhs.shape[1])]
    out = stage(0, points, wanted, branch, zs[0], basis, transfer, None)
    packed, index, turned, lifting, top = pack(
        branch, basis, transfer, top_blocks, far_blocks, far_mask, far_slot, near_index, near_mask,
        inner, slots,
    )
    state = out["state"]
    for k in range(1, STEPS + 1):
        recv = exchange(out["send"], "inner")
        before = lax.ppermute(out["high"], "inner", up_pairs)
        after = lax.ppermute(out["low"], "inner", down_pairs)
        earlier = (packed,) if k == 1 else ()
        near = near_field(index, near_blocks, out["coarse"], *earlier)
        done = near
        if k == 1:
            chosen = near_blocks
        elif k == 2:
            chosen = done = choose(index, near_blocks, near)
        if k == STEPS:
            krylov = done = vectors(state, zs, list(range(STEPS - 1)), near, CHUNKS)[0]
        summed = gather_sum(recv, slots * rank, done)
        local_far, blocks, (near,) = far_field(
            index, recv, packed, chosen, (near,), summed
        )

        def between(column):
            held = (basis, turned, transfer, lifting, top, *zs)
            return halo_part(index, blocks, before, after, near, held, column)

        column, other, (near, *held) = over_branches(summed, outer, local_far, between)
        later = [column, other, state, local_far, near, *held]
        out = stage(k, points, wanted, branch, zs[0], basis, transfer, later)
        state = out["state"]
        zs = zs + [out["z"]]
    held = held[-STEPS:] + [out["z"]]
    krylov = vectors(state, held, [STEPS - 1], krylov, 2)[0]
    products, last, pin = out["send"], krylov, AFTER
    strides = [("inner", 1 << i) for i in range(inner.bit_length() - 1)]
    strides += [("outer", 2 << i) for i in range(outer.bit_length() - 2)] + [("outer", 1)]
    for axis, stride in strides:
        products = sum_over(products, axis, stride, 2, last, pin)
        last, pin = products, AFTER_VMEM
    krylov, hessenberg = vectors(state, held, [STEPS], krylov, 2, products, points)
    return krylov.reshape(STEPS + 1, *rhs.shape), hessenberg


def solution(mesh):
    return jax.shard_map(
        shards,
        mesh=mesh,
        in_specs=(
            P(("outer", "inner"), None),
            P(("outer", "inner"), None, None, None),
            P(("outer", "inner"), None),
            P(("outer", "inner"), None),
            P(("outer", "inner"), None, None),
            P(("outer", "inner"), None, None, None),
            P(("outer", "inner"), None),
            P(("outer", "inner"), None),
            P(("outer", "inner"), None, None),
            P(("outer", "inner"), None, None),
            P("outer", None, None, None),
        ),
        out_specs=(P(None, ("outer", "inner"), None), P()),
        check_vma=False,
    )
```
